128 devices in a mesh: section: 2 (over core), tensor: 4 (over z), dp: 16 (over y, x).
Axes of the slice: x: 4, y: 4, z: 4, core: 2. Of those that a mesh axis runs over, the one named last changes fastest.
Arguments:
- tokens: bfloat16 [4096, 1536], P('dp'), may hold values from -6 to 6
- plan_order: int32 [16, 2], P('dp'), may hold values from 0 to 1, each once within a row
- cotangent: bfloat16 [4096, 1536], P('dp'), may hold values from -6 to 6
- norm_gains: float32 [2, 2, 1536], P('section'), may hold values from 0.5 to 1.5
- ffn_gate: bfloat16 [2, 1536, 4608], P('section', None, 'tensor'), may hold values from -0.15625 to 0.15625
- ffn_up: bfloat16 [2, 1536, 4608], P('section', None, 'tensor'), may hold values from -0.15625 to 0.15625
- ffn_down: bfloat16 [2, 4608, 1536], P('section', 'tensor'), may hold values from -0.09375 to 0.09375
- rec_in: bfloat16 [1536, 2, 2048], P('section', None, 'tensor'), may hold values from -0.15625 to 0.15625
- rec_gates: bfloat16 [128, 2, 2048], P('section', None, 'tensor'), may hold values from -0.5 to 0.5
- rec_conv: bfloat16 [4, 2048], P('section', 'tensor'), may hold values from -3 to 3
- rec_vec: bfloat16 [4, 2048], P('section', 'tensor'), may hold values from -8 to 2
- rec_out: bfloat16 [2048, 1536], P('tensor', 'section'), may hold values from -0.125 to 0.125
- att_q: bfloat16 [1536, 1536], P('section', 'tensor'), may hold values from -0.15625 to 0.15625
- att_kv: bfloat16 [1536, 256], P('section'), may hold values from -0.15625 to 0.15625
- att_out: bfloat16 [1536, 1536], P('tensor', 'section'), may hold values from -0.4375 to 0.4375
Outputs:
- boundary: float32 [2, 4096, 1536], P('section', 'dp')
- grad_gains: float32 [2, 2, 1536], P('section')
- grad_ffn_gate: float32 [2, 1536, 4608], P('section', None, 'tensor')
- grad_ffn_up: float32 [2, 1536, 4608], P('section', None, 'tensor')
- grad_ffn_down: float32 [2, 4608, 1536], P('section', 'tensor')
- grad_rec_in: float32 [1536, 2, 2048], P('section', None, 'tensor')
- grad_rec_gates: float32 [128, 2, 2048], P('section', None, 'tensor')
- grad_rec_conv: float32 [4, 2048], P('section', 'tensor')
- grad_rec_vec: float32 [4, 2048], P('section', 'tensor')
- grad_rec_out: float32 [2048, 1536], P('tensor', 'section')
- grad_att_q: float32 [1536, 1536], P('section', 'tensor')
- grad_att_kv: float32 [1536, 256], P('section')
- grad_att_out: float32 [1536, 1536], P('tensor', 'section')
The draws below stay inside these ranges and needn't reach their ends.
Inputs may be any that keep to these rules, and one draw needn't show every extreme that they name: `plan_order`: each row is an order of the 2 micro-batches.
All inputs are finite; a program needn't handle non-finite values.
Results may differ from the reference program's by a relative error of at most 0.04.
Values may be sent and summed in bfloat16 or wider, within the bound.
A program may use at most 256 MiB of HBM per device.

```python
import math
import jax
import jax.numpy as jnp
from jax import lax

D = 1536
RW = 2048
FF = 4608
HQ = 12
HD = 128
BW = 128
SEQ = 128
MICRO = 2
TOKENS = 4096
N_DP = 16


def draw_rec_vec(key, part):
    key = jax.random.fold_in(key, 7)
    bias_key, rate_key = jax.random.split(key)
    biases = jnp.clip(0.5 * jax.random.normal(bias_key, (3, RW), jnp.float32), -1.5, 1.5)
    low_end = math.log(0.001)
    high_end = math.log(1.0)
    decay_rates = jnp.exp(jax.random.uniform(rate_key, (1, RW), jnp.float32, low_end, high_end))
    return jnp.concatenate([biases, jnp.log(jnp.expm1(decay_rates))], 0).astype(jnp.bfloat16)


def strengthened(values, own_key, source, target, shards_of, factor):
    def block_of(dim):
        return (jnp.arange(values.shape[dim]) // (values.shape[dim] // shards_of)).reshape((-1,) + (1,) * (values.ndim - 1 - dim))

    near = jax.random.permutation(own_key, shards_of)[block_of(target)]
    second = (block_of(target) + shards_of // 2) % shards_of
    return jnp.where((block_of(source) == near) | (block_of(source) == second), factor * values, values)


def block_scale(stream_key, dims, cuts, low, top_value):
    loudness, own = 1.0, jax.random.fold_in(stream_key, 6)
    for axis_at, parts in cuts:
        steps = jnp.exp(jax.random.uniform(jax.random.fold_in(own, axis_at), (parts,), jnp.float32, low / len(cuts), top_value / len(cuts)))
        loudness = loudness * jnp.repeat(steps, dims[axis_at] // parts).reshape([-1 if axis == axis_at else 1 for axis in range(len(dims))])
    return loudness


def normal_values(key, extent, spread, most, cuts=(), dtype=jnp.bfloat16):
    loudness = block_scale(key, extent, cuts, -0.22, 0.18) if cuts else 1.0
    array = jax.random.normal(key, extent, jnp.float32) * spread * loudness
    return jnp.minimum(jnp.maximum(array, -most), most).astype(dtype)


def bell_draw_with(rng, extent, spread, limit, cuts, heavy, dtype=jnp.bfloat16):
    values = spread * jax.random.normal(rng, extent, jnp.float32)
    if cuts:
        values = values * block_scale(rng, extent, cuts, -0.22, 0.18)
    return jnp.clip(strengthened(values, jax.random.fold_in(rng, 3), *heavy), -limit, limit).astype(dtype)


def setup_inputs(seed: int = 0) -> dict:
    key_list = jax.random.split(jax.random.key(seed), 16)
    return {
        "tokens": bell_draw_with(key_list[0], (TOKENS, D), 1.0, 6.0, ((0, 16),), (0, 1, 16, 2.0)),
        "plan_order": jax.vmap(lambda own: jax.random.permutation(own, MICRO))(jax.random.split(key_list[1], N_DP)).reshape((N_DP, MICRO)).astype(jnp.int32),
        "cotangent": normal_values(key_list[2], (TOKENS, D), 1.0, 6.0, ((0, 16),)),
        "norm_gains": jnp.clip(1.0 + 0.1 * jax.random.normal(key_list[3], (2, 2, D), jnp.float32), 0.5, 1.5),
        "ffn_gate": normal_values(key_list[4], (2, D, FF), D ** -0.5, 0.15625, ((0, 2), (2, 4))),
        "ffn_up": normal_values(key_list[5], (2, D, FF), D ** -0.5, 0.15625, ((0, 2), (2, 4))),
        "ffn_down": normal_values(key_list[6], (2, FF, D), FF ** -0.5, 0.09375, ((0, 2), (1, 4))),
        "rec_in": normal_values(key_list[7], (D, 2, RW), D ** -0.5, 0.15625, ((0, 2), (2, 4))),
        "rec_gates": normal_values(key_list[8], (BW, 2, RW), BW ** -0.5, 0.5, ((0, 2), (2, 4))),
        "rec_conv": normal_values(key_list[9], (4, RW), 0.5, 3.0, ((0, 2), (1, 4))),
        "rec_vec": draw_rec_vec(jax.random.fold_in(key_list[15], 71), 0),
        "rec_out": normal_values(key_list[11], (RW, D), RW ** -0.5, 0.125, ((0, 4), (1, 2))),
        "att_q": normal_values(key_list[12], (D, HQ * HD), D ** -0.5, 0.15625, ((0, 2), (1, 4))),
        "att_kv": normal_values(key_list[13], (D, 2 * HD), D ** -0.5, 0.15625, ((0, 2),)),
        "att_out": normal_values(key_list[14], (HQ * HD, D), (HQ * HD // 8) ** -0.5, 0.4375, ((0, 4), (1, 2))),
    }


NORM_EPS = 1e-06
RATE_FLOOR = 0.01
FULL_PRECISION = lax.Precision.HIGHEST

@jax.custom_vjp
def low(v):
    return lax.optimization_barrier(v.astype(jnp.bfloat16)).astype(jnp.float32)

@jax.custom_vjp
def low_back(v):
    return v

def low_keep(v):
    return (low(v), None)

def low_pass(kept, grad):
    return (grad,)

def back_keep(v):
    return (v, None)

def back_low(kept, grad):
    return (low(grad),)
low.defvjp(low_keep, low_pass)
low_back.defvjp(back_keep, back_low)

def product(left, right):
    return jnp.dot(left, right, precision=FULL_PRECISION)

def rms_piece(values, gain):
    return values * lax.rsqrt(lax.optimization_barrier(jnp.mean(values * values, -1, keepdims=True)) + NORM_EPS) * gain

def softplus_fn(values):
    return jnp.maximum(values, 0.0) + jnp.log1p(jnp.exp(-jnp.abs(values)))

def geglu_piece(gate_pre, up_pre):
    return jax.nn.gelu(gate_pre, approximate=True) * up_pre

def conv_piece(inflow, conv_taps, offset):
    length = inflow.shape[0]
    padded = jnp.pad(inflow, ((3, 0), (0, 0)))
    result = offset[None, :] + conv_taps[0] * inflow
    for shift_by in range(1, 4):
        result = result + conv_taps[shift_by] * padded[3 - shift_by:3 - shift_by + length]
    return result

def link_pairs(earlier, later):
    return (earlier[0] * later[0], later[0] * earlier[1] + later[1])

def lru_piece(conv_out, pre_input, pre_decay, branch, vectors):
    input_gate = jax.nn.sigmoid(pre_input + vectors[0])
    decay_gate = jax.nn.sigmoid(pre_decay + vectors[1])
    decay_rate = jnp.exp(-8.0 * decay_gate * softplus_fn(vectors[2]))
    scale_in = jnp.sqrt(jnp.maximum(1.0 - decay_rate * decay_rate, RATE_FLOOR))
    states = lax.associative_scan(link_pairs, (decay_rate, scale_in * input_gate * conv_out), axis=0)[1]
    return states * jax.nn.gelu(branch, approximate=True)

def attention_probs(raw_scores):
    length = raw_scores.shape[-1]
    row_ids = lax.broadcasted_iota(jnp.int32, (length, length), 0)
    col_ids = lax.broadcasted_iota(jnp.int32, (length, length), 1)
    allowed = col_ids <= row_ids
    scaled = jnp.where(allowed, raw_scores * HD ** (-0.5), -1e+30)
    row_top = lax.optimization_barrier(jnp.max(scaled, -1, keepdims=True))
    expo_terms = jnp.exp(scaled - row_top)
    return expo_terms / lax.optimization_barrier(jnp.sum(expo_terms, -1, keepdims=True))

def feed_forward(values, gain, gate_w, up_w, down_w):
    normed = low(rms_piece(values, gain))
    gate_pre = low_back(product(normed, gate_w))
    up_pre = low_back(product(normed, up_w))
    hidden = low(geglu_piece(gate_pre, up_pre))
    return values + low_back(product(hidden, down_w))

def recurrent_block(values, gain_pair, gate_w, up_w, down_w, in_w, gates_w, taps_w, vec_w, out_w):
    length = values.shape[0]
    rec_width = out_w.shape[0]
    head_count = rec_width // BW
    normed = low(rms_piece(values, gain_pair[0]))
    inflow = low_back(product(normed, in_w[:, 0]))
    branch = low_back(product(normed, in_w[:, 1]))
    conv_out = conv_piece(inflow, taps_w, vec_w[0])
    conv_heads = low(conv_out).reshape(length, head_count, BW)
    gate_mats = gates_w.reshape(BW, 2, head_count, BW)
    pre_both = low_back(jnp.einsum('thi,iqhj->qthj', conv_heads, gate_mats, precision=FULL_PRECISION).reshape(2, length, rec_width))
    mixed = low(lru_piece(conv_out, pre_both[0], pre_both[1], branch, vec_w[1:]))
    middle = values + low_back(product(mixed, out_w))
    return feed_forward(middle, gain_pair[1], gate_w, up_w, down_w)

def attention_block(values, gain_pair, gate_w, up_w, down_w, q_w, kv_w, out_w):
    length = values.shape[0]
    normed = low(rms_piece(values, gain_pair[0]))
    queries = low(low_back(product(normed, q_w))).reshape(length, -1, HD)
    keys_values = low(low_back(product(normed, kv_w)))
    raw_scores = low_back(jnp.einsum('ihd,jd->hij', queries, keys_values[:, :HD], precision=FULL_PRECISION))
    attn_probs = low(attention_probs(raw_scores))
    attended = low(low_back(jnp.einsum('hij,jd->ihd', attn_probs, keys_values[:, HD:], precision=FULL_PRECISION))).reshape(length, -1)
    middle = values + low_back(product(attended, out_w))
    return feed_forward(middle, gain_pair[1], gate_w, up_w, down_w)

def reference(tokens, plan_order, cotangent, norm_gains, ffn_gate, ffn_up, ffn_down, rec_in, rec_gates, rec_conv, rec_vec, rec_out, att_q, att_kv, att_out):
    float_args = tuple((array_in.astype(jnp.float32) for array_in in (tokens, norm_gains, ffn_gate, ffn_up, ffn_down, rec_in, rec_gates, rec_conv, rec_vec, rec_out, att_q, att_kv, att_out)))

    def whole_run(tok_f, gains_f, gate_f, up_f, down_f, in_f, gates_f, conv_f, vec_f, rout_f, q_f, kv_f, aout_f):
        grouped = tok_f.reshape(N_DP, MICRO, SEQ, D)
        index_map = jnp.broadcast_to(plan_order[:, :, None, None], (N_DP, MICRO, SEQ, D))
        picked = jnp.take_along_axis(grouped, index_map, axis=1).reshape(N_DP * MICRO, SEQ, D)

        def one_sequence(values):
            first_out = recurrent_block(values, gains_f[0], gate_f[0], up_f[0], down_f[0], in_f, gates_f, conv_f, vec_f, rout_f)
            handed = low_back(low(first_out))
            return attention_block(handed, gains_f[1], gate_f[1], up_f[1], down_f[1], q_f, kv_f, aout_f)
        outputs = lax.map(jax.checkpoint(one_sequence), picked)
        return outputs.reshape(TOKENS, D)
    outputs, pull_back = jax.vjp(whole_run, *float_args)
    gradients = pull_back(cotangent.astype(jnp.float32))
    boundary = jnp.stack([gradients[0], outputs])
    return (boundary, gradients[1], gradients[2], gradients[3], gradients[4], gradients[5], gradients[6], gradients[7], gradients[8], gradients[9], gradients[10], gradients[11], gradients[12])
```

```python
import jax
import jax.numpy as jnp
from jax import lax
from jax.experimental import pallas as pl
from jax.experimental.pallas import tpu as pltpu
from jax.sharding import PartitionSpec as P

HD = 128
SEQ = 128
NORM_EPS = 1e-06
RATE_FLOOR = 0.01
BF = jnp.bfloat16
F32 = jnp.float32
MESH = pl.DeviceIdType.MESH
NT = (((1,), (1,)), ((), ()))

D = 1536
FQ = 1152
RQ = 512
AQ = 384
SH = 32
CR = 144
CC = 384
RR = 64
HALF_A = 80
N_ITEMS = 8
ITEM_ATT = 6
ITEM_REC = 7


def mm(left, right):
    return jnp.dot(left, right, preferred_element_type=F32)


def mm_nt(left, right):
    return lax.dot_general(left, right, NT, preferred_element_type=F32)


def rms(values, gain):
    return values * lax.rsqrt(jnp.mean(values * values, -1, keepdims=True) + NORM_EPS) * gain


def rms_back(values, gain, dn):
    r = lax.rsqrt(jnp.mean(values * values, -1, keepdims=True) + NORM_EPS)
    dng = dn * gain
    dv = r * (dng - values * (r * r) * jnp.mean(dng * values, -1, keepdims=True))
    return dv, jnp.sum(dn * values * r, 0, keepdims=True)


GC = 0.7978845608028654
GA = 0.044715


def gelu(x):
    return 0.5 * x * (1.0 + jnp.tanh(GC * (x + GA * x * x * x)))


def gelu_both(x):
    th = jnp.tanh(GC * (x + GA * x * x * x))
    value = 0.5 * x * (1.0 + th)
    slope = 0.5 * (1.0 + th) + 0.5 * x * (1.0 - th * th) * GC * (1.0 + 3.0 * GA * x * x)
    return value, slope


def sigmoid(x):
    return 1.0 / (1.0 + jnp.exp(-x))


def softplus(x):
    return jnp.maximum(x, 0.0) + jnp.log(1.0 + jnp.exp(-jnp.abs(x)))


def rows_back(values, rows, k):
    return jnp.where(rows >= k, pltpu.roll(values, k, 0), 0.0)


def rows_ahead(values, rows, k):
    return jnp.where(rows < SEQ - k, pltpu.roll(values, SEQ - k, 0), 0.0)


def blocks_kernel(
    x_ref, cot_ref, sm_in, win, wgt, wro, wg, wu, wd, wq, wkv, wao,
    y_o, dx_o, gp, gr,
    s_in, s_gt, s_ro, s_sm, s_g, s_u, s_d, s_q, s_kv, s_ao,
    ag, sb, rb, res, n1_s, uv_s, c_s, ig_s, rg_s, a_s, h_s, o_s,
    q_s, kv_s, p_s, at_s, gate_s, up_s, hid_s, dg_s, du_s, both_s,
    dkvb, gnb, stg, stg_r, yb, xb,
    wl_sem, ws_sem, wr_sem, ags_sem, agr_sem, rss_sem, rsr_sem,
    kvs_sem, kvr_sem, gns_sem, gnr_sem, st_sem, dl_sem, dls_sem, dlr_sem,
):
    s = lax.axis_index("section")
    t = lax.axis_index("tensor")
    d = lax.axis_index("dp")
    peers = [lax.rem(t + k, 4) for k in range(4)]
    mine = pl.ds(pl.multiple_of(t * SH, SH), SH)

    barrier = pltpu.get_barrier_semaphore()
    for k in range(4):
        if k:
            pl.semaphore_signal(barrier, inc=1, device_id=(s, peers[k], d), device_id_type=MESH)
        pl.semaphore_signal(barrier, inc=1, device_id=(1 - s, peers[k], d), device_id_type=MESH)

    half_in = pl.ds(pl.multiple_of(s * 768, 768), 768)
    half_gt = pl.ds(pl.multiple_of(s * 64, 64), 64)
    moves = [
        (win, s_in.at[half_in, :]),
        (sm_in, s_sm.at[s]),
        (wgt, s_gt.at[half_gt, :]),
        (wro, s_ro.at[s]),
        (wg.at[0], s_g.at[s]),
        (wu.at[0], s_u.at[s]),
        (wd.at[0], s_d.at[s]),
        (wq, s_q.at[half_in, :]),
        (wkv, s_kv.at[half_in, :]),
        (wao, s_ao.at[s]),
    ]
    local = [pltpu.make_async_copy(a, b, wl_sem.at[i]) for i, (a, b) in enumerate(moves)]
    swap = [
        pltpu.make_async_remote_copy(
            src_ref=a, dst_ref=b, send_sem=ws_sem.at[i], recv_sem=wr_sem.at[i],
            device_id=(1 - s, t, d), device_id_type=MESH,
        )
        for i, (a, b) in enumerate(moves)
    ]
    for copy in local:
        copy.start()
    pl.semaphore_wait(barrier, 7)
    for copy in swap:
        copy.start()

    def weights(*which):
        for i in which:
            local[i].wait()
            swap[i].wait_recv()

    def gather(p):
        return [
            pltpu.make_async_remote_copy(
                src_ref=ag.at[p, mine], dst_ref=ag.at[p, mine],
                send_sem=ags_sem.at[p, k], recv_sem=agr_sem.at[p, k],
                device_id=(s, peers[k], d), device_id_type=MESH,
            )
            for k in range(1, 4)
        ]

    def gather_start(p, shard):
        ag[p, mine, :] = shard.astype(BF)
        for copy in gather(p):
            copy.start()

    def gather_wait(p):
        for copy in gather(p):
            copy.wait()

    def scatter(p):
        return [
            pltpu.make_async_remote_copy(
                src_ref=sb.at[p, pl.ds(pl.multiple_of(peers[k] * SH, SH), SH)],
                dst_ref=rb.at[p, k - 1],
                send_sem=rss_sem.at[p, k], recv_sem=rsr_sem.at[p, k],
                device_id=(s, peers[k], d), device_id_type=MESH,
            )
            for k in range(1, 4)
        ]

    def scatter_start(p):
        for copy in scatter(p):
            copy.start()

    def scatter_wait(p):
        for copy in scatter(p):
            copy.wait()
        total = sb[p, mine, :].astype(F32)
        for k in range(3):
            total = total + rb[p, k].astype(F32)
        return total

    def deliver(shard, buf, out, core, which):
        buf[...] = shard.astype(BF)

        @pl.when(s == core)
        def _():
            own = pltpu.make_async_copy(buf, out.at[s, mine], dl_sem.at[which])
            own.start()
            for k in range(1, 4):
                deliver_copy(buf, out, core, which, k).start()
            own.wait()

        @pl.when(s != core)
        def _():
            for k in range(4):
                deliver_copy(buf, out, core, which, k).start()

    def deliver_copy(buf, out, core, which, k):
        return pltpu.make_async_remote_copy(
            src_ref=buf, dst_ref=out.at[s, mine],
            send_sem=dls_sem.at[which, k], recv_sem=dlr_sem.at[which, s, k],
            device_id=(core, peers[k], d), device_id_type=MESH,
        )

    def deliver_wait(buf, out, core, which):
        def landed(sender, k):
            pltpu.make_async_remote_copy(
                src_ref=buf, dst_ref=out.at[sender, mine],
                send_sem=dls_sem.at[which, k], recv_sem=dlr_sem.at[which, sender, k],
                device_id=(core, peers[k], d), device_id_type=MESH,
            ).wait_recv()

        @pl.when(s == core)
        def _():
            for k in range(1, 4):
                deliver_copy(buf, out, core, which, k).wait_send()
                landed(core, k)
            for k in range(4):
                landed(1 - core, k)

        @pl.when(s != core)
        def _():
            for k in range(4):
                deliver_copy(buf, out, core, which, k).wait_send()

    pending = [None, None]
    count = [0]

    def stage(item, half, fill):
        slot = count[0] % 2
        count[0] += 1
        if pending[slot] is not None:
            pending[slot].wait()
        fill(stg.at[slot])
        copy = pltpu.make_async_copy(stg.at[slot], gp.at[item, half], st_sem.at[slot])
        copy.start()
        pending[slot] = copy

    def gain(block, which):
        return s_sm[block, which : which + 1, :]

    rows = lax.broadcasted_iota(jnp.int32, (SEQ, RQ), 0)

    weights(0, 1)
    n1 = rms(x_ref[...].astype(F32), gain(0, 0)).astype(BF)
    n1_s[...] = n1
    uv_s[...] = mm(n1, s_in[...])
    taps = [s_sm[k // 2, 2 + k % 2 : 3 + k % 2, :RQ] for k in range(4)]
    vec = [s_sm[k // 2, 2 + k % 2 : 3 + k % 2, RQ : 2 * RQ] for k in range(4)]
    u = uv_s[:, :RQ]
    c = vec[0] + taps[0] * u
    for k in range(1, 4):
        c = c + taps[k] * rows_back(u, rows, k)
    c_s[...] = c
    weights(2, 3)
    for head in range(4):
        cols = slice(head * HD, head * HD + HD)
        cb = c_s[:, cols].astype(BF)
        ig_s[:, cols] = sigmoid(mm(cb, s_gt[:, cols]) + vec[1][:, cols])
        rg_s[:, cols] = sigmoid(
            mm(cb, s_gt[:, RQ + head * HD : RQ + head * HD + HD]) + vec[2][:, cols]
        )
    speed = softplus(vec[3])
    a = jnp.exp(-8.0 * rg_s[...] * speed)
    a_s[...] = a
    run = jnp.sqrt(jnp.maximum(1.0 - a * a, RATE_FLOOR)) * ig_s[...] * c_s[...]
    step = 1
    while step < SEQ:
        run = run + a * rows_back(run, rows, step)
        if 2 * step < SEQ:
            a = a * jnp.where(rows >= step, pltpu.roll(a, step, 0), 1.0)
        step *= 2
    h_s[...] = run
    o = (run * gelu(uv_s[:, RQ:])).astype(BF)
    o_s[...] = o
    for half in range(2):
        sb[0, :, half * 768 : half * 768 + 768] = mm(o, s_ro[half]).astype(BF)
    scatter_start(0)
    x_mine = x_ref[mine, :].astype(F32)
    x1 = x_mine + scatter_wait(0)
    res[0] = x1
    gather_start(0, rms(x1, gain(0, 1)))

    def ffn_forward(block, p_in, p_out):
        gather_wait(p_in)
        n2 = ag[p_in]
        for j in range(3):
            cols = slice(j * CC, j * CC + CC)
            gate = mm(n2, s_g[block, :, cols])
            up = mm(n2, s_u[block, :, cols])
            gate_s[block, :, cols] = gate
            up_s[block, :, cols] = up
            hid_s[block, :, cols] = (gelu(gate) * up).astype(BF)
        if block == 0:
            weights(6)
        hid = hid_s[block]
        for j in range(4):
            cols = slice(j * CC, j * CC + CC)
            sb[p_out, :, cols] = mm(hid, s_d[block, :, cols]).astype(BF)
        scatter_start(p_out)

    weights(4, 5)
    ffn_forward(0, 0, 1)
    mid = (res[0] + scatter_wait(1)).astype(BF).astype(F32)
    res[1] = mid
    gather_start(1, rms(mid, gain(1, 0)))

    weights(7, 8, 9)
    gather_wait(1)
    na = ag[1]
    q_s[...] = mm(na, s_q[...]).astype(BF)
    kv_s[...] = mm(na, s_kv[...]).astype(BF)
    keys = kv_s[:, :HD]
    vals = kv_s[:, HD:]
    allowed = lax.broadcasted_iota(jnp.int32, (SEQ, SEQ), 1) <= lax.broadcasted_iota(
        jnp.int32, (SEQ, SEQ), 0
    )
    for head in range(3):
        cols = slice(head * HD, head * HD + HD)
        score = jnp.where(allowed, mm_nt(q_s[:, cols], keys) * HD ** (-0.5), -1e30)
        expo = jnp.exp(score - jnp.max(score, -1, keepdims=True))
        p = expo / jnp.sum(expo, -1, keepdims=True)
        p_s[head] = p
        at_s[:, cols] = mm(p.astype(BF), vals).astype(BF)
    att = at_s[...]
    for half in range(2):
        sb[2, :, half * 768 : half * 768 + 768] = mm(att, s_ao[half]).astype(BF)
    scatter_start(2)
    x1 = res[1] + scatter_wait(2)
    res[2] = x1
    gather_start(2, rms(x1, gain(1, 1)))
    ffn_forward(1, 2, 3)
    y = res[2] + scatter_wait(3)
    deliver(y, yb, y_o, 1, 0)

    def ffn_backward(block, dF, p_n2, p_out):
        for j in range(3):
            cols = slice(j * CC, j * CC + CC)
            dhid = mm_nt(dF, s_d[block, cols, :])
            value, slope = gelu_both(gate_s[block, :, cols])
            dg_s[:, cols] = (dhid * up_s[block, :, cols] * slope).astype(BF)
            du_s[:, cols] = (dhid * value).astype(BF)
        dg = dg_s[...]
        du = du_s[...]
        for j in range(4):
            cols = slice(j * CC, j * CC + CC)
            sb[p_out, :, cols] = (
                mm_nt(dg, s_g[block, cols, :]) + mm_nt(du, s_u[block, cols, :])
            ).astype(BF)
        scatter_start(p_out)
        n2t = ag[p_n2].T
        for item, right in ((3 * block, dg_s), (3 * block + 1, du_s)):
            for half in range(2):

                def fill(ref, right=right, half=half):
                    for j in range(3):
                        part = mm(n2t[half * 768 : half * 768 + 768], right[:, j * CC : j * CC + CC])
                        ref[:, j * 48 : j * 48 + 48, :] = part.astype(BF).reshape(16, 48, CC)

                stage(item, half, fill)
        hidt = hid_s[block].T
        for half in range(2):

            def fill_down(ref, half=half):
                for j in range(4):
                    part = mm(hidt[half * 576 : half * 576 + 576], dF[:, j * CC : j * CC + CC])
                    part = part.astype(BF).reshape(4, CR, CC)
                    for i in range(4):
                        ref[i * 4 + j] = part[i]

            stage(3 * block + 2, half, fill_down)

    cot = cot_ref[...]
    ffn_backward(1, cot, 2, 4)
    dn = scatter_wait(4)
    dv, gg11 = rms_back(res[2], gain(1, 1), dn)
    dx1 = cot_ref[mine, :].astype(F32) + dv
    res[3] = dx1
    gather_start(3, dx1)

    gather_wait(3)
    dA = ag[3]
    datt_s = both_s.at[:, :AQ]
    dq_s = both_s.at[:, AQ : 2 * AQ]
    datt_s[...] = (mm_nt(dA[:, :768], s_ao[0]) + mm_nt(dA[:, 768:], s_ao[1])).astype(BF)
    dk = jnp.zeros((SEQ, HD), F32)
    dw = jnp.zeros((SEQ, HD), F32)
    for head in range(3):
        cols = slice(head * HD, head * HD + HD)
        p = p_s[head]
        datt = datt_s[:, cols]
        dpr = mm_nt(datt, kv_s[:, HD:])
        dw = dw + mm(p.astype(BF).T, datt)
        ds = (p * (dpr - jnp.sum(p * dpr, -1, keepdims=True)) * HD ** (-0.5)).astype(BF)
        dq_s[:, cols] = mm(ds, kv_s[:, :HD]).astype(BF)
        dk = dk + mm(ds.T, q_s[:, cols])
    dkvb[0, :, :HD] = dk.astype(BF)
    dkvb[0, :, HD:] = dw.astype(BF)
    kv_copies = [
        pltpu.make_async_remote_copy(
            src_ref=dkvb.at[0], dst_ref=dkvb.at[k], send_sem=kvs_sem.at[k], recv_sem=kvr_sem.at[k],
            device_id=(s, peers[k], d), device_id_type=MESH,
        )
        for k in range(1, 4)
    ]
    for copy in kv_copies:
        copy.start()
    dq = dq_s[...]
    for j in range(4):
        cols = slice(j * CC, j * CC + CC)
        sb[5, :, cols] = mm_nt(dq, s_q[cols, :]).astype(BF)
    scatter_start(5)
    for copy in kv_copies:
        copy.wait()
    total = dkvb[0].astype(F32)
    for k in range(1, 4):
        total = total + dkvb[k].astype(F32)
    dkv_s = both_s.at[:, 2 * AQ : 2 * AQ + 256]
    dkv_s[...] = total.astype(BF)
    nat = ag[1].T
    attt = at_s[...].T
    for half in range(2):

        def fill_att(ref, half=half):
            top = nat[half * 768 : half * 768 + 768]
            ref[:, :48, :] = mm(top, dq_s[...]).astype(BF).reshape(16, 48, CC)
            ref[:, 96:144, :256] = mm(top, dkv_s[...]).astype(BF).reshape(16, 48, 256)
            ref[:, 96:144, 256:] = jnp.zeros((16, 48, 128), BF)
            for j in range(2):
                at = half * 768 + j * CC
                part = mm(attt, dA[:, at : at + CC]).astype(BF).reshape(8, 48, CC)
                for i in range(8):
                    ref[i * 2 + j, 48:96, :] = part[i]

        stage(ITEM_ATT, half, fill_att)
    dn = scatter_wait(5) + mm_nt(dkv_s[mine, :], s_kv[...])
    dv, gg10 = rms_back(res[1], gain(1, 0), dn)
    dmid = res[3] + dv
    big_g = dmid.astype(BF).astype(F32)
    gather_start(4, big_g)
    res[3] = big_g
    gather_wait(4)
    ffn_backward(0, ag[4], 0, 6)
    dn = scatter_wait(6)
    dv, gg01 = rms_back(res[0], gain(0, 1), dn)
    dx1 = res[3] + dv
    res[3] = dx1
    gather_start(5, dx1)

    gather_wait(5)
    dA = ag[5]
    dO = mm_nt(dA[:, :768], s_ro[0]) + mm_nt(dA[:, 768:], s_ro[1])
    value, slope = gelu_both(uv_s[:, RQ:])
    h = h_s[...]
    both_s[:, RQ:] = (dO * h * slope).astype(BF)
    e = dO * value
    a = a_s[...]
    coef = rows_ahead(a, rows, 1)
    step = 1
    while step < SEQ:
        e = e + coef * rows_ahead(e, rows, step)
        if 2 * step < SEQ:
            coef = coef * rows_ahead(coef, rows, step)
        step *= 2
    ig = ig_s[...]
    rg = rg_s[...]
    c = c_s[...]
    room = 1.0 - a * a
    m = jnp.sqrt(jnp.maximum(room, RATE_FLOOR))
    ga = e * rows_back(h, rows, 1) - jnp.where(room > RATE_FLOOR, e * ig * c * a / m, 0.0)
    dl = ga * a
    gv3 = jnp.sum(dl * rg, 0, keepdims=True) * (-8.0) * sigmoid(vec[3])
    er = -8.0 * dl * speed * rg * (1.0 - rg)
    ei = e * m * c * ig * (1.0 - ig)
    gv1 = jnp.sum(ei, 0, keepdims=True)
    gv2 = jnp.sum(er, 0, keepdims=True)
    c_s[...] = e * m * ig
    ig_s[...] = ei
    rg_s[...] = er
    gts = []
    for head in range(4):
        cols = slice(head * HD, head * HD + HD)
        dpin = ig_s[:, cols].astype(BF)
        dprec = rg_s[:, cols].astype(BF)
        cbt = c[:, cols].astype(BF).T
        gts.append((mm(cbt, dpin), mm(cbt, dprec)))
        c_s[:, cols] += mm_nt(dpin, s_gt[:, cols]) + mm_nt(
            dprec, s_gt[:, RQ + head * HD : RQ + head * HD + HD]
        )
    dc = c_s[...]
    u = uv_s[:, :RQ]
    du = taps[0] * dc
    gtap = [jnp.sum(u * dc, 0, keepdims=True)]
    for k in range(1, 4):
        du = du + taps[k] * rows_ahead(dc, rows, k)
        gtap.append(jnp.sum(rows_back(u, rows, k) * dc, 0, keepdims=True))
    gv0 = jnp.sum(dc, 0, keepdims=True)
    both_s[:, :RQ] = du.astype(BF)
    both = both_s[...]
    for j in range(4):
        cols = slice(j * CC, j * CC + CC)
        sb[7, :, cols] = mm_nt(both, s_in[cols, :]).astype(BF)
    scatter_start(7)
    ot = o_s[...].T
    n1t = n1_s[...].T
    for half in range(2):
        for j in range(2):
            at = half * 768 + j * CC
            part = mm(ot, dA[:, at : at + CC]).astype(BF).reshape(8, RR, CC)
            for i in range(8):
                stg_r[half, i * 2 + j] = part[i]
        out_r = pltpu.make_async_copy(stg_r.at[half], gr.at[half], dl_sem.at[2 + half])
        out_r.start()

    dn = scatter_wait(7)
    dv, gg00 = rms_back(x_mine, gain(0, 0), dn)
    deliver(res[3] + dv, xb, dx_o, 0, 1)
    gnb[0, 0:1] = gg00
    gnb[0, 1:2] = gg01
    gnb[0, 2:3] = gg10
    gnb[0, 3:4] = gg11
    gnb[0, 4:8] = jnp.zeros((4, D), F32)
    gn_copies = [
        pltpu.make_async_remote_copy(
            src_ref=gnb.at[0], dst_ref=gnb.at[k], send_sem=gns_sem.at[k], recv_sem=gnr_sem.at[k],
            device_id=(s, peers[k], d), device_id_type=MESH,
        )
        for k in range(1, 4)
    ]
    for copy in gn_copies:
        copy.start()
    for copy in gn_copies:
        copy.wait()
    gains = gnb[0] + gnb[1] + gnb[2] + gnb[3]
    gvec = [gv0, gv1, gv2, gv3]
    for half in range(2):

        def fill_rec(ref, half=half):
            top = n1t[half * 768 : half * 768 + 768]
            for j, width in enumerate((CC, CC, 256)):
                part = mm(top, both_s[:, j * CC : j * CC + width])
                ref[:, j * 48 : j * 48 + 48, :width] = part.astype(BF).reshape(16, 48, width)
            for q in range(2):
                for head in range(4):
                    part = gts[head][q][half * 64 : half * 64 + 64].astype(BF)
                    for r in range(2):
                        ref[(q * 4 + head) * 2 + r, 96:128, 256:] = part[r * 32 : r * 32 + 32]
            ref[:, 128:144, 256:] = jnp.zeros((16, 16, HD), BF)
            blank = jnp.zeros((10, HD), F32)
            for i in range(12):
                lanes = slice(i * HD, i * HD + HD)
                pieces = [gains[2 * half : 2 * half + 2, lanes]]
                if i < 4:
                    pieces += [gtap[2 * half][:, lanes], gtap[2 * half + 1][:, lanes]]
                    pieces += [gvec[2 * half][:, lanes], gvec[2 * half + 1][:, lanes]]
                else:
                    pieces.append(jnp.zeros((4, HD), F32))
                ref[i, 128:144, 256:] = jnp.concatenate(pieces + [blank], 0).astype(BF)

        stage(ITEM_REC, half, fill_rec)
    for half in range(2):
        pltpu.make_async_copy(stg_r.at[half], gr.at[half], dl_sem.at[2 + half]).wait()
    for copy in pending:
        copy.wait()
    for copy in swap:
        copy.wait_send()
    deliver_wait(yb, y_o, 1, 0)
    deliver_wait(xb, dx_o, 0, 1)


def blocks_call(x, cot, small, weights):
    vm = pl.BlockSpec(memory_space=pltpu.VMEM)
    hbm = pl.BlockSpec(memory_space=pl.ANY)
    V = pltpu.VMEM
    dma = pltpu.SemaphoreType.DMA
    return pl.pallas_call(
        blocks_kernel,
        name="blocks",
        out_shape=[
            jax.ShapeDtypeStruct((2, SEQ, D), BF),
            jax.ShapeDtypeStruct((2, SEQ, D), BF),
            jax.ShapeDtypeStruct((N_ITEMS, 2, 16, CR, CC), BF),
            jax.ShapeDtypeStruct((2, 16, RR, CC), BF),
        ],
        in_specs=[vm, vm, hbm] + [hbm] * 9,
        out_specs=[hbm] * 4,
        scratch_shapes=[
            V((D, 2 * RQ), BF), V((HD, 2 * RQ), BF), V((2, RQ, 768), BF), V((2, 8, D), F32),
            V((2, D, FQ), BF), V((2, D, FQ), BF), V((2, FQ, D), BF),
            V((D, AQ), BF), V((D, 256), BF), V((2, AQ, 768), BF),
            V((6, SEQ, D), BF), V((8, SEQ, D), BF), V((8, 3, SH, D), BF), V((4, SH, D), F32),
            V((SEQ, D), BF), V((SEQ, 2 * RQ), F32),
            V((SEQ, RQ), F32), V((SEQ, RQ), F32), V((SEQ, RQ), F32), V((SEQ, RQ), F32), V((SEQ, RQ), F32),
            V((SEQ, RQ), BF),
            V((SEQ, AQ), BF), V((SEQ, 256), BF), V((3, SEQ, SEQ), F32), V((SEQ, AQ), BF),
            V((2, SEQ, FQ), F32), V((2, SEQ, FQ), F32), V((2, SEQ, FQ), BF),
            V((SEQ, FQ), BF), V((SEQ, FQ), BF), V((SEQ, 2 * RQ), BF),
            V((4, SEQ, 256), BF), V((4, 8, D), F32), V((2, 16, CR, CC), BF), V((2, 16, RR, CC), BF),
            V((SH, D), BF), V((SH, D), BF),
            dma((10,)), dma((10,)), dma((10,)), dma((6, 4)), dma((6, 4)), dma((8, 4)), dma((8, 4)),
            dma((4,)), dma((4,)), dma((4,)), dma((4,)), dma((2,)), dma((4,)), dma((2, 4)), dma((2, 2, 4)),
        ],
        compiler_params=pltpu.CompilerParams(
            collective_id=0, has_side_effects=True, vmem_limit_bytes=62 * 2**20
        ),
    )(x, cot, small, *weights)


def reduce_kernel(
    gp, gr, fo, mo, ro,
    g, gx, hb, hx, r1a, r1b, r2a, r2b, x1a, x1b, x2a, x2b,
    l_sem, cs_sem, cr_sem, s_sem, r_sem, o_sem, ps_sem, pr_sem,
):
    s = lax.axis_index("section")
    t = lax.axis_index("tensor")
    d = lax.axis_index("dp")
    px = lax.rem(d, 4)
    py = d // 4

    def along(axis, k):
        if axis == 0:
            return (s, t, py * 4 + lax.rem(px + k, 4))
        return (s, t, lax.rem(py + k, 4) * 4 + px)

    other = (1 - s, t, d)
    barrier = pltpu.get_barrier_semaphore()
    for target in (other, along(0, 1), along(0, 3), along(1, 1), along(1, 3)):
        pl.semaphore_signal(barrier, inc=1, device_id=target, device_id_type=MESH)

    n_all = N_ITEMS + 1
    place = [px, py]

    class Item:
        pass

    items = []
    for i in range(n_all):
        it = Item()
        it.i = i
        big = i < N_ITEMS
        it.g = g.at[i] if big else gx
        it.h = hb.at[i] if big else hx
        it.r1a = r1a.at[i] if big else x1a
        it.r1b = r1b.at[i] if big else x1b
        it.r2a = r2a.at[i] if big else x2a
        it.r2b = r2b.at[i] if big else x2b
        it.src = gp.at[i] if big else gr
        it.rows = CR if big else RR
        it.cut = HALF_A if big else 32
        it.first = i % 2
        it.m = place[it.first]
        it.n = place[1 - it.first]
        it.waits = []
        items.append(it)

    def pos(base, k):
        return lax.rem(base + k, 4)

    def send(it, step, side, axis, src, dst):
        copy = pltpu.make_async_remote_copy(
            src_ref=src, dst_ref=dst,
            send_sem=s_sem.at[it.i, step, side], recv_sem=r_sem.at[it.i, step, side],
            device_id=along(axis, 1 if side == 0 else 3), device_id_type=MESH,
        )
        copy.start()
        it.waits.append(copy)

    def settle(it):
        for copy in it.waits:
            copy.wait()
        it.waits = []

    def quarter(ref, it, k, lo=0, n=4):
        return ref.at[pl.ds(pos(it.m, k) * 4 + lo, n)]

    def chunk(ref, it, k, lo, n):
        return ref.at[it.m * 4 + pos(it.n, k), pl.ds(lo, n)]

    def add_into(ref, start, n, *others):
        def body(j, carry):
            total = ref[start + j].astype(F32)
            for o in others:
                total = total + o[j].astype(F32)
            ref[start + j] = total.astype(BF)
            return carry

        lax.fori_loop(0, n, body, 0)

    own = []
    for it in items:
        copy = pltpu.make_async_copy(it.src.at[s], it.g, l_sem.at[it.i])
        copy.start()
        own.append(copy)
    pl.semaphore_wait(barrier, 5)
    swap = []
    for it in items:
        copy = pltpu.make_async_remote_copy(
            src_ref=it.src.at[1 - s], dst_ref=it.h, send_sem=cs_sem.at[it.i], recv_sem=cr_sem.at[it.i],
            device_id=other, device_id_type=MESH,
        )
        copy.start()
        swap.append(copy)

    for it in items:
        own[it.i].wait()
        swap[it.i].wait()
        add_into(it.g, 0, 16, it.h)
        send(it, 0, 0, it.first, quarter(it.g, it, 2, 0, 2), it.r1a.at[0])
        send(it, 0, 1, it.first, quarter(it.g, it, 2, 2, 2), it.r1a.at[1])
    for it in items:
        settle(it)
        add_into(it.g, pos(it.m, 1) * 4, 2, it.r1a.at[0])
        add_into(it.g, pos(it.m, 3) * 4 + 2, 2, it.r1a.at[1])
        send(it, 1, 0, it.first, quarter(it.g, it, 1), it.r1b.at[0])
        send(it, 1, 1, it.first, quarter(it.g, it, 3), it.r1b.at[1])
    for it in items:
        settle(it)
        add_into(it.g, it.m * 4, 4, it.r1b.at[0], it.r1b.at[1])
        send(it, 2, 0, 1 - it.first, chunk(it.g, it, 2, 0, it.cut), it.r2a.at[pl.ds(0, it.cut)])
        send(
            it, 2, 1, 1 - it.first, chunk(it.g, it, 2, it.cut, it.rows - it.cut),
            it.r2a.at[pl.ds(it.cut, it.rows - it.cut)],
        )
    for it in items:
        settle(it)
        at = it.m * 4 + pos(it.n, 1)
        it.g[at, : it.cut] = it.g[at, : it.cut] + it.r2a[: it.cut]
        at = it.m * 4 + pos(it.n, 3)
        it.g[at, it.cut :] = it.g[at, it.cut :] + it.r2a[it.cut :]
        send(it, 3, 0, 1 - it.first, chunk(it.g, it, 1, 0, it.rows), it.r2b.at[0])
        send(it, 3, 1, 1 - it.first, chunk(it.g, it, 3, 0, it.rows), it.r2b.at[1])
    for it in items:
        settle(it)
        here = it.m * 4 + it.n
        it.h[here] = (
            it.g[here].astype(F32) + it.r2b[0].astype(F32) + it.r2b[1].astype(F32)
        ).astype(BF)
        here = chunk(it.h, it, 0, 0, it.rows)
        send(it, 4, 0, 1 - it.first, here, here)
        send(it, 4, 1, 1 - it.first, here, here)
    for it in items:
        settle(it)
        part = chunk(it.h, it, 3, 0, it.cut)
        send(it, 5, 0, 1 - it.first, part, part)
        part = chunk(it.h, it, 1, it.cut, it.rows - it.cut)
        send(it, 5, 1, 1 - it.first, part, part)
    for it in items:
        settle(it)
        here = quarter(it.h, it, 0)
        send(it, 6, 0, it.first, here, here)
        send(it, 6, 1, it.first, here, here)
    for it in items:
        settle(it)
        part = quarter(it.h, it, 3, 0, 2)
        send(it, 7, 0, it.first, part, part)
        part = quarter(it.h, it, 1, 2, 2)
        send(it, 7, 1, it.first, part, part)
    outs = []
    for it in items:
        settle(it)
        if it.i == ITEM_ATT or it.i == ITEM_REC:
            copy = pltpu.make_async_copy(it.h, mo.at[it.i - ITEM_ATT], o_sem.at[it.i])
            copy.start()
            outs.append(copy)
        elif it.i == N_ITEMS:
            copy = pltpu.make_async_copy(it.h, ro, o_sem.at[it.i])
            copy.start()
            outs.append(copy)
    for m in range(3):
        copy = pltpu.make_async_copy(hb.at[3 * s + m], fo.at[m, s], o_sem.at[m])
        copy.start()
        outs.append(copy)
        copy = pltpu.make_async_remote_copy(
            src_ref=hb.at[3 * (1 - s) + m], dst_ref=fo.at[m, s], send_sem=ps_sem.at[m], recv_sem=pr_sem.at[m],
            device_id=other, device_id_type=MESH,
        )
        copy.start()
        outs.append(copy)
    for copy in outs:
        copy.wait()


def reduce_call(gp, gr):
    hbm = pl.BlockSpec(memory_space=pl.ANY)
    V = pltpu.VMEM
    dma = pltpu.SemaphoreType.DMA
    n = N_ITEMS
    return pl.pallas_call(
        reduce_kernel,
        name="reduce",
        out_shape=[
            jax.ShapeDtypeStruct((3, 2, 16, CR, CC), BF),
            jax.ShapeDtypeStruct((2, 16, CR, CC), BF),
            jax.ShapeDtypeStruct((16, RR, CC), BF),
        ],
        in_specs=[hbm, hbm],
        out_specs=[hbm] * 3,
        scratch_shapes=[
            V((n, 16, CR, CC), BF), V((16, RR, CC), BF),
            V((n, 16, CR, CC), BF), V((16, RR, CC), BF),
            V((n, 2, 2, CR, CC), BF), V((n, 2, 4, CR, CC), BF), V((n, CR, CC), BF), V((n, 2, CR, CC), BF),
            V((2, 2, RR, CC), BF), V((2, 4, RR, CC), BF), V((RR, CC), BF), V((2, RR, CC), BF),
            dma((n + 1,)), dma((n + 1,)), dma((n + 1,)), dma((n + 1, 8, 2)), dma((n + 1, 8, 2)),
            dma((n + 1,)), dma((3,)), dma((3,)),
        ],
        compiler_params=pltpu.CompilerParams(
            collective_id=1, has_side_effects=True, vmem_limit_bytes=62 * 2**20
        ),
    )(gp, gr)


def per_device(
    tokens, plan_order, cotangent, norm_gains, ffn_gate, ffn_up, ffn_down,
    rec_in, rec_gates, rec_conv, rec_vec, rec_out, att_q, att_kv, att_out,
):
    s = lax.axis_index("section")
    plan = plan_order[0]
    seqs = tokens.reshape(2, SEQ, D)
    x = jnp.where(plan[s] == 0, seqs[0], seqs[1])
    cot = lax.dynamic_index_in_dim(cotangent.reshape(2, SEQ, D), s, 0, keepdims=False)
    small = jnp.zeros((8, D), F32)
    small = small.at[0:2].set(norm_gains[0])
    small = small.at[2:4, :RQ].set(rec_conv.astype(F32))
    small = small.at[2:4, RQ : 2 * RQ].set(rec_vec.astype(F32))
    y, dx, gp, gr = blocks_call(
        x, cot, small,
        (
            rec_in.reshape(768, 2 * RQ), rec_gates.reshape(64, 2 * RQ), rec_out,
            ffn_gate, ffn_up, ffn_down, att_q, att_kv, att_out,
        ),
    )
    fo, mo, ro = reduce_call(gp, gr)
    in_order = jnp.where(plan[0] == 0, dx, dx[::-1])
    boundary = jnp.where(s == 0, in_order, y).astype(F32).reshape(1, 2 * SEQ, D)

    def wide(part):
        return part.reshape(2, 16, 3, 48, CC).transpose(0, 1, 3, 2, 4).reshape(1, D, FQ).astype(F32)

    g_gate = wide(fo[0])
    g_up = wide(fo[1])
    g_down = (
        fo[2].reshape(2, 4, 4, CR, CC).transpose(0, 1, 3, 2, 4).reshape(1, FQ, D).astype(F32)
    )
    att, rec = mo[0], mo[1]
    g_q = att[:, :48].reshape(768, AQ).astype(F32)
    g_kv = att[:, 96:, :256].reshape(768, 256).astype(F32)
    g_ao = att[:, 48:96].reshape(8, 2, 48, CC).transpose(0, 2, 1, 3).reshape(AQ, 768).astype(F32)
    g_ro = ro.reshape(8, 2, RR, CC).transpose(0, 2, 1, 3).reshape(RQ, 768).astype(F32)
    g_in = jnp.concatenate(
        [rec[:, :48].reshape(768, CC), rec[:, 48:96].reshape(768, CC), rec[:, 96:, :256].reshape(768, 256)], 1
    )
    g_in = g_in.reshape(768, 2, RQ).astype(F32)
    g_gt = rec[:, 96:128, 256:].reshape(8, 64, HD).transpose(1, 0, 2).reshape(64, 2, RQ).astype(F32)
    tiny = rec[:12, 128:144, 256:].transpose(1, 0, 2).reshape(16, D).astype(F32)
    return (
        boundary, tiny[0:2][None], g_gate, g_up, g_down, g_in, g_gt,
        tiny[2:4, :RQ], tiny[4:6, :RQ], g_ro, g_q, g_kv, g_ao,
    )


def solution(mesh):
    placed = (
        P("dp", None),
        P("dp", None),
        P("dp", None),
        P("section", None, None),
        P("section", None, "tensor"),
        P("section", None, "tensor"),
        P("section", "tensor", None),
        P("section", None, "tensor"),
        P("section", None, "tensor"),
        P("section", "tensor"),
        P("section", "tensor"),
        P("tensor", "section"),
        P("section", "tensor"),
        P("section", None),
        P("tensor", "section"),
    )
    return jax.shard_map(
        per_device,
        mesh=mesh,
        in_specs=placed,
        out_specs=(
            P("section", "dp", None),
            P("section", None, None),
            P("section", None, "tensor"),
            P("section", None, "tensor"),
            P("section", "tensor", None),
            P("section", None, "tensor"),
            P("section", None, "tensor"),
            P("section", "tensor"),
            P("section", "tensor"),
            P("tensor", "section"),
            P("section", "tensor"),
            P("section", None),
            P("tensor", "section"),
        ),
        check_vma=False,
    )
```

```python
import jax
import jax.numpy as jnp
from jax import lax
from jax.experimental import pallas as pl
from jax.experimental.pallas import tpu as pltpu
from jax.sharding import PartitionSpec as P

HD = 128
SEQ = 128
NORM_EPS = 1e-06
RATE_FLOOR = 0.01
BF = jnp.bfloat16
F32 = jnp.float32
MESH = pl.DeviceIdType.MESH
NT = (((1,), (1,)), ((), ()))

D = 1536
FQ = 1152
RQ = 512
AQ = 384
SH = 32
CC = 384
HW = 768
X_AXIS = 0
Y_AXIS = 1
GU1, DN1, GU2, DN2, QKV, AO, IN, RO, MISC = range(9)
PLAN = {
    GU1: ("r", 2 * FQ, Y_AXIS),
    DN1: ("c", FQ, X_AXIS),
    GU2: ("r", 2 * FQ, X_AXIS),
    DN2: ("c", FQ, Y_AXIS),
    QKV: ("r", 640, Y_AXIS),
    AO: ("c", AQ, Y_AXIS),
    IN: ("r", 1024, X_AXIS),
    RO: ("c", RQ, X_AXIS),
    MISC: ("r", HD, Y_AXIS),
}
RING_AXIS = (X_AXIS, Y_AXIS, Y_AXIS, X_AXIS)


def mm(left, right):
    return jnp.dot(left, right, preferred_element_type=F32)


def mm_nt(left, right):
    return lax.dot_general(left, right, NT, preferred_element_type=F32)


def rms(values, gain):
    return values * lax.rsqrt(jnp.mean(values * values, -1, keepdims=True) + NORM_EPS) * gain


def rms_back(values, gain, dn):
    r = lax.rsqrt(jnp.mean(values * values, -1, keepdims=True) + NORM_EPS)
    dng = dn * gain
    dv = r * (dng - values * (r * r) * jnp.mean(dng * values, -1, keepdims=True))
    return dv, jnp.sum(dn * values * r, 0, keepdims=True)


GC = 0.7978845608028654
GA = 0.044715


def gelu(x):
    return 0.5 * x * (1.0 + jnp.tanh(GC * (x + GA * x * x * x)))


def gelu_both(x):
    th = jnp.tanh(GC * (x + GA * x * x * x))
    value = 0.5 * x * (1.0 + th)
    slope = 0.5 * (1.0 + th) + 0.5 * x * (1.0 - th * th) * GC * (1.0 + 3.0 * GA * x * x)
    return value, slope


def sigmoid(x):
    return 1.0 / (1.0 + jnp.exp(-x))


def softplus(x):
    return jnp.maximum(x, 0.0) + jnp.log(1.0 + jnp.exp(-jnp.abs(x)))


def rows_back(values, rows, k):
    return jnp.where(rows >= k, pltpu.roll(values, k, 0), 0.0)


def rows_ahead(values, rows, k):
    return jnp.where(rows < SEQ - k, pltpu.roll(values, SEQ - k, 0), 0.0)


class Item:
    pass


def whole_kernel(
    tok_ref, plan_ref, cot_ref, gain_ref, conv_ref, vec_ref,
    win, wgt, wro, wg, wu, wd, wq, wkv, wao,
    y_o, dx_o, ra, f_gu, f_dn, f_qkv, f_ao, f_in, f_ro, f_misc,
    s_in, s_gt, s_ro, s_sm, s_g, s_u, s_d, s_q, s_kv, s_ao,
    ag, sb, rb, res, x_s, n1_s, uv_s, c_s, ig_s, rg_s, a_s, h_s,
    q_s, kv_s, p_s, at_s, gate_s, up_s, hid_s, du_s, both_s,
    dkvb, gnb, yb, xb, smb,
    work, hid_t, o_t, att_t, gu_t, qkv_t, in_t, misc_t,
    la1, la2, la_o, la_a, rc1, rc2, rc_o, rc_a, l_gu1, l_gu2, l_qkv, l_in, l_misc,
    a_gu1, a_dn1, a_gu2, a_dn2, a_qkv, a_ao, a_in, a_ro, a_misc,
    r_gu1, r_dn1, r_gu2, r_dn2, r_qkv, r_ao, r_in, r_ro, r_misc,
    e_gu1, e_dn1, e_gu2, e_dn2, e_qkv, e_ao, e_in, e_ro, e_misc,
    wl_sem, ws_sem, wr_sem, ags_sem, agr_sem, rss_sem, rsr_sem,
    kvs_sem, kvr_sem, gns_sem, gnr_sem, dl_sem, dls_sem, dlr_sem,
    rgs_sem, rgr_sem, wk_sem, xs_sem, xr_sem, ys_sem, yr_sem, gs_sem, gr_sem, loc_sem,
):
    s = lax.axis_index("section")
    t = lax.axis_index("tensor")
    d = lax.axis_index("dp")
    place = (lax.rem(d, 4), d // 4)
    peers = [lax.rem(t + k, 4) for k in range(4)]
    mine = pl.ds(pl.multiple_of(t * SH, SH), SH)

    def pos(base, k):
        return lax.rem(base + k, 4)

    def along(axis, k, core):
        if axis == X_AXIS:
            return (core, t, place[1] * 4 + pos(place[0], k))
        return (core, t, pos(place[1], k) * 4 + place[0])

    barrier = pltpu.get_barrier_semaphore()
    for k in range(4):
        for core in (s, 1 - s):
            if k:
                for axis in (X_AXIS, Y_AXIS):
                    pl.semaphore_signal(
                        barrier, inc=1, device_id=along(axis, k, core), device_id_type=MESH
                    )
                pl.semaphore_signal(
                    barrier, inc=1, device_id=(core, peers[k], d), device_id_type=MESH
                )
    other = (1 - s, t, d)
    pl.semaphore_signal(barrier, inc=1, device_id=other, device_id_type=MESH)

    def push(src, dst, send_sem, recv_sem, target):
        return pltpu.make_async_remote_copy(
            src_ref=src, dst_ref=dst, send_sem=send_sem, recv_sem=recv_sem,
            device_id=target, device_id_type=MESH,
        )

    smb[...] = jnp.zeros((8, D), F32)
    smb[0:2, :] = gain_ref[0]
    smb[2:4, :RQ] = conv_ref[...].astype(F32)
    smb[2:4, RQ : 2 * RQ] = vec_ref[...].astype(F32)
    half_in = pl.ds(pl.multiple_of(s * HW, HW), HW)
    half_gt = pl.ds(pl.multiple_of(s * 64, 64), 64)
    moves = [
        (win, s_in.at[half_in, :]),
        (smb, s_sm.at[s]),
        (wgt, s_gt.at[half_gt, :]),
        (wro, s_ro.at[s]),
        (wg.at[0], s_g.at[s]),
        (wu.at[0], s_u.at[s]),
        (wd.at[0], s_d.at[s]),
        (wq, s_q.at[half_in, :]),
        (wkv, s_kv.at[half_in, :]),
        (wao, s_ao.at[s]),
    ]
    local = [pltpu.make_async_copy(a, b, wl_sem.at[i]) for i, (a, b) in enumerate(moves)]
    swap = [push(a, b, ws_sem.at[i], wr_sem.at[i], other) for i, (a, b) in enumerate(moves)]
    for copy in local:
        copy.start()
    pl.semaphore_wait(barrier, 19)
    for copy in swap:
        copy.start()

    def weights(*which):
        for i in which:
            local[i].wait()
            swap[i].wait_recv()


    def gather(p):
        return [
            push(ag.at[p, mine], ag.at[p, mine], ags_sem.at[p, k], agr_sem.at[p, k], (s, peers[k], d))
            for k in range(1, 4)
        ]

    def gather_start(p, shard):
        ag[p, mine, :] = shard.astype(BF)
        for copy in gather(p):
            copy.start()

    def gather_wait(p):
        for copy in gather(p):
            copy.wait()

    def scatter(p):
        return [
            push(
                sb.at[p % 2, pl.ds(pl.multiple_of(peers[k] * SH, SH), SH)], rb.at[p % 2, k - 1],
                rss_sem.at[p, k], rsr_sem.at[p, k], (s, peers[k], d),
            )
            for k in range(1, 4)
        ]

    def scatter_start(p):
        for copy in scatter(p):
            copy.start()

    def scatter_wait(p):
        for copy in scatter(p):
            copy.wait()
        total = sb[p % 2, mine, :].astype(F32)
        for k in range(3):
            total = total + rb[p % 2, k].astype(F32)
        return total

    def deliver(shard, buf, out, core, which):
        buf[...] = shard.astype(BF)

        @pl.when(s == core)
        def _():
            own = pltpu.make_async_copy(buf, out.at[s, mine], dl_sem.at[which])
            own.start()
            for k in range(1, 4):
                deliver_copy(buf, out, core, which, k).start()
            own.wait()

        @pl.when(s != core)
        def _():
            for k in range(4):
                deliver_copy(buf, out, core, which, k).start()

    def deliver_copy(buf, out, core, which, k):
        return push(
            buf, out.at[s, mine], dls_sem.at[which, k], dlr_sem.at[which, s, k], (core, peers[k], d)
        )

    def deliver_wait(buf, out, core, which):
        def landed(sender, k):
            push(
                buf, out.at[sender, mine], dls_sem.at[which, k], dlr_sem.at[which, sender, k],
                (core, peers[k], d),
            ).wait_recv()

        @pl.when(s == core)
        def _():
            for k in range(1, 4):
                deliver_copy(buf, out, core, which, k).wait_send()
                landed(core, k)
            for k in range(4):
                landed(1 - core, k)

        @pl.when(s != core)
        def _():
            for k in range(4):
                deliver_copy(buf, out, core, which, k).wait_send()


    sends = []

    def slot(place_at, core):
        return pl.ds(pl.multiple_of((place_at * 2 + core) * SEQ, SEQ), SEQ)

    def ring(g, src):
        m = place[RING_AXIS[g]]
        here = ra.at[g, slot(m, s)]
        copies = [push(src, here, rgs_sem.at[g, 1], rgr_sem.at[g, 1], other)]
        for k in range(1, 4):
            copies.append(
                push(src, here, rgs_sem.at[g, 2 * k], rgr_sem.at[g, 2 * k], along(RING_AXIS[g], k, s))
            )
        return copies

    def ring_start(g, src):
        own = pltpu.make_async_copy(src, ra.at[g, slot(place[RING_AXIS[g]], s)], wk_sem.at[g])
        own.start()
        copies = ring(g, src)
        for copy in copies:
            copy.start()
        sends.extend(copies)
        ring_own[g] = own
        ring_got[g] = copies

    ring_own = [None] * 4
    ring_got = [None] * 4

    def ring_pass(g):
        m = place[RING_AXIS[g]]
        for k in range(1, 4):
            ring_got[g][k].wait_recv()
            part = ra.at[g, slot(pos(m, 4 - k), s)]
            copy = push(part, part, rgs_sem.at[g, 2 * k + 1], rgr_sem.at[g, 2 * k + 1], other)
            copy.start()
            sends.append(copy)
            ring_got[g].append(copy)

    def ring_load(g):
        ring_own[g].wait()
        ring_got[g][0].wait_recv()
        for copy in ring_got[g][4:]:
            copy.wait_recv()
        copy = pltpu.make_async_copy(ra.at[g], work, wk_sem.at[4 + g])
        copy.start()
        return copy


    acc = (a_gu1, a_dn1, a_gu2, a_dn2, a_qkv, a_ao, a_in, a_ro, a_misc)
    got = (r_gu1, r_dn1, r_gu2, r_dn2, r_qkv, r_ao, r_in, r_ro, r_misc)
    fin = (e_gu1, e_dn1, e_gu2, e_dn2, e_qkv, e_ao, e_in, e_ro, e_misc)
    full = {QKV: f_qkv, AO: f_ao, IN: f_in, RO: f_ro, MISC: f_misc}
    owner = {GU1: 0, DN1: 0, GU2: 1, DN2: 1}
    items = []
    for i in range(9):
        it = Item()
        it.i = i
        it.style, it.total, it.axis = PLAN[i]
        it.n8 = it.total // 8
        it.m = place[it.axis]
        it.n = place[1 - it.axis]
        it.acc, it.got, it.fin = acc[i], got[i], fin[i]
        if i in owner:
            base = f_gu if i in (GU1, GU2) else f_dn
            it.full = base.at[s if owner[i] == 0 else 1 - s]
            it.home = base.at[0]
        else:
            it.full = full[i]
            it.home = full[i]
        it.waits = []
        items.append(it)

    def mult(x, by):
        return pl.multiple_of(x * by, by)

    def spread(i, which, axis, source, target):
        m = place[axis]
        copies = []
        for k in range(4):
            for c in range(2):
                j = 2 * k + c
                core = s if c == 0 else 1 - s
                if j == 0:
                    continue
                copy = push(
                    source(pos(m, k), core), target(m, s, j),
                    xs_sem.at[i, which, j], xr_sem.at[i, which, j], along(axis, k, core),
                )
                copy.start()
                copies.append(copy)
        sends.extend(copies)
        return copies

    def lanes(place_at, core):
        return pl.ds(mult(place_at * 2 + core, SEQ), SEQ)

    def spread_rows(i, parts, into):
        it = items[i]
        into[:, lanes(it.m, s)] = parts[it.m * 2 + s]
        it.waits += spread(
            i, 0, it.axis, lambda f, c: parts.at[f * 2 + c], lambda f, c, j: into.at[:, lanes(f, c)]
        )

    def spread_left(i, parts, into):
        it = items[i]
        into[:, lanes(it.m, s)] = parts[s]
        it.waits += spread(
            i, 0, it.axis, lambda f, c: parts.at[c], lambda f, c, j: into.at[:, lanes(f, c)]
        )

    def spread_cols(i, src, into):
        it = items[i]

        def cut(f):
            return pl.ds(mult(f, CC), CC)

        into[slot(it.m, s), :] = src[:, cut(it.m)]
        it.waits += spread(
            i, 1, it.axis, lambda f, c: src.at[:, cut(f)], lambda f, c, j: into.at[slot(f, c), :]
        )

    def arrived(it):
        for copy in it.waits:
            copy.wait_recv()
        it.waits = []

    def settle(it):
        for copy in it.waits:
            copy.wait()
        it.waits = []

    def piece(it, q):
        if it.style == "r":
            return it.acc.at[:, pl.ds(mult(q, CC), CC)]
        return it.acc.at[pl.ds(mult(q, it.n8), it.n8), :]

    def sum_start(it):
        for k in range(1, 4):
            copy = push(
                piece(it, pos(it.n, k)), it.got.at[k - 1], ys_sem.at[it.i, k], yr_sem.at[it.i, k],
                along(1 - it.axis, k, s),
            )
            copy.start()
            it.waits.append(copy)

    def rect(it, ref, f, q):
        if it.style == "r":
            return ref.at[pl.ds(mult(f * 2 + s, it.n8), it.n8), pl.ds(mult(q, CC), CC)]
        return ref.at[pl.ds(mult(s * 4 + q, it.n8), it.n8), pl.ds(mult(f, CC), CC)]

    def quarter(it, ref, f, part=None):
        if it.style == "r":
            rows = pl.ds(mult(f * 2 + s, it.n8), it.n8)
            if part is None:
                return ref.at[rows, :]
            return ref.at[rows, part * HW : part * HW + HW]
        cols = pl.ds(mult(f, CC), CC)
        if part is None:
            return ref.at[pl.ds(mult(s, 4 * it.n8), 4 * it.n8), cols]
        return ref.at[pl.ds(mult(s * 2 + part, 2 * it.n8), 2 * it.n8), cols]

    def e2_rows(i, left, load):
        it = items[i]
        arrived(it)
        load.wait()
        for j in range(4):
            cols = slice(j * CC, j * CC + CC)
            it.acc[:, cols] = mm(left[...], work[:, cols]).astype(BF)
        sum_start(it)

    def e2_cols(i, left, right):
        it = items[i]
        arrived(it)
        it.acc[...] = mm(left[...], right[...]).astype(BF)
        sum_start(it)

    def e3(i):
        it = items[i]
        settle(it)
        total = piece(it, it.n)[...].astype(F32)
        for k in range(3):
            total = total + it.got[k].astype(F32)
        it.fin[...] = total.astype(BF)
        spot = rect(it, it.full, it.m, it.n)
        for k in range(1, 4):
            copy = push(
                it.fin, spot, gs_sem.at[i, k], gr_sem.at[i, k], along(1 - it.axis, k, s)
            )
            copy.start()
            it.waits.append(copy)
        own = pltpu.make_async_copy(it.fin, spot, loc_sem.at[i])
        own.start()
        it.waits.append(own)

    def both_ways(it, at, right, left):
        for side, part in ((1, right), (3, left)):
            copy = push(
                part, part, gs_sem.at[it.i, at + side // 2], gr_sem.at[it.i, at + side // 2],
                along(it.axis, side, s),
            )
            copy.start()
            it.waits.append(copy)

    def e4(i):
        it = items[i]
        settle(it)
        part = quarter(it, it.full, it.m)
        both_ways(it, 4, part, part)

    def e5(i):
        it = items[i]
        settle(it)
        both_ways(
            it, 6, quarter(it, it.full, pos(it.m, 3), 0), quarter(it, it.full, pos(it.m, 1), 1)
        )

    def to_other(it):
        if it.style == "c":
            rows = [pl.ds(mult(s, 4 * it.n8), 4 * it.n8)]
        else:
            rows = [pl.ds(mult(f * 2 + s, it.n8), it.n8) for f in range(4)]
        cols = pl.ds(0, D)
        if it.i in (QKV, AO, IN, RO):
            cols = pl.ds(mult(1 - s, HW), HW)
        return [
            push(
                it.full.at[r, cols], it.home.at[r, cols],
                gs_sem.at[it.i, 8 + j], gr_sem.at[it.i, 8 + j], other,
            )
            for j, r in enumerate(rows)
        ]

    def e6(i):
        it = items[i]
        settle(it)
        if i in owner:

            @pl.when(s != owner[i])
            def _():
                for copy in to_other(it):
                    copy.start()
        else:
            for copy in to_other(it):
                copy.start()

    def e7(i):
        it = items[i]
        if i in owner:

            @pl.when(s != owner[i])
            def _():
                for copy in to_other(it):
                    copy.wait_send()

            @pl.when(s == owner[i])
            def _():
                for copy in to_other(it):
                    copy.wait_recv()
        else:
            for copy in to_other(it):
                copy.wait()

    def gain(block, which):
        return s_sm[block, which : which + 1, :]

    rows = lax.broadcasted_iota(jnp.int32, (SEQ, RQ), 0)

    first = plan_ref[0, s] == 0
    x_s[...] = jnp.where(first, tok_ref[:SEQ, :], tok_ref[SEQ:, :])
    cot_at = pl.ds(mult(s, SEQ), SEQ)
    spread_cols(DN2, cot_ref.at[cot_at], rc2)
    weights(0, 1)
    n1 = rms(x_s[...].astype(F32), gain(0, 0)).astype(BF)
    n1_s[...] = n1
    ring_start(0, n1_s)
    uv_s[...] = mm(n1, s_in[...])
    taps = [s_sm[k // 2, 2 + k % 2 : 3 + k % 2, :RQ] for k in range(4)]
    vec = [s_sm[k // 2, 2 + k % 2 : 3 + k % 2, RQ : 2 * RQ] for k in range(4)]
    u = uv_s[:, :RQ]
    c = vec[0] + taps[0] * u
    for k in range(1, 4):
        c = c + taps[k] * rows_back(u, rows, k)
    c_s[...] = c
    weights(2, 3)
    for head in range(4):
        cols = slice(head * HD, head * HD + HD)
        cb = c_s[:, cols].astype(BF)
        ig_s[:, cols] = sigmoid(mm(cb, s_gt[:, cols]) + vec[1][:, cols])
        rg_s[:, cols] = sigmoid(
            mm(cb, s_gt[:, RQ + head * HD : RQ + head * HD + HD]) + vec[2][:, cols]
        )
    speed = softplus(vec[3])
    a = jnp.exp(-8.0 * rg_s[...] * speed)
    a_s[...] = a
    run = jnp.sqrt(jnp.maximum(1.0 - a * a, RATE_FLOOR)) * ig_s[...] * c_s[...]
    step = 1
    while step < SEQ:
        run = run + a * rows_back(run, rows, step)
        if 2 * step < SEQ:
            a = a * jnp.where(rows >= step, pltpu.roll(a, step, 0), 1.0)
        step *= 2
    h_s[...] = run
    o = (run * gelu(uv_s[:, RQ:])).astype(BF)
    for half in range(2):
        sb[0, :, half * HW : half * HW + HW] = mm(o, s_ro[half]).astype(BF)
    scatter_start(0)
    ot = o.T
    for half in range(2):
        o_t[half] = ot[half * 256 : half * 256 + 256]
    spread_left(RO, o_t, la_o)
    x_mine = x_s[mine, :].astype(F32)
    x1 = x_mine + scatter_wait(0)
    res[0] = x1
    gather_start(0, rms(x1, gain(0, 1)))

    def ffn_forward(block, p_in, p_out):
        n2 = ag[p_in]
        for j in range(3):
            cols = slice(j * CC, j * CC + CC)
            gate = mm(n2, s_g[block, :, cols])
            up = mm(n2, s_u[block, :, cols])
            gate_s[block, :, cols] = gate
            up_s[block, :, cols] = up
            hid_s[:, cols] = (gelu(gate) * up).astype(BF)
        if block == 0:
            weights(6)
        hid = hid_s[...]
        for j in range(4):
            cols = slice(j * CC, j * CC + CC)
            sb[p_out % 2, :, cols] = mm(hid, s_d[block, :, cols]).astype(BF)
        scatter_start(p_out)
        hidt = hid_s[...].T
        for half in range(2):
            hid_t[block, half] = hidt[half * 576 : half * 576 + 576]

    weights(4, 5)
    gather_wait(0)
    ring_start(1, ag.at[0])
    ffn_forward(0, 0, 1)
    spread_left(DN1, hid_t.at[0], la1)
    mid = (res[0] + scatter_wait(1)).astype(BF).astype(F32)
    res[1] = mid
    gather_start(1, rms(mid, gain(1, 0)))
    weights(7, 8, 9)
    ring_pass(0)

    gather_wait(1)
    ring_start(2, ag.at[1])
    na = ag[1]
    q_s[...] = mm(na, s_q[...]).astype(BF)
    kv_s[...] = mm(na, s_kv[...]).astype(BF)
    keys = kv_s[:, :HD]
    vals = kv_s[:, HD:]
    allowed = lax.broadcasted_iota(jnp.int32, (SEQ, SEQ), 1) <= lax.broadcasted_iota(
        jnp.int32, (SEQ, SEQ), 0
    )
    for head in range(3):
        cols = slice(head * HD, head * HD + HD)
        score = jnp.where(allowed, mm_nt(q_s[:, cols], keys) * HD ** (-0.5), -1e30)
        expo = jnp.exp(score - jnp.max(score, -1, keepdims=True))
        p = expo / jnp.sum(expo, -1, keepdims=True)
        p_s[head] = p
        at_s[:, cols] = mm(p.astype(BF), vals).astype(BF)
    att = at_s[...]
    for half in range(2):
        sb[0, :, half * HW : half * HW + HW] = mm(att, s_ao[half]).astype(BF)
    scatter_start(2)
    attt = att.T
    for half in range(2):
        att_t[half] = attt[half * 192 : half * 192 + 192]
    spread_left(AO, att_t, la_a)
    x1 = res[1] + scatter_wait(2)
    res[2] = x1
    gather_start(2, rms(x1, gain(1, 1)))
    ring_pass(1)
    gather_wait(2)
    ring_start(3, ag.at[2])
    ffn_forward(1, 2, 3)
    spread_left(DN2, hid_t.at[1], la2)
    ring_pass(2)
    y = res[2] + scatter_wait(3)
    deliver(y, yb, y_o, 1, 0)

    def ffn_backward(block, dF, p_out, item):
        for j in range(3):
            cols = slice(j * CC, j * CC + CC)
            dhid = mm_nt(dF, s_d[block, cols, :])
            value, slope = gelu_both(gate_s[block, :, cols])
            hid_s[:, cols] = (dhid * up_s[block, :, cols] * slope).astype(BF)
            du_s[:, cols] = (dhid * value).astype(BF)
        dg = hid_s[...]
        du = du_s[...]
        for j in range(4):
            cols = slice(j * CC, j * CC + CC)
            sb[p_out % 2, :, cols] = (
                mm_nt(dg, s_g[block, cols, :]) + mm_nt(du, s_u[block, cols, :])
            ).astype(BF)
        scatter_start(p_out)
        gu_t[block, :, :144] = dg.T.reshape(8, 144, SEQ)
        gu_t[block, :, 144:] = du.T.reshape(8, 144, SEQ)
        spread_rows(item, gu_t.at[block], l_gu1 if block == 0 else l_gu2)

    cot = cot_ref[cot_at, :]
    ffn_backward(1, cot, 4, GU2)
    e2_cols(DN2, la2, rc2)
    ring_pass(3)
    dn = scatter_wait(4)
    dv, gg11 = rms_back(res[2], gain(1, 1), dn)
    dx1 = cot_ref[pl.ds(pl.multiple_of(s * SEQ + t * SH, SH), SH), :].astype(F32) + dv
    res[3] = dx1
    gather_start(3, dx1)
    load = ring_load(3)
    e2_rows(GU2, l_gu2, load)
    load = ring_load(2)

    gather_wait(3)
    spread_cols(AO, ag.at[3], rc_a)
    dA = ag[3]
    datt_s = both_s.at[:, :AQ]
    dq_s = both_s.at[:, AQ : 2 * AQ]
    datt_s[...] = (mm_nt(dA[:, :HW], s_ao[0]) + mm_nt(dA[:, HW:], s_ao[1])).astype(BF)
    dk = jnp.zeros((SEQ, HD), F32)
    dw = jnp.zeros((SEQ, HD), F32)
    for head in range(3):
        cols = slice(head * HD, head * HD + HD)
        p = p_s[head]
        datt = datt_s[:, cols]
        dpr = mm_nt(datt, kv_s[:, HD:])
        dw = dw + mm(p.astype(BF).T, datt)
        ds = (p * (dpr - jnp.sum(p * dpr, -1, keepdims=True)) * HD ** (-0.5)).astype(BF)
        dq_s[:, cols] = mm(ds, kv_s[:, :HD]).astype(BF)
        dk = dk + mm(ds.T, q_s[:, cols])
    dkvb[0, :, :HD] = dk.astype(BF)
    dkvb[0, :, HD:] = dw.astype(BF)
    kv_copies = [
        push(dkvb.at[0], dkvb.at[k], kvs_sem.at[k], kvr_sem.at[k], (s, peers[k], d))
        for k in range(1, 4)
    ]
    for copy in kv_copies:
        copy.start()
    dq = dq_s[...]
    for j in range(4):
        cols = slice(j * CC, j * CC + CC)
        sb[1, :, cols] = mm_nt(dq, s_q[cols, :]).astype(BF)
    scatter_start(5)
    e3(DN2)
    for copy in kv_copies:
        copy.wait()
    total = dkvb[0].astype(F32)
    for k in range(1, 4):
        total = total + dkvb[k].astype(F32)
    dkv_s = both_s.at[:, 2 * AQ : 2 * AQ + 256]
    dkv_s[...] = total.astype(BF)
    qkv_t[:, :48] = dq_s[...].T.reshape(8, 48, SEQ)
    qkv_t[:, 48:] = dkv_s[...].T.reshape(8, 32, SEQ)
    spread_rows(QKV, qkv_t, l_qkv)
    dn = scatter_wait(5) + mm_nt(dkv_s[mine, :], s_kv[...])
    dv, gg10 = rms_back(res[1], gain(1, 0), dn)
    dmid = res[3] + dv
    big_g = dmid.astype(BF).astype(F32)
    gather_start(4, big_g)
    res[3] = big_g
    e3(GU2)
    e2_cols(AO, la_a, rc_a)
    e4(DN2)
    gather_wait(4)
    spread_cols(DN1, ag.at[4], rc1)
    ffn_backward(0, ag[4], 6, GU1)
    e2_rows(QKV, l_qkv, load)
    load = ring_load(1)
    e4(GU2)
    dn = scatter_wait(6)
    dv, gg01 = rms_back(res[0], gain(0, 1), dn)
    dx1 = res[3] + dv
    res[3] = dx1
    gather_start(5, dx1)
    e5(DN2)
    e3(AO)
    e2_cols(DN1, la1, rc1)

    gather_wait(5)
    spread_cols(RO, ag.at[5], rc_o)
    dA = ag[5]
    dO = mm_nt(dA[:, :HW], s_ro[0]) + mm_nt(dA[:, HW:], s_ro[1])
    value, slope = gelu_both(uv_s[:, RQ:])
    h = h_s[...]
    both_s[:, RQ:] = (dO * h * slope).astype(BF)
    e = dO * value
    a = a_s[...]
    coef = rows_ahead(a, rows, 1)
    step = 1
    while step < SEQ:
        e = e + coef * rows_ahead(e, rows, step)
        if 2 * step < SEQ:
            coef = coef * rows_ahead(coef, rows, step)
        step *= 2
    ig = ig_s[...]
    rg = rg_s[...]
    c = c_s[...]
    room = 1.0 - a * a
    m = jnp.sqrt(jnp.maximum(room, RATE_FLOOR))
    ga = e * rows_back(h, rows, 1) - jnp.where(room > RATE_FLOOR, e * ig * c * a / m, 0.0)
    dl = ga * a
    gv3 = jnp.sum(dl * rg, 0, keepdims=True) * (-8.0) * sigmoid(vec[3])
    er = -8.0 * dl * speed * rg * (1.0 - rg)
    ei = e * m * c * ig * (1.0 - ig)
    gv1 = jnp.sum(ei, 0, keepdims=True)
    gv2 = jnp.sum(er, 0, keepdims=True)
    c_s[...] = e * m * ig
    ig_s[...] = ei
    rg_s[...] = er
    for head in range(4):
        cols = slice(head * HD, head * HD + HD)
        late = slice(RQ + head * HD, RQ + head * HD + HD)
        dpin = ig_s[:, cols].astype(BF)
        dprec = rg_s[:, cols].astype(BF)
        cbt = c[:, cols].astype(BF).T
        misc_t[:, cols] = mm(cbt, dpin).astype(BF)
        misc_t[:, late] = mm(cbt, dprec).astype(BF)
        c_s[:, cols] += mm_nt(dpin, s_gt[:, cols]) + mm_nt(dprec, s_gt[:, late])
    dc = c_s[...]
    u = uv_s[:, :RQ]
    du = taps[0] * dc
    gtap = [jnp.sum(u * dc, 0, keepdims=True)]
    for k in range(1, 4):
        du = du + taps[k] * rows_ahead(dc, rows, k)
        gtap.append(jnp.sum(rows_back(u, rows, k) * dc, 0, keepdims=True))
    gv0 = jnp.sum(dc, 0, keepdims=True)
    both_s[:, :RQ] = du.astype(BF)
    both = both_s[...]
    for j in range(4):
        cols = slice(j * CC, j * CC + CC)
        sb[1, :, cols] = mm_nt(both, s_in[cols, :]).astype(BF)
    scatter_start(7)
    in_t[...] = both.T.reshape(8, SEQ, SEQ)
    spread_rows(IN, in_t, l_in)
    e2_rows(GU1, l_gu1, load)
    load = ring_load(0)
    dn = scatter_wait(7)
    dv, gg00 = rms_back(x_mine, gain(0, 0), dn)
    deliver(res[3] + dv, xb, dx_o, 0, 1)
    gnb[0, 0:1] = gg00
    gnb[0, 1:2] = gg01
    gnb[0, 2:3] = gg10
    gnb[0, 3:4] = gg11
    gnb[0, 4:8] = jnp.zeros((4, D), F32)
    gn_copies = [
        push(gnb.at[0], gnb.at[k], gns_sem.at[k], gnr_sem.at[k], (s, peers[k], d))
        for k in range(1, 4)
    ]
    for copy in gn_copies:
        copy.start()
    e3(QKV)
    e5(GU2)
    e4(AO)
    e2_cols(RO, la_o, rc_o)
    e2_rows(IN, l_in, load)
    for copy in gn_copies:
        copy.wait()
    gains = gnb[0] + gnb[1] + gnb[2] + gnb[3]
    small = gtap + [gv0, gv1, gv2, gv3]
    for g in range(4):
        for part in range(3):
            small.append(gains[g : g + 1, part * RQ : part * RQ + RQ])
    small.append(jnp.zeros((HD - len(small), RQ), F32))
    misc_t[:, 2 * RQ :] = jnp.concatenate(small, 0).astype(BF)
    it = items[MISC]
    l_misc[0] = misc_t[pl.ds(mult(it.m * 2 + s, 16), 16), :]
    it.waits += spread(
        MISC, 0, it.axis, lambda f, c: misc_t.at[pl.ds(mult(f * 2 + c, 16), 16), :],
        lambda f, c, j: l_misc.at[j],
    )
    e3(DN1)
    e6(DN2)
    e3(GU1)
    e4(QKV)
    arrived(it)
    total = l_misc[0].astype(F32)
    for j in range(1, 8):
        total = total + l_misc[j].astype(F32)
    it.acc[...] = total.astype(BF)
    sum_start(it)
    e5(AO)
    e3(RO)
    e3(IN)
    e4(DN1)
    e4(GU1)
    e6(GU2)
    e5(QKV)
    e3(MISC)
    e6(AO)
    e4(RO)
    e4(IN)
    e5(DN1)
    e5(GU1)
    e4(MISC)
    e6(QKV)
    e5(RO)
    e5(IN)
    e5(MISC)
    e6(DN1)
    e6(GU1)
    e6(RO)
    e6(IN)
    e6(MISC)
    deliver_wait(yb, y_o, 1, 0)
    deliver_wait(xb, dx_o, 0, 1)
    for copy in swap:
        copy.wait_send()
    for copy in sends:
        copy.wait_send()
    for i in (DN2, GU2, AO, QKV, DN1, GU1, RO, IN, MISC):
        e7(i)


def whole_call(tokens, plan, cot, gains, conv, vec, weights):
    vm = pl.BlockSpec(memory_space=pltpu.VMEM)
    hbm = pl.BlockSpec(memory_space=pl.ANY)
    V = pltpu.VMEM
    dma = pltpu.SemaphoreType.DMA
    accs, gots, fins = [], [], []
    for i in range(9):
        style, total, _ = PLAN[i]
        n8 = total // 8
        accs.append(V((n8, D) if style == "r" else (4 * n8, CC), BF))
        gots.append(V((3, n8, CC), BF))
        fins.append(V((n8, CC), BF))
    shapes = [
        (2, SEQ, D), (2, SEQ, D), (4, 8 * SEQ, D),
        (2, 2 * FQ, D), (2, FQ, D), (640, D), (AQ, D), (1024, D), (RQ, D), (HD, D),
    ]
    return pl.pallas_call(
        whole_kernel,
        name="whole",
        out_shape=[jax.ShapeDtypeStruct(shape, BF) for shape in shapes],
        in_specs=[vm, pl.BlockSpec(memory_space=pltpu.SMEM), vm, vm, vm, vm] + [hbm] * 9,
        out_specs=[hbm] * 10,
        scratch_shapes=[
            V((D, 2 * RQ), BF), V((HD, 2 * RQ), BF), V((2, RQ, HW), BF), V((2, 8, D), F32),
            V((2, D, FQ), BF), V((2, D, FQ), BF), V((2, FQ, D), BF),
            V((D, AQ), BF), V((D, 256), BF), V((2, AQ, HW), BF),
            V((6, SEQ, D), BF), V((2, SEQ, D), BF), V((2, 3, SH, D), BF), V((4, SH, D), F32),
            V((SEQ, D), BF), V((SEQ, D), BF), V((SEQ, 2 * RQ), F32),
            V((SEQ, RQ), F32), V((SEQ, RQ), F32), V((SEQ, RQ), F32), V((SEQ, RQ), F32), V((SEQ, RQ), F32),
            V((SEQ, AQ), BF), V((SEQ, 256), BF), V((3, SEQ, SEQ), F32), V((SEQ, AQ), BF),
            V((2, SEQ, FQ), F32), V((2, SEQ, FQ), F32), V((SEQ, FQ), BF),
            V((SEQ, FQ), BF), V((SEQ, 2 * RQ), BF),
            V((4, SEQ, 256), BF), V((4, 8, D), F32), V((SH, D), BF), V((SH, D), BF), V((8, D), F32),
            V((8 * SEQ, D), BF), V((2, 2, 576, SEQ), BF), V((2, 256, SEQ), BF), V((2, 192, SEQ), BF),
            V((2, 8, 288, SEQ), BF), V((8, 80, SEQ), BF), V((8, SEQ, SEQ), BF), V((HD, D), BF),
            V((576, 1024), BF), V((576, 1024), BF), V((256, 1024), BF), V((192, 1024), BF),
            V((1024, CC), BF), V((1024, CC), BF), V((1024, CC), BF), V((1024, CC), BF),
            V((288, 1024), BF), V((288, 1024), BF), V((80, 1024), BF), V((SEQ, 1024), BF), V((8, 16, D), BF),
            *accs, *gots, *fins,
            dma((10,)), dma((10,)), dma((10,)), dma((6, 4)), dma((6, 4)), dma((8, 4)), dma((8, 4)),
            dma((4,)), dma((4,)), dma((4,)), dma((4,)), dma((2,)), dma((2, 4)), dma((2, 2, 4)),
            dma((4, 8)), dma((4, 8)), dma((8,)), dma((9, 2, 8)), dma((9, 2, 8)),
            dma((9, 4)), dma((9, 4)), dma((9, 12)), dma((9, 12)), dma((9,)),
        ],
        compiler_params=pltpu.CompilerParams(
            collective_id=0, has_side_effects=True, vmem_limit_bytes=63 * 2**20
        ),
    )(tokens, plan, cot, gains, conv, vec, *weights)


def unpack_kernel(s_ref, gu, dn, qkv, ao, rin, ro, g_gate, g_up, g_dn, g_q, g_kv, g_ao, g_in, g_ro):
    i = pl.program_id(0)
    for b in range(8):
        cols = slice(b * 144, b * 144 + 144)
        part = gu[0, b * 288 : b * 288 + 288, :].T.astype(F32)
        g_gate[0, :, cols] = part[:, :144]
        g_up[0, :, cols] = part[:, 144:]
    g_dn[0] = dn[0].astype(F32)
    for b in range(8):
        part = qkv[b * 80 : b * 80 + 80, :].T.astype(F32)
        g_q[:, b * 48 : b * 48 + 48] = part[:, :48]
        g_kv[:, b * 32 : b * 32 + 32] = part[:, 48:]
    g_in[...] = rin[...].T.astype(F32)

    @pl.when(i == 0)
    def _():
        g_ao[...] = ao[...].astype(F32)
        g_ro[...] = ro[...].astype(F32)


def unpack_call(s, gu, dn, qkv, ao, rin, ro):
    n = 6
    wide = D // n
    part = HW // n
    sds = jax.ShapeDtypeStruct
    return pl.pallas_call(
        unpack_kernel,
        name="unpack",
        out_shape=[
            sds((1, D, FQ), F32), sds((1, D, FQ), F32), sds((1, FQ, D), F32),
            sds((HW, AQ), F32), sds((HW, 256), F32), sds((AQ, HW), F32),
            sds((HW, 1024), F32), sds((RQ, HW), F32),
        ],
        grid_spec=pltpu.PrefetchScalarGridSpec(
            num_scalar_prefetch=1,
            grid=(n,),
            in_specs=[
                pl.BlockSpec((1, 2 * FQ, wide), lambda i, s: (0, 0, i)),
                pl.BlockSpec((1, FQ // n, D), lambda i, s: (0, i, 0)),
                pl.BlockSpec((640, part), lambda i, s: (0, s[0] * n + i)),
                pl.BlockSpec((AQ, HW), lambda i, s: (0, s[0])),
                pl.BlockSpec((1024, part), lambda i, s: (0, s[0] * n + i)),
                pl.BlockSpec((RQ, HW), lambda i, s: (0, s[0])),
            ],
            out_specs=[
                pl.BlockSpec((1, wide, FQ), lambda i, s: (0, i, 0)),
                pl.BlockSpec((1, wide, FQ), lambda i, s: (0, i, 0)),
                pl.BlockSpec((1, FQ // n, D), lambda i, s: (0, i, 0)),
                pl.BlockSpec((part, AQ), lambda i, s: (i, 0)),
                pl.BlockSpec((part, 256), lambda i, s: (i, 0)),
                pl.BlockSpec((AQ, HW), lambda i, s: (0, 0)),
                pl.BlockSpec((part, 1024), lambda i, s: (i, 0)),
                pl.BlockSpec((RQ, HW), lambda i, s: (0, 0)),
            ],
        ),
        compiler_params=pltpu.CompilerParams(vmem_limit_bytes=40 * 2**20),
    )(s, gu, dn, qkv, ao, rin, ro)


def per_device(
    tokens, plan_order, cotangent, norm_gains, ffn_gate, ffn_up, ffn_down,
    rec_in, rec_gates, rec_conv, rec_vec, rec_out, att_q, att_kv, att_out,
):
    s = lax.axis_index("section")
    plan = plan_order[0]
    y, dx, _, gu, dn, qkv, ao, rin, ro, misc = whole_call(
        tokens, plan_order, cotangent, norm_gains, rec_conv, rec_vec,
        (
            rec_in.reshape(HW, 2 * RQ), rec_gates.reshape(64, 2 * RQ), rec_out,
            ffn_gate, ffn_up, ffn_down, att_q, att_kv, att_out,
        ),
    )
    in_order = jnp.where(plan[0] == 0, dx, dx[::-1])
    boundary = jnp.where(s == 0, in_order, y).astype(F32).reshape(1, 2 * SEQ, D)
    g_gate, g_up, g_dn, g_q, g_kv, g_ao, g_in, g_ro = unpack_call(
        s.astype(jnp.int32).reshape(1), gu, dn, qkv, ao, rin, ro
    )
    misc = misc.astype(F32)
    g_gt = lax.dynamic_slice_in_dim(misc[:, : 2 * RQ], s * 64, 64, 0).reshape(64, 2, RQ)
    small = misc[:, 2 * RQ :]
    g_conv = lax.dynamic_slice_in_dim(small, s * 2, 2, 0)
    g_vec = lax.dynamic_slice_in_dim(small, 4 + s * 2, 2, 0)
    g_gain = lax.dynamic_slice_in_dim(small, 8 + s * 6, 6, 0).reshape(1, 2, D)
    return (
        boundary, g_gain, g_gate, g_up, g_dn, g_in.reshape(HW, 2, RQ), g_gt,
        g_conv, g_vec, g_ro, g_q, g_kv, g_ao,
    )


def solution(mesh):
    placed = (
        P("dp", None),
        P("dp", None),
        P("dp", None),
        P("section", None, None),
        P("section", None, "tensor"),
        P("section", None, "tensor"),
        P("section", "tensor", None),
        P("section", None, "tensor"),
        P("section", None, "tensor"),
        P("section", "tensor"),
        P("section", "tensor"),
        P("tensor", "section"),
        P("section", "tensor"),
        P("section", None),
        P("tensor", "section"),
    )
    return jax.shard_map(
        per_device,
        mesh=mesh,
        in_specs=placed,
        out_specs=(
            P("section", "dp", None),
            P("section", None, None),
            P("section", None, "tensor"),
            P("section", None, "tensor"),
            P("section", "tensor", None),
            P("section", None, "tensor"),
            P("section", None, "tensor"),
            P("section", "tensor"),
            P("section", "tensor"),
            P("tensor", "section"),
            P("section", "tensor"),
            P("section", None),
            P("tensor", "section"),
        ),
        check_vma=False,
    )
```

```python
import jax
import jax.numpy as jnp
from jax import lax
from jax.experimental import pallas as pl
from jax.experimental.pallas import tpu as pltpu
from jax.sharding import PartitionSpec as P

HD = 128
SEQ = 128
NORM_EPS = 1e-06
RATE_FLOOR = 0.01
BF = jnp.bfloat16
F32 = jnp.float32
MESH = pl.DeviceIdType.MESH
NT = (((1,), (1,)), ((), ()))

D = 1536
FQ = 1152
RQ = 512
AQ = 384
SH = 32
CC = 384
HW = 768
X_AXIS = 0
Y_AXIS = 1
G1, U1, D1, G2, U2, D2, QKV, AO, IN, RO, MISC = range(11)
PLAN = {
    G1: ("r", FQ, Y_AXIS),
    U1: ("r", FQ, Y_AXIS),
    D1: ("c", FQ, X_AXIS),
    G2: ("r", FQ, X_AXIS),
    U2: ("r", FQ, X_AXIS),
    D2: ("r", FQ, Y_AXIS),
    QKV: ("r", 640, Y_AXIS),
    AO: ("c", AQ, Y_AXIS),
    IN: ("r", 1024, X_AXIS),
    RO: ("c", RQ, X_AXIS),
    MISC: ("r", HD, Y_AXIS),
}
RING_AXIS = (X_AXIS, Y_AXIS, Y_AXIS, X_AXIS, Y_AXIS)
RN1, RN2, RNA, RN2B, RCOT = range(5)
ROOM = {G2: 0, U2: 144, G1: 288, U1: 432, D1: 576, QKV: 720, IN: 800, AO: 928, RO: 976, MISC: 1040}


def mm(left, right):
    return jnp.dot(left, right, preferred_element_type=F32)


def mm_nt(left, right):
    return lax.dot_general(left, right, NT, preferred_element_type=F32)


def rms(values, gain):
    return values * lax.rsqrt(jnp.mean(values * values, -1, keepdims=True) + NORM_EPS) * gain


def rms_back(values, gain, dn):
    r = lax.rsqrt(jnp.mean(values * values, -1, keepdims=True) + NORM_EPS)
    dng = dn * gain
    dv = r * (dng - values * (r * r) * jnp.mean(dng * values, -1, keepdims=True))
    return dv, jnp.sum(dn * values * r, 0, keepdims=True)


GC = 0.7978845608028654
GA = 0.044715


def gelu(x):
    return 0.5 * x * (1.0 + jnp.tanh(GC * (x + GA * x * x * x)))


def gelu_both(x):
    th = jnp.tanh(GC * (x + GA * x * x * x))
    value = 0.5 * x * (1.0 + th)
    slope = 0.5 * (1.0 + th) + 0.5 * x * (1.0 - th * th) * GC * (1.0 + 3.0 * GA * x * x)
    return value, slope


def sigmoid(x):
    return 1.0 / (1.0 + jnp.exp(-x))


def softplus(x):
    return jnp.maximum(x, 0.0) + jnp.log(1.0 + jnp.exp(-jnp.abs(x)))


def rows_back(values, rows, k):
    return jnp.where(rows >= k, pltpu.roll(values, k, 0), 0.0)


def rows_ahead(values, rows, k):
    return jnp.where(rows < SEQ - k, pltpu.roll(values, SEQ - k, 0), 0.0)


class Item:
    pass


def whole_kernel(
    tok_ref, plan_ref, cot_ref, gain_ref, conv_ref, vec_ref,
    win, wgt, wro, wg, wu, wd, wq, wkv, wao,
    y_o, dx_o, ra, f_ffn, f_qkv, f_ao, f_in, f_ro, f_misc,
    s_in, s_gt, s_ro, s_sm, s_g, s_u, s_d, s_q, s_kv, s_ao,
    ag, sb, rb, res, x_s, n1_s, uv_s, c_s, ig_s, rg_s, a_s, h_s,
    q_s, kv_s, p_s, at_s, gate_s, up_s, hid_s, du_s, both_s,
    dkvb, gnb, yb, xb, smb,
    work, hid_t, o_t, att_t, g_t, u_t, qkv_t, in_t, misc_t,
    la1, la_o, la_a, rc1, rc_o, rc_a, l_g1, l_u1, l_g2, l_u2, l_d2, l_qkv, l_in, l_misc,
    a_d2, cs, *rest,
):
    crs, gots, fins = rest[:11], rest[11:22], rest[22:33]
    (
        wl_sem, ws_sem, wr_sem, ags_sem, agr_sem, rss_sem, rsr_sem,
        kvs_sem, kvr_sem, gns_sem, gnr_sem, dl_sem, dls_sem, dlr_sem,
        rgs_sem, rgr_sem, wk_sem, xs_sem, xr_sem, ys_sem, yr_sem, gs_sem, gr_sem, loc_sem,
        cs_sem, cr_sem,
    ) = rest[33:]
    s = lax.axis_index("section")
    t = lax.axis_index("tensor")
    d = lax.axis_index("dp")
    place = (lax.rem(d, 4), d // 4)
    peers = [lax.rem(t + k, 4) for k in range(4)]
    mine = [pl.ds(pl.multiple_of(t * SH + h * 16, 16), 16) for h in range(2)]

    def pos(base, k):
        return lax.rem(base + k, 4)

    def along(axis, k, core):
        if axis == X_AXIS:
            return (core, t, place[1] * 4 + pos(place[0], k))
        return (core, t, pos(place[1], k) * 4 + place[0])

    barrier = pltpu.get_barrier_semaphore()
    other = (1 - s, t, d)
    for k in range(1, 4):
        for target in (
            (s, peers[k], d), (1 - s, peers[k], d), along(X_AXIS, k, s), along(Y_AXIS, k, s),
        ):
            pl.semaphore_signal(barrier, inc=1, device_id=target, device_id_type=MESH)
    pl.semaphore_signal(barrier, inc=1, device_id=other, device_id_type=MESH)

    def push(src, dst, send_sem, recv_sem, target):
        return pltpu.make_async_remote_copy(
            src_ref=src, dst_ref=dst, send_sem=send_sem, recv_sem=recv_sem,
            device_id=target, device_id_type=MESH,
        )

    smb[...] = jnp.zeros((8, D), F32)
    smb[0:2, :] = gain_ref[0]
    smb[2:4, :RQ] = conv_ref[...].astype(F32)
    smb[2:4, RQ : 2 * RQ] = vec_ref[...].astype(F32)
    half_in = pl.ds(pl.multiple_of(s * HW, HW), HW)
    half_gt = pl.ds(pl.multiple_of(s * 64, 64), 64)
    moves = [
        (win, s_in.at[half_in, :]),
        (smb, s_sm.at[s]),
        (wgt, s_gt.at[half_gt, :]),
        (wro, s_ro.at[s]),
        (wg.at[0], s_g.at[s]),
        (wu.at[0], s_u.at[s]),
        (wd.at[0], s_d.at[s]),
        (wq, s_q.at[half_in, :]),
        (wkv, s_kv.at[half_in, :]),
        (wao, s_ao.at[s]),
    ]
    local = [pltpu.make_async_copy(a, b, wl_sem.at[i]) for i, (a, b) in enumerate(moves)]
    swap = [push(a, b, ws_sem.at[i], wr_sem.at[i], other) for i, (a, b) in enumerate(moves)]
    for copy in local:
        copy.start()
    pl.semaphore_wait(barrier, 13)
    for copy in swap:
        copy.start()

    def weights(*which):
        for i in which:
            local[i].wait()
            swap[i].wait_recv()


    def gather(p, h):
        return [
            push(
                ag.at[p, mine[h]], ag.at[p, mine[h]], ags_sem.at[p, h, k], agr_sem.at[p, h, k],
                (s, peers[k], d),
            )
            for k in (2, 1, 3)
        ]

    def gather_start(p, h, shard):
        ag[p, mine[h], :] = shard.astype(BF)
        for copy in gather(p, h):
            copy.start()

    def gather_wait(p):
        for h in range(2):
            for copy in gather(p, h):
                copy.wait()

    def scatter(p, h):
        return [
            push(
                sb.at[p % 2, pl.ds(pl.multiple_of(peers[k] * SH + h * 16, 16), 16)],
                rb.at[p % 2, k - 1, h * 16 : h * 16 + 16],
                rss_sem.at[p, h, k], rsr_sem.at[p, h, k], (s, peers[k], d),
            )
            for k in (2, 1, 3)
        ]

    def scatter_start(p):
        for h in range(2):
            for copy in scatter(p, h):
                copy.start()

    def scatter_wait(p, h):
        for copy in scatter(p, h):
            copy.wait()
        total = sb[p % 2, mine[h], :].astype(F32)
        for k in range(3):
            total = total + rb[p % 2, k, h * 16 : h * 16 + 16].astype(F32)
        return total

    whole = pl.ds(pl.multiple_of(t * SH, SH), SH)

    def deliver(buf, out, core, which):
        @pl.when(s == core)
        def _():
            own = pltpu.make_async_copy(buf, out.at[s, whole], dl_sem.at[which])
            own.start()
            for k in range(1, 4):
                deliver_copy(buf, out, core, which, k).start()
            own.wait()

        @pl.when(s != core)
        def _():
            for k in range(4):
                deliver_copy(buf, out, core, which, k).start()

    def deliver_copy(buf, out, core, which, k):
        return push(
            buf, out.at[s, whole], dls_sem.at[which, k], dlr_sem.at[which, s, k],
            (core, peers[k], d),
        )

    def deliver_wait(buf, out, core, which):
        def landed(sender, k):
            push(
                buf, out.at[sender, whole], dls_sem.at[which, k], dlr_sem.at[which, sender, k],
                (core, peers[k], d),
            ).wait_recv()

        @pl.when(s == core)
        def _():
            for k in range(1, 4):
                deliver_copy(buf, out, core, which, k).wait_send()
                landed(core, k)
            for k in range(4):
                landed(1 - core, k)

        @pl.when(s != core)
        def _():
            for k in range(4):
                deliver_copy(buf, out, core, which, k).wait_send()


    sends = []

    def mult(x, by):
        return pl.multiple_of(x * by, by)

    def slot(place_at):
        return pl.ds(mult(place_at, SEQ), SEQ)

    ring_got = [None] * 5

    def ring_start(g, src):
        axis = RING_AXIS[g]
        here = ra.at[g, slot(place[axis])]
        own = pltpu.make_async_copy(src, here, wk_sem.at[g])
        own.start()
        copies = [
            push(src, here, rgs_sem.at[g, k], rgr_sem.at[g, k], along(axis, k, s)) for k in range(1, 4)
        ]
        for copy in copies:
            copy.start()
        sends.extend(copies)
        ring_got[g] = [own, copies]

    in_work = [None, None]

    def ring_load(g):
        if in_work[0] == g:
            return
        ring_got[g][0].wait()
        for copy in ring_got[g][1]:
            copy.wait_recv()
        copy = pltpu.make_async_copy(ra.at[g], work, wk_sem.at[5 + g])
        copy.start()
        in_work[0] = g
        in_work[1] = copy

    def ring_use(g):
        ring_load(g)
        if in_work[1] is not None:
            in_work[1].wait()
            in_work[1] = None


    full = {QKV: f_qkv, AO: f_ao, IN: f_in, RO: f_ro, MISC: f_misc}
    owner = {G1: 0, U1: 0, D1: 0, G2: 1, U2: 1, D2: 1}
    items = []
    for i in range(11):
        it = Item()
        it.i = i
        it.style, it.total, it.axis = PLAN[i]
        it.n8 = it.total // 8
        it.m = place[it.axis]
        it.n = place[1 - it.axis]
        it.cr, it.got, it.fin = crs[i], gots[i], fins[i]
        it.acc = a_d2 if i == D2 else s_d.at[1, ROOM[i] : ROOM[i] + it.n8]
        if i in owner:
            it.full = f_ffn.at[(s if owner[i] == 0 else 1 - s) * 3 + i % 3]
            it.home = f_ffn.at[i % 3]
        else:
            it.full = full[i]
            it.home = full[i]
        it.waits = []
        items.append(it)

    def spread(i, which, source, target):
        it = items[i]
        for k in range(1, 4):
            copy = push(
                source(pos(it.m, k)), target(k), xs_sem.at[i, which, k], xr_sem.at[i, which, k],
                along(it.axis, k, s),
            )
            copy.start()
            sends.append(copy)
            it.waits.append(copy)

    def spread_rows(i, whole, into):
        it = items[i]

        def part(f):
            return whole.at[pl.ds(mult(f, 2 * it.n8), 2 * it.n8), :]

        into[:, slot(it.m)] = part(it.m)[...]
        spread(i, 0, part, lambda k: into.at[:, slot(it.m)])

    def spread_left(i, whole, into):
        it = items[i]
        into[:, slot(it.m)] = whole[...]
        spread(i, 0, lambda f: whole, lambda k: into.at[:, slot(it.m)])

    def spread_cols(i, src, into):
        it = items[i]

        def cut(f):
            return pl.ds(mult(f, CC), CC)

        into[slot(it.m), :] = src[:, cut(it.m)]
        spread(i, 1, lambda f: src.at[:, cut(f)], lambda k: into.at[slot(it.m), :])

    def arrived(it):
        for copy in it.waits:
            copy.wait_recv()
        it.waits = []

    def settle(it):
        for copy in it.waits:
            copy.wait()
        it.waits = []

    def piece(it, q):
        return it.acc.at[:, pl.ds(mult(q, CC), CC)]

    cs_busy = [None, None]
    cs_count = [0]

    def halves(i, fill):
        it = items[i]
        at = cs_count[0] % 2
        cs_count[0] += 1
        if cs_busy[at] is not None:
            cs_busy[at].wait_send()
        out = cs.at[at, : it.n8]
        fill(1 - s, out)
        copy = push(out, it.cr, cs_sem.at[i], cr_sem.at[i], other)
        copy.start()
        cs_busy[at] = copy
        it.swap = copy
        fill(s, it.acc)

    def rows_product(i, ring, left):
        it = items[i]
        arrived(it)
        ring_use(ring)

        def fill(h, ref):
            rows = left[pl.ds(mult(h, it.n8), it.n8), :]
            for j in range(4):
                cols = slice(j * CC, j * CC + CC)
                ref[:, cols] = mm(rows, work[:, cols]).astype(BF)

        halves(i, fill)

    def cols_product(i, left, right):
        it = items[i]
        arrived(it)

        def fill(h, ref):
            for q in range(4):
                rows = left[pl.ds(mult(h * 4 + q, it.n8), it.n8), :]
                ref[:, q * CC : q * CC + CC] = mm(rows, right[...]).astype(BF)

        halves(i, fill)

    def misc_sum():
        it = items[MISC]
        arrived(it)

        def fill(h, ref):
            at = pl.ds(mult(h, it.n8), it.n8)
            total = l_misc[0, at, :].astype(F32)
            for k in range(1, 4):
                total = total + l_misc[k, at, :].astype(F32)
            ref[...] = total.astype(BF)

        halves(MISC, fill)

    row_items = {
        G1: (RN2, l_g1), U1: (RN2, l_u1), G2: (RN2B, l_g2), U2: (RN2B, l_u2),
        D2: (RCOT, l_d2), QKV: (RNA, l_qkv), IN: (RN1, l_in),
    }
    col_items = {D1: (la1, rc1), AO: (la_a, rc_a), RO: (la_o, rc_o)}

    def e1(i):
        if i in row_items:
            rows_product(i, *row_items[i])
        elif i in col_items:
            cols_product(i, *col_items[i])
        else:
            misc_sum()

    def e2(i):
        it = items[i]
        it.swap.wait_recv()
        it.acc[...] = (it.acc[...].astype(F32) + it.cr[...].astype(F32)).astype(BF)
        for k in range(1, 4):
            copy = push(
                piece(it, pos(it.n, k)), it.got.at[k - 1], ys_sem.at[it.i, k], yr_sem.at[it.i, k],
                along(1 - it.axis, k, s),
            )
            copy.start()
            it.waits.append(copy)

    def rect(it, ref, f, q):
        if it.style == "r":
            return ref.at[pl.ds(mult(f * 2 + s, it.n8), it.n8), pl.ds(mult(q, CC), CC)]
        return ref.at[pl.ds(mult(s * 4 + q, it.n8), it.n8), pl.ds(mult(f, CC), CC)]

    def quarter(it, ref, f, part=None):
        if it.style == "r":
            rows = pl.ds(mult(f * 2 + s, it.n8), it.n8)
            if part is None:
                return ref.at[rows, :]
            return ref.at[rows, part * HW : part * HW + HW]
        cols = pl.ds(mult(f, CC), CC)
        if part is None:
            return ref.at[pl.ds(mult(s, 4 * it.n8), 4 * it.n8), cols]
        return ref.at[pl.ds(mult(s * 2 + part, 2 * it.n8), 2 * it.n8), cols]

    def e3(i):
        it = items[i]
        settle(it)
        total = piece(it, it.n)[...].astype(F32)
        for k in range(3):
            total = total + it.got[k].astype(F32)
        it.fin[...] = total.astype(BF)
        spot = rect(it, it.full, it.m, it.n)
        for k in range(1, 4):
            copy = push(
                it.fin, spot, gs_sem.at[i, k], gr_sem.at[i, k], along(1 - it.axis, k, s)
            )
            copy.start()
            it.waits.append(copy)
        own = pltpu.make_async_copy(it.fin, spot, loc_sem.at[i])
        own.start()
        it.waits.append(own)

    def both_ways(it, at, right, left):
        for side, part in ((1, right), (3, left)):
            copy = push(
                part, part, gs_sem.at[it.i, at + side // 2], gr_sem.at[it.i, at + side // 2],
                along(it.axis, side, s),
            )
            copy.start()
            it.waits.append(copy)

    def e4(i):
        it = items[i]
        settle(it)
        part = quarter(it, it.full, it.m)
        both_ways(it, 4, part, part)

    def e5(i):
        it = items[i]
        settle(it)
        both_ways(
            it, 6, quarter(it, it.full, pos(it.m, 3), 0), quarter(it, it.full, pos(it.m, 1), 1)
        )

    def to_other(it):
        if it.style == "c":
            rows = [pl.ds(mult(s, 4 * it.n8), 4 * it.n8)]
        else:
            rows = [pl.ds(mult(f * 2 + s, it.n8), it.n8) for f in range(4)]
        cols = pl.ds(0, D)
        if it.i in (QKV, AO, IN, RO):
            cols = pl.ds(mult(1 - s, HW), HW)
        return [
            push(
                it.full.at[r, cols], it.home.at[r, cols],
                gs_sem.at[it.i, 8 + j], gr_sem.at[it.i, 8 + j], other,
            )
            for j, r in enumerate(rows)
        ]

    def e6(i):
        it = items[i]
        settle(it)
        if i in owner:

            @pl.when(s != owner[i])
            def _():
                for copy in to_other(it):
                    copy.start()
        else:
            for copy in to_other(it):
                copy.start()

    def e7(i):
        it = items[i]
        if i in owner:

            @pl.when(s != owner[i])
            def _():
                for copy in to_other(it):
                    copy.wait_send()

            @pl.when(s == owner[i])
            def _():
                for copy in to_other(it):
                    copy.wait_recv()
        else:
            for copy in to_other(it):
                copy.wait()

    def gain(block, which):
        return s_sm[block, which : which + 1, :]

    rows = lax.broadcasted_iota(jnp.int32, (SEQ, RQ), 0)
    part = [slice(0, 16), slice(16, 32)]

    first = plan_ref[0, s] == 0
    x_s[...] = jnp.where(first, tok_ref[:SEQ, :], tok_ref[SEQ:, :])
    cot_at = pl.ds(mult(s, SEQ), SEQ)
    ring_start(RCOT, cot_ref.at[cot_at])
    weights(0, 1)
    n1 = rms(x_s[...].astype(F32), gain(0, 0)).astype(BF)
    n1_s[...] = n1
    ring_start(RN1, n1_s)
    uv_s[...] = mm(n1, s_in[...])
    taps = [s_sm[k // 2, 2 + k % 2 : 3 + k % 2, :RQ] for k in range(4)]
    vec = [s_sm[k // 2, 2 + k % 2 : 3 + k % 2, RQ : 2 * RQ] for k in range(4)]
    u = uv_s[:, :RQ]
    c = vec[0] + taps[0] * u
    for k in range(1, 4):
        c = c + taps[k] * rows_back(u, rows, k)
    c_s[...] = c
    weights(2, 3)
    for head in range(4):
        cols = slice(head * HD, head * HD + HD)
        cb = c_s[:, cols].astype(BF)
        ig_s[:, cols] = sigmoid(mm(cb, s_gt[:, cols]) + vec[1][:, cols])
        rg_s[:, cols] = sigmoid(
            mm(cb, s_gt[:, RQ + head * HD : RQ + head * HD + HD]) + vec[2][:, cols]
        )
    speed = softplus(vec[3])
    a = jnp.exp(-8.0 * rg_s[...] * speed)
    a_s[...] = a
    run = jnp.sqrt(jnp.maximum(1.0 - a * a, RATE_FLOOR)) * ig_s[...] * c_s[...]
    step = 1
    while step < SEQ:
        run = run + a * rows_back(run, rows, step)
        if 2 * step < SEQ:
            a = a * jnp.where(rows >= step, pltpu.roll(a, step, 0), 1.0)
        step *= 2
    h_s[...] = run
    o = (run * gelu(uv_s[:, RQ:])).astype(BF)
    for half in range(2):
        sb[0, :, half * HW : half * HW + HW] = mm(o, s_ro[half]).astype(BF)
    scatter_start(0)
    o_t[...] = o.T
    spread_left(RO, o_t, la_o)
    for h in range(2):
        x1 = x_s[mine[h], :].astype(F32) + scatter_wait(0, h)
        res[0, part[h]] = x1
        gather_start(0, h, rms(x1, gain(0, 1)))

    def ffn_forward(block, p_in, p_out):
        n2 = ag[p_in]
        for j in range(3):
            cols = slice(j * CC, j * CC + CC)
            gate = mm(n2, s_g[block, :, cols])
            up = mm(n2, s_u[block, :, cols])
            gate_s[block, :, cols] = gate
            up_s[block, :, cols] = up
            hid_s[:, cols] = (gelu(gate) * up).astype(BF)
        if block == 0:
            weights(6)
        hid = hid_s[...]
        for j in range(4):
            cols = slice(j * CC, j * CC + CC)
            sb[p_out % 2, :, cols] = mm(hid, s_d[block, :, cols]).astype(BF)
        scatter_start(p_out)
        hid_t[block] = hid_s[...].T

    weights(4, 5)
    gather_wait(0)
    ring_start(RN2, ag.at[0])
    ffn_forward(0, 0, 1)
    spread_left(D1, hid_t.at[0], la1)
    for h in range(2):
        mid = (res[0, part[h]] + scatter_wait(1, h)).astype(BF).astype(F32)
        res[1, part[h]] = mid
        gather_start(1, h, rms(mid, gain(1, 0)))
    weights(7, 8, 9)

    gather_wait(1)
    ring_start(RNA, ag.at[1])
    na = ag[1]
    q_s[...] = mm(na, s_q[...]).astype(BF)
    kv_s[...] = mm(na, s_kv[...]).astype(BF)
    keys = kv_s[:, :HD]
    vals = kv_s[:, HD:]
    allowed = lax.broadcasted_iota(jnp.int32, (SEQ, SEQ), 1) <= lax.broadcasted_iota(
        jnp.int32, (SEQ, SEQ), 0
    )
    for head in range(3):
        cols = slice(head * HD, head * HD + HD)
        score = jnp.where(allowed, mm_nt(q_s[:, cols], keys) * HD ** (-0.5), -1e30)
        expo = jnp.exp(score - jnp.max(score, -1, keepdims=True))
        p = expo / jnp.sum(expo, -1, keepdims=True)
        p_s[head] = p
        at_s[:, cols] = mm(p.astype(BF), vals).astype(BF)
    att = at_s[...]
    for half in range(2):
        sb[0, :, half * HW : half * HW + HW] = mm(att, s_ao[half]).astype(BF)
    scatter_start(2)
    att_t[...] = att.T
    spread_left(AO, att_t, la_a)
    for h in range(2):
        x1 = res[1, part[h]] + scatter_wait(2, h)
        res[2, part[h]] = x1
        gather_start(2, h, rms(x1, gain(1, 1)))
    gather_wait(2)
    ring_start(RN2B, ag.at[2])
    ffn_forward(1, 2, 3)
    spread_rows(D2, hid_t.at[1], l_d2)
    ring_load(RCOT)
    for h in range(2):
        yb[part[h], :] = (res[2, part[h]] + scatter_wait(3, h)).astype(BF)
    deliver(yb, y_o, 1, 0)

    def ffn_backward(block, dF, p_out):
        for j in range(3):
            cols = slice(j * CC, j * CC + CC)
            dhid = mm_nt(dF, s_d[block, cols, :])
            value, slope = gelu_both(gate_s[block, :, cols])
            hid_s[:, cols] = (dhid * up_s[block, :, cols] * slope).astype(BF)
            du_s[:, cols] = (dhid * value).astype(BF)
        dg = hid_s[...]
        du = du_s[...]
        for j in range(4):
            cols = slice(j * CC, j * CC + CC)
            sb[p_out % 2, :, cols] = (
                mm_nt(dg, s_g[block, cols, :]) + mm_nt(du, s_u[block, cols, :])
            ).astype(BF)
        scatter_start(p_out)
        g_t[block] = dg.T
        spread_rows(G2 if block else G1, g_t.at[block], l_g2 if block else l_g1)
        u_t[block] = du.T
        spread_rows(U2 if block else U1, u_t.at[block], l_u2 if block else l_u1)

    cot = cot_ref[cot_at, :]
    ffn_backward(1, cot, 4)
    e1(D2)
    e2(D2)
    gg11 = []
    for h in range(2):
        dv, gg = rms_back(res[2, part[h]], gain(1, 1), scatter_wait(4, h))
        gg11.append(gg)
        own = pl.ds(pl.multiple_of(s * SEQ + t * SH + h * 16, 16), 16)
        dx1 = cot_ref[own, :].astype(F32) + dv
        res[3, part[h]] = dx1
        gather_start(3, h, dx1)
    e1(G2)

    gather_wait(3)
    spread_cols(AO, ag.at[3], rc_a)
    dA = ag[3]
    datt_s = both_s.at[:, :AQ]
    dq_s = both_s.at[:, AQ : 2 * AQ]
    datt_s[...] = (mm_nt(dA[:, :HW], s_ao[0]) + mm_nt(dA[:, HW:], s_ao[1])).astype(BF)
    dk = jnp.zeros((SEQ, HD), F32)
    dw = jnp.zeros((SEQ, HD), F32)
    for head in range(3):
        cols = slice(head * HD, head * HD + HD)
        p = p_s[head]
        datt = datt_s[:, cols]
        dpr = mm_nt(datt, kv_s[:, HD:])
        dw = dw + mm(p.astype(BF).T, datt)
        ds = (p * (dpr - jnp.sum(p * dpr, -1, keepdims=True)) * HD ** (-0.5)).astype(BF)
        dq_s[:, cols] = mm(ds, kv_s[:, :HD]).astype(BF)
        dk = dk + mm(ds.T, q_s[:, cols])
    dkvb[0, :, :HD] = dk.astype(BF)
    dkvb[0, :, HD:] = dw.astype(BF)
    kv_copies = [
        push(dkvb.at[0], dkvb.at[k], kvs_sem.at[k], kvr_sem.at[k], (s, peers[k], d))
        for k in range(1, 4)
    ]
    for copy in kv_copies:
        copy.start()
    dq = dq_s[...]
    for j in range(4):
        cols = slice(j * CC, j * CC + CC)
        sb[1, :, cols] = mm_nt(dq, s_q[cols, :]).astype(BF)
    scatter_start(5)
    e2(G2)
    e1(U2)
    ring_load(RNA)
    e3(D2)
    e1(AO)
    for copy in kv_copies:
        copy.wait()
    total = dkvb[0].astype(F32)
    for k in range(1, 4):
        total = total + dkvb[k].astype(F32)
    dkv_s = both_s.at[:, 2 * AQ : 2 * AQ + 256]
    dkv_s[...] = total.astype(BF)
    qkv_t[:AQ] = dq_s[...].T
    qkv_t[AQ:] = dkv_s[...].T
    spread_rows(QKV, qkv_t, l_qkv)
    e2(U2)
    gg10 = []
    for h in range(2):
        dn = scatter_wait(5, h) + mm_nt(dkv_s[mine[h], :], s_kv[...])
        dv, gg = rms_back(res[1, part[h]], gain(1, 0), dn)
        gg10.append(gg)
        big_g = (res[3, part[h]] + dv).astype(BF)
        gather_start(4, h, big_g)
        res[3, part[h]] = big_g.astype(F32)
    e2(AO)
    e3(G2)
    e4(D2)
    e1(QKV)
    ring_load(RN2)
    gather_wait(4)
    spread_cols(D1, ag.at[4], rc1)
    ffn_backward(0, ag[4], 6)
    e3(AO)
    e2(QKV)
    e3(U2)
    e1(D1)
    e4(G2)
    e4(AO)
    gg01 = []
    for h in range(2):
        dv, gg = rms_back(res[0, part[h]], gain(0, 1), scatter_wait(6, h))
        gg01.append(gg)
        dx1 = res[3, part[h]] + dv
        res[3, part[h]] = dx1
        gather_start(5, h, dx1)
    e2(D1)
    e3(QKV)

    gather_wait(5)
    spread_cols(RO, ag.at[5], rc_o)
    dA = ag[5]
    dO = mm_nt(dA[:, :HW], s_ro[0]) + mm_nt(dA[:, HW:], s_ro[1])
    value, slope = gelu_both(uv_s[:, RQ:])
    h = h_s[...]
    both_s[:, RQ:] = (dO * h * slope).astype(BF)
    e = dO * value
    a = a_s[...]
    coef = rows_ahead(a, rows, 1)
    step = 1
    while step < SEQ:
        e = e + coef * rows_ahead(e, rows, step)
        if 2 * step < SEQ:
            coef = coef * rows_ahead(coef, rows, step)
        step *= 2
    ig = ig_s[...]
    rg = rg_s[...]
    c = c_s[...]
    room = 1.0 - a * a
    m = jnp.sqrt(jnp.maximum(room, RATE_FLOOR))
    ga = e * rows_back(h, rows, 1) - jnp.where(room > RATE_FLOOR, e * ig * c * a / m, 0.0)
    dl = ga * a
    gv3 = jnp.sum(dl * rg, 0, keepdims=True) * (-8.0) * sigmoid(vec[3])
    er = -8.0 * dl * speed * rg * (1.0 - rg)
    ei = e * m * c * ig * (1.0 - ig)
    gv1 = jnp.sum(ei, 0, keepdims=True)
    gv2 = jnp.sum(er, 0, keepdims=True)
    c_s[...] = e * m * ig
    ig_s[...] = ei
    rg_s[...] = er
    for head in range(4):
        cols = slice(head * HD, head * HD + HD)
        late = slice(RQ + head * HD, RQ + head * HD + HD)
        dpin = ig_s[:, cols].astype(BF)
        dprec = rg_s[:, cols].astype(BF)
        cbt = c[:, cols].astype(BF).T
        misc_t[:, cols] = mm(cbt, dpin).astype(BF)
        misc_t[:, late] = mm(cbt, dprec).astype(BF)
        c_s[:, cols] += mm_nt(dpin, s_gt[:, cols]) + mm_nt(dprec, s_gt[:, late])
    dc = c_s[...]
    u = uv_s[:, :RQ]
    du = taps[0] * dc
    gtap = [jnp.sum(u * dc, 0, keepdims=True)]
    for k in range(1, 4):
        du = du + taps[k] * rows_ahead(dc, rows, k)
        gtap.append(jnp.sum(rows_back(u, rows, k) * dc, 0, keepdims=True))
    gv0 = jnp.sum(dc, 0, keepdims=True)
    both_s[:, :RQ] = du.astype(BF)
    both = both_s[...]
    for j in range(4):
        cols = slice(j * CC, j * CC + CC)
        sb[1, :, cols] = mm_nt(both, s_in[cols, :]).astype(BF)
    scatter_start(7)
    in_t[...] = both.T
    spread_rows(IN, in_t, l_in)
    e5(D2)
    e5(G2)
    e1(G1)
    e4(QKV)
    gg00 = []
    for h in range(2):
        dv, gg = rms_back(x_s[mine[h], :].astype(F32), gain(0, 0), scatter_wait(7, h))
        gg00.append(gg)
        xb[part[h], :] = (res[3, part[h]] + dv).astype(BF)
    deliver(xb, dx_o, 0, 1)
    gnb[0, 0:1] = gg00[0] + gg00[1]
    gnb[0, 1:2] = gg01[0] + gg01[1]
    gnb[0, 2:3] = gg10[0] + gg10[1]
    gnb[0, 3:4] = gg11[0] + gg11[1]
    gnb[0, 4:8] = jnp.zeros((4, D), F32)
    gn_copies = [
        push(gnb.at[0], gnb.at[k], gns_sem.at[k], gnr_sem.at[k], (s, peers[k], d))
        for k in range(1, 4)
    ]
    for copy in gn_copies:
        copy.start()
    e1(U1)
    ring_load(RN1)
    e2(G1)
    e1(RO)
    e2(U1)
    for copy in gn_copies:
        copy.wait()
    gains = gnb[0] + gnb[1] + gnb[2] + gnb[3]
    small = gtap + [gv0, gv1, gv2, gv3]
    for g in range(4):
        for part in range(3):
            small.append(gains[g : g + 1, part * RQ : part * RQ + RQ])
    small.append(jnp.zeros((HD - len(small), RQ), F32))
    misc_t[:, 2 * RQ :] = jnp.concatenate(small, 0).astype(BF)
    it = items[MISC]

    def misc_rows(f):
        return misc_t.at[pl.ds(mult(f, 32), 32), :]

    l_misc[0] = misc_rows(it.m)[...]
    spread(MISC, 0, misc_rows, lambda k: l_misc.at[k])
    e4(U2)
    e2(RO)
    e1(IN)
    e5(AO)
    e2(IN)
    e6(G2)
    e3(D1)
    e3(G1)
    e6(D2)
    e3(U1)
    e5(QKV)
    e1(MISC)
    e2(MISC)
    e3(RO)
    e5(U2)
    e6(AO)
    e4(G1)
    e3(IN)
    e4(U1)
    e4(D1)
    e3(MISC)
    e6(QKV)
    e4(RO)
    e6(U2)
    e5(G1)
    e5(D1)
    e4(MISC)
    e4(IN)
    e5(RO)
    e6(D1)
    e5(U1)
    e5(IN)
    e6(G1)
    e5(MISC)
    e6(RO)
    e6(U1)
    e6(IN)
    e6(MISC)
    deliver_wait(yb, y_o, 1, 0)
    deliver_wait(xb, dx_o, 0, 1)
    for copy in swap:
        copy.wait_send()
    for copy in sends + cs_busy:
        copy.wait_send()
    for i in (D2, G2, AO, U2, QKV, G1, U1, D1, RO, IN, MISC):
        e7(i)


def whole_call(tokens, plan, cot, gains, conv, vec, weights):
    vm = pl.BlockSpec(memory_space=pltpu.VMEM)
    hbm = pl.BlockSpec(memory_space=pl.ANY)
    V = pltpu.VMEM
    dma = pltpu.SemaphoreType.DMA
    crs, gots, fins = [], [], []
    for i in range(11):
        n8 = PLAN[i][1] // 8
        crs.append(V((n8, D), BF))
        gots.append(V((3, n8, CC), BF))
        fins.append(V((n8, CC), BF))
    shapes = [
        (2, SEQ, D), (2, SEQ, D), (5, 4 * SEQ, D),
        (6, FQ, D), (640, D), (AQ, D), (1024, D), (RQ, D), (HD, D),
    ]
    return pl.pallas_call(
        whole_kernel,
        name="whole",
        out_shape=[jax.ShapeDtypeStruct(shape, BF) for shape in shapes],
        in_specs=[vm, pl.BlockSpec(memory_space=pltpu.SMEM), vm, vm, vm, vm] + [hbm] * 9,
        out_specs=[hbm] * 9,
        scratch_shapes=[
            V((D, 2 * RQ), BF), V((HD, 2 * RQ), BF), V((2, RQ, HW), BF), V((2, 8, D), F32),
            V((2, D, FQ), BF), V((2, D, FQ), BF), V((2, FQ, D), BF),
            V((D, AQ), BF), V((D, 256), BF), V((2, AQ, HW), BF),
            V((6, SEQ, D), BF), V((2, SEQ, D), BF), V((2, 3, SH, D), BF), V((4, SH, D), F32),
            V((SEQ, D), BF), V((SEQ, D), BF), V((SEQ, 2 * RQ), F32),
            V((SEQ, RQ), F32), V((SEQ, RQ), F32), V((SEQ, RQ), F32), V((SEQ, RQ), F32), V((SEQ, RQ), F32),
            V((SEQ, AQ), BF), V((SEQ, 256), BF), V((3, SEQ, SEQ), F32), V((SEQ, AQ), BF),
            V((2, SEQ, FQ), F32), V((2, SEQ, FQ), F32), V((SEQ, FQ), BF),
            V((SEQ, FQ), BF), V((SEQ, 2 * RQ), BF),
            V((4, SEQ, 256), BF), V((4, 8, D), F32), V((SH, D), BF), V((SH, D), BF), V((8, D), F32),
            V((4 * SEQ, D), BF), V((2, FQ, SEQ), BF), V((RQ, SEQ), BF), V((AQ, SEQ), BF),
            V((2, FQ, SEQ), BF), V((2, FQ, SEQ), BF), V((640, SEQ), BF), V((1024, SEQ), BF), V((HD, D), BF),
            V((FQ, 512), BF), V((RQ, 512), BF), V((AQ, 512), BF),
            V((512, CC), BF), V((512, CC), BF), V((512, CC), BF),
            V((288, 512), BF), V((288, 512), BF), V((288, 512), BF), V((288, 512), BF), V((288, 512), BF),
            V((160, 512), BF), V((256, 512), BF), V((4, 32, D), BF),
            V((144, D), BF), V((2, 144, D), BF),
            *crs, *gots, *fins,
            dma((10,)), dma((10,)), dma((10,)), dma((6, 2, 4)), dma((6, 2, 4)), dma((8, 2, 4)), dma((8, 2, 4)),
            dma((4,)), dma((4,)), dma((4,)), dma((4,)), dma((2,)), dma((2, 4)), dma((2, 2, 4)),
            dma((5, 4)), dma((5, 4)), dma((10,)), dma((11, 2, 4)), dma((11, 2, 4)),
            dma((11, 4)), dma((11, 4)), dma((11, 12)), dma((11, 12)), dma((11,)), dma((11,)), dma((11,)),
        ],
        compiler_params=pltpu.CompilerParams(
            collective_id=0, has_side_effects=True, vmem_limit_bytes=63 * 2**20
        ),
    )(tokens, plan, cot, gains, conv, vec, *weights)


def unpack_kernel(
    n_ref, dx, y, ffn, qkv, ao, rin, ro, misc,
    o_bound, o_gain, o_gate, o_up, o_dn, o_in, o_gt, o_conv, o_vec, o_ro, o_q, o_kv, o_ao,
):
    i = pl.program_id(0)
    s = n_ref[0]
    straight = n_ref[1] == 0
    for j in range(2):
        mine = jnp.where(straight, dx[j], dx[1 - j])
        o_bound[0, j * SEQ : j * SEQ + SEQ, :] = jnp.where(s == 0, mine, y[j]).astype(F32)
    o_gate[0] = ffn[0].T.astype(F32)
    o_up[0] = ffn[1].T.astype(F32)
    o_dn[0] = ffn[2].astype(F32)
    part = qkv[...].T.astype(F32)
    o_q[...] = part[:, :AQ]
    o_kv[...] = part[:, AQ:]
    part = rin[...].T.astype(F32)
    o_in[:, 0, :] = part[:, :RQ]
    o_in[:, 1, :] = part[:, RQ:]

    @pl.when(i == 0)
    def _():
        o_ao[...] = ao[...].astype(F32)
        o_ro[...] = ro[...].astype(F32)
        rows = pl.ds(pl.multiple_of(s * 64, 64), 64)
        o_gt[:, 0, :] = misc[rows, :RQ].astype(F32)
        o_gt[:, 1, :] = misc[rows, RQ : 2 * RQ].astype(F32)
        small = misc[:32, 2 * RQ :].astype(F32)

        def pick(at, step):
            return jnp.where(s == 0, small[at : at + step], small[at + step : at + 2 * step])

        o_conv[...] = pick(0, 2)
        o_vec[...] = pick(4, 2)
        gains = pick(8, 6)
        for j in range(2):
            for p in range(3):
                o_gain[0, j : j + 1, p * RQ : p * RQ + RQ] = gains[j * 3 + p : j * 3 + p + 1]


def unpack_call(scalars, dx, y, ffn, qkv, ao, rin, ro, misc):
    n = 6
    wide = D // n
    part = HW // n
    sds = jax.ShapeDtypeStruct
    fixed = lambda *zero: (lambda i, s: zero)
    return pl.pallas_call(
        unpack_kernel,
        name="unpack",
        out_shape=[
            sds((1, 2 * SEQ, D), F32), sds((1, 2, D), F32),
            sds((1, D, FQ), F32), sds((1, D, FQ), F32), sds((1, FQ, D), F32),
            sds((HW, 2, RQ), F32), sds((64, 2, RQ), F32), sds((2, RQ), F32), sds((2, RQ), F32),
            sds((RQ, HW), F32), sds((HW, AQ), F32), sds((HW, 256), F32), sds((AQ, HW), F32),
        ],
        grid_spec=pltpu.PrefetchScalarGridSpec(
            num_scalar_prefetch=1,
            grid=(n,),
            in_specs=[
                pl.BlockSpec((2, SEQ, wide), lambda i, s: (0, 0, i)),
                pl.BlockSpec((2, SEQ, wide), lambda i, s: (0, 0, i)),
                pl.BlockSpec((3, FQ, wide), lambda i, s: (0, 0, i)),
                pl.BlockSpec((640, part), lambda i, s: (0, s[0] * n + i)),
                pl.BlockSpec((AQ, HW), lambda i, s: (0, s[0])),
                pl.BlockSpec((1024, part), lambda i, s: (0, s[0] * n + i)),
                pl.BlockSpec((RQ, HW), lambda i, s: (0, s[0])),
                pl.BlockSpec((HD, D), fixed(0, 0)),
            ],
            out_specs=[
                pl.BlockSpec((1, 2 * SEQ, wide), lambda i, s: (0, 0, i)),
                pl.BlockSpec((1, 2, D), fixed(0, 0, 0)),
                pl.BlockSpec((1, wide, FQ), lambda i, s: (0, i, 0)),
                pl.BlockSpec((1, wide, FQ), lambda i, s: (0, i, 0)),
                pl.BlockSpec((1, FQ, wide), lambda i, s: (0, 0, i)),
                pl.BlockSpec((part, 2, RQ), lambda i, s: (i, 0, 0)),
                pl.BlockSpec((64, 2, RQ), fixed(0, 0, 0)),
                pl.BlockSpec((2, RQ), fixed(0, 0)),
                pl.BlockSpec((2, RQ), fixed(0, 0)),
                pl.BlockSpec((RQ, HW), fixed(0, 0)),
                pl.BlockSpec((part, AQ), lambda i, s: (i, 0)),
                pl.BlockSpec((part, 256), lambda i, s: (i, 0)),
                pl.BlockSpec((AQ, HW), fixed(0, 0)),
            ],
        ),
        compiler_params=pltpu.CompilerParams(vmem_limit_bytes=62 * 2**20),
    )(scalars, dx, y, ffn, qkv, ao, rin, ro, misc)


def per_device(
    tokens, plan_order, cotangent, norm_gains, ffn_gate, ffn_up, ffn_down,
    rec_in, rec_gates, rec_conv, rec_vec, rec_out, att_q, att_kv, att_out,
):
    y, dx, _, ffn, qkv, ao, rin, ro, misc = whole_call(
        tokens, plan_order, cotangent, norm_gains, rec_conv, rec_vec,
        (
            rec_in.reshape(HW, 2 * RQ), rec_gates.reshape(64, 2 * RQ), rec_out,
            ffn_gate, ffn_up, ffn_down, att_q, att_kv, att_out,
        ),
    )
    s = lax.axis_index("section").astype(jnp.int32)
    scalars = jnp.stack([s, plan_order[0, 0]])
    return unpack_call(scalars, dx, y, ffn, qkv, ao, rin, ro, misc)


def solution(mesh):
    placed = (
        P("dp", None),
        P("dp", None),
        P("dp", None),
        P("section", None, None),
        P("section", None, "tensor"),
        P("section", None, "tensor"),
        P("section", "tensor", None),
        P("section", None, "tensor"),
        P("section", None, "tensor"),
        P("section", "tensor"),
        P("section", "tensor"),
        P("tensor", "section"),
        P("section", "tensor"),
        P("section", None),
        P("tensor", "section"),
    )
    return jax.shard_map(
        per_device,
        mesh=mesh,
        in_specs=placed,
        out_specs=(
            P("section", "dp", None),
            P("section", None, None),
            P("section", None, "tensor"),
            P("section", None, "tensor"),
            P("section", "tensor", None),
            P("section", None, "tensor"),
            P("section", None, "tensor"),
            P("section", "tensor"),
            P("section", "tensor"),
            P("tensor", "section"),
            P("section", "tensor"),
            P("section", None),
            P("tensor", "section"),
        ),
        check_vma=False,
    )
```

```python
import jax
import jax.numpy as jnp
from jax import lax
from jax.experimental import pallas as pl
from jax.experimental.pallas import tpu as pltpu
from jax.sharding import PartitionSpec as P

HD = 128
SEQ = 128
NORM_EPS = 1e-06
RATE_FLOOR = 0.01
BF = jnp.bfloat16
F32 = jnp.float32
MESH = pl.DeviceIdType.MESH
NT = (((1,), (1,)), ((), ()))

D = 1536
FQ = 1152
RQ = 512
AQ = 384
SH = 32
CC = 384
HW = 768
X_AXIS = 0
Y_AXIS = 1
G1, U1, D1, G2, U2, D2, QKV, AO, IN, RO, MISC = range(11)
PLAN = {
    G1: ("r", FQ, Y_AXIS),
    U1: ("r", FQ, Y_AXIS),
    D1: ("c", FQ, X_AXIS),
    G2: ("r", FQ, X_AXIS),
    U2: ("r", FQ, X_AXIS),
    D2: ("r", FQ, Y_AXIS),
    QKV: ("r", 640, Y_AXIS),
    AO: ("c", AQ, Y_AXIS),
    IN: ("r", 1024, X_AXIS),
    RO: ("c", RQ, X_AXIS),
    MISC: ("r", HD, Y_AXIS),
}
RING_AXIS = (X_AXIS, Y_AXIS, Y_AXIS, X_AXIS, Y_AXIS)
RN1, RN2, RNA, RN2B, RCOT = range(5)
DIRECT = (U2, D2, AO, MISC,)
ROOM = {G2: 0, U2: 144, G1: 288, U1: 432, D1: 576, QKV: 720, IN: 800, AO: 928, RO: 976, MISC: 1040}


def mm(left, right):
    return jnp.dot(left, right, preferred_element_type=F32)


def mm_nt(left, right):
    return lax.dot_general(left, right, NT, preferred_element_type=F32)


def rms(values, gain):
    return values * lax.rsqrt(jnp.mean(values * values, -1, keepdims=True) + NORM_EPS) * gain


def rms_back(values, gain, dn):
    r = lax.rsqrt(jnp.mean(values * values, -1, keepdims=True) + NORM_EPS)
    dng = dn * gain
    dv = r * (dng - values * (r * r) * jnp.mean(dng * values, -1, keepdims=True))
    return dv, jnp.sum(dn * values * r, 0, keepdims=True)


GC = 0.7978845608028654
GA = 0.044715


def gelu(x):
    return 0.5 * x * (1.0 + jnp.tanh(GC * (x + GA * x * x * x)))


def gelu_both(x):
    th = jnp.tanh(GC * (x + GA * x * x * x))
    value = 0.5 * x * (1.0 + th)
    slope = 0.5 * (1.0 + th) + 0.5 * x * (1.0 - th * th) * GC * (1.0 + 3.0 * GA * x * x)
    return value, slope


def sigmoid(x):
    return 1.0 / (1.0 + jnp.exp(-x))


def softplus(x):
    return jnp.maximum(x, 0.0) + jnp.log(1.0 + jnp.exp(-jnp.abs(x)))


def rows_back(values, rows, k):
    return jnp.where(rows >= k, pltpu.roll(values, k, 0), 0.0)


def rows_ahead(values, rows, k):
    return jnp.where(rows < SEQ - k, pltpu.roll(values, SEQ - k, 0), 0.0)


class Item:
    pass


def whole_kernel(
    tok_ref, plan_ref, cot_ref, gain_ref, conv_ref, vec_ref,
    win, wgt, wro, wg, wu, wd, wq, wkv, wao,
    y_o, dx_o, ra, f_ffn, f_qkv, f_ao, f_in, f_ro, f_misc,
    s_in, s_gt, s_ro, s_sm, s_g, s_u, s_d, s_q, s_kv, s_ao,
    ag, sb, rb, res, x_s, n1_s, uv_s, c_s, ig_s, rg_s, a_s, h_s,
    q_s, kv_s, p_s, at_s, gate_s, up_s, hid_s, du_s, both_s,
    dkvb, gnb, yb, xb, smb,
    work, hid_t, o_t, att_t, g_t, u_t, qkv_t, in_t, misc_t,
    la1, la_o, la_a, rc1, rc_o, rc_a, l_g1, l_u1, l_g2, l_u2, l_d2, l_qkv, l_in, l_misc,
    a_d2, cs, *rest,
):
    crs, gots, fins = rest[:11], rest[11:22], rest[22:33]
    (
        wl_sem, ws_sem, wr_sem, ags_sem, agr_sem, rss_sem, rsr_sem,
        kvs_sem, kvr_sem, gns_sem, gnr_sem, dl_sem, dls_sem, dlr_sem,
        rgs_sem, rgr_sem, wk_sem, xs_sem, xr_sem, ys_sem, yr_sem, gs_sem, gr_sem, loc_sem,
        cs_sem, cr_sem,
    ) = rest[33:]
    s = lax.axis_index("section")
    t = lax.axis_index("tensor")
    d = lax.axis_index("dp")
    place = (lax.rem(d, 4), d // 4)
    peers = [lax.rem(t + k, 4) for k in range(4)]
    def own_rows(h):
        return pl.ds(pl.multiple_of(h * 64 + t * 16, 16), 16)

    mine = [own_rows(h) for h in range(2)]

    def half_of(h):
        return pl.ds(pl.multiple_of(h * 64, 64), 64)


    def pos(base, k):
        return lax.rem(base + k, 4)

    def along(axis, k, core):
        if axis == X_AXIS:
            return (core, t, place[1] * 4 + pos(place[0], k))
        return (core, t, pos(place[1], k) * 4 + place[0])

    barrier = pltpu.get_barrier_semaphore()
    other = (1 - s, t, d)
    for k in range(1, 4):
        for target in (
            (s, peers[k], d), (1 - s, peers[k], d), along(X_AXIS, k, s), along(Y_AXIS, k, s),
        ):
            pl.semaphore_signal(barrier, inc=1, device_id=target, device_id_type=MESH)
    pl.semaphore_signal(barrier, inc=1, device_id=other, device_id_type=MESH)

    def push(src, dst, send_sem, recv_sem, target):
        return pltpu.make_async_remote_copy(
            src_ref=src, dst_ref=dst, send_sem=send_sem, recv_sem=recv_sem,
            device_id=target, device_id_type=MESH,
        )

    smb[...] = jnp.zeros((8, D), F32)
    smb[0:2, :] = gain_ref[0]
    smb[2:4, :RQ] = conv_ref[...].astype(F32)
    smb[2:4, RQ : 2 * RQ] = vec_ref[...].astype(F32)
    half_in = pl.ds(pl.multiple_of(s * HW, HW), HW)
    half_gt = pl.ds(pl.multiple_of(s * 64, 64), 64)
    moves = [
        (win, s_in.at[half_in, :]),
        (smb, s_sm.at[s]),
        (wgt, s_gt.at[half_gt, :]),
        (wro, s_ro.at[s]),
        (wg.at[0], s_g.at[s]),
        (wu.at[0], s_u.at[s]),
        (wd.at[0], s_d.at[s]),
        (wq, s_q.at[half_in, :]),
        (wkv, s_kv.at[half_in, :]),
        (wao, s_ao.at[s]),
    ]
    local = [pltpu.make_async_copy(a, b, wl_sem.at[i]) for i, (a, b) in enumerate(moves)]
    swap = [push(a, b, ws_sem.at[i], wr_sem.at[i], other) for i, (a, b) in enumerate(moves)]
    for copy in local:
        copy.start()
    pl.semaphore_wait(barrier, 13)
    for copy in swap:
        copy.start()

    def weights(*which):
        for i in which:
            local[i].wait()
            swap[i].wait_recv()


    sub = [slice(0, 16), slice(16, 32)]

    def gather(p, h):
        return [
            push(
                ag.at[p, own_rows(h)], ag.at[p, own_rows(h)], ags_sem.at[p, h, k], agr_sem.at[p, h, k],
                (s, peers[k], d),
            )
            for k in (2, 1, 3)
        ]

    def gather_start(p, h, shard):
        ag[p, mine[h], :] = shard.astype(BF)
        for copy in gather(p, h):
            copy.start()

    def gather_wait(p, h):
        for copy in gather(p, h):
            copy.wait()

    def scatter(p, h):
        return [
            push(
                sb.at[p % 2, pl.ds(pl.multiple_of(h * 64 + peers[k] * 16, 16), 16)],
                rb.at[p % 2, k - 1, pl.ds(pl.multiple_of(h * 16, 16), 16)],
                rss_sem.at[p, h, k], rsr_sem.at[p, h, k], (s, peers[k], d),
            )
            for k in (2, 1, 3)
        ]

    def scatter_start(p, *halves):
        for h in halves:
            for copy in scatter(p, h):
                copy.start()

    def scatter_wait(p, h):
        for copy in scatter(p, h):
            copy.wait()
        total = sb[p % 2, mine[h], :].astype(F32)
        for k in range(3):
            total = total + rb[p % 2, k, h * 16 : h * 16 + 16].astype(F32)
        return total

    def deliver_copy(buf, out, core, which, k, h):
        return push(
            buf.at[sub[h]], out.at[s, mine[h]], dls_sem.at[which, k, h],
            dlr_sem.at[which, s, k, h], (core, peers[k], d),
        )

    def deliver(buf, out, core, which):
        @pl.when(s == core)
        def _():
            own = [
                pltpu.make_async_copy(buf.at[sub[h]], out.at[s, mine[h]], dl_sem.at[which, h])
                for h in range(2)
            ]
            for copy in own:
                copy.start()
            for k in range(1, 4):
                for h in range(2):
                    deliver_copy(buf, out, core, which, k, h).start()
            for copy in own:
                copy.wait()

        @pl.when(s != core)
        def _():
            for k in range(4):
                for h in range(2):
                    deliver_copy(buf, out, core, which, k, h).start()

    def deliver_wait(buf, out, core, which):
        def landed(sender, k, h):
            push(
                buf.at[sub[h]], out.at[sender, mine[h]], dls_sem.at[which, k, h],
                dlr_sem.at[which, sender, k, h], (core, peers[k], d),
            ).wait_recv()

        for h in range(2):

            @pl.when(s == core)
            def _(h=h):
                for k in range(1, 4):
                    deliver_copy(buf, out, core, which, k, h).wait_send()
                    landed(core, k, h)
                for k in range(4):
                    landed(1 - core, k, h)

            @pl.when(s != core)
            def _(h=h):
                for k in range(4):
                    deliver_copy(buf, out, core, which, k, h).wait_send()


    sends = []

    def mult(x, by):
        return pl.multiple_of(x * by, by)

    def slot(place_at):
        return pl.ds(mult(place_at, SEQ), SEQ)

    ring_got = [None] * 5

    def ring_make(g, src):
        axis = RING_AXIS[g]
        here = ra.at[g, slot(place[axis])]
        stay = pltpu.make_async_copy(src, here, wk_sem.at[g])
        copies = [
            push(src, here, rgs_sem.at[g, k], rgr_sem.at[g, k], along(axis, k, s)) for k in (1, 3)
        ]
        sends.extend(copies)
        ring_got[g] = [stay, copies]

    def ring_go(g):
        ring_got[g][0].start()
        for copy in ring_got[g][1]:
            copy.start()

    def ring_start(g, src):
        ring_make(g, src)
        ring_go(g)

    def ring_pass(g):
        axis = RING_AXIS[g]
        copies = []
        for j, (side, back) in enumerate(((1, 3), (3, 1))):
            ring_got[g][1][j].wait_recv()
            rows = ra.at[g, pl.ds(mult(pos(place[axis], back) * 2 + j, 64), 64)]
            copy = push(rows, rows, rgs_sem.at[g, 2 * j], rgr_sem.at[g, 2 * j], along(axis, side, s))
            copy.start()
            copies.append(copy)
        sends.extend(copies)
        ring_got[g][1] = copies

    in_work = [None, None]

    def ring_load(g):
        if in_work[0] == g:
            return
        ring_got[g][0].wait()
        for copy in ring_got[g][1]:
            copy.wait_recv()
        copy = pltpu.make_async_copy(ra.at[g], work, wk_sem.at[5 + g])
        copy.start()
        in_work[0] = g
        in_work[1] = copy

    def ring_use(g):
        ring_load(g)
        if in_work[1] is not None:
            in_work[1].wait()
            in_work[1] = None


    full = {QKV: f_qkv, AO: f_ao, IN: f_in, RO: f_ro, MISC: f_misc}
    owner = {G1: 0, U1: 0, D1: 0, G2: 1, U2: 1, D2: 1}
    items = []
    for i in range(11):
        it = Item()
        it.i = i
        it.style, it.total, it.axis = PLAN[i]
        it.n8 = it.total // 8
        it.m = place[it.axis]
        it.n = place[1 - it.axis]
        it.cr, it.got, it.fin = crs[i], gots[i], fins[i]
        it.acc = a_d2 if i == D2 else s_d.at[1, ROOM[i] : ROOM[i] + it.n8]
        if i in owner:
            it.full = f_ffn.at[(s if owner[i] == 0 else 1 - s) * 3 + i % 3]
            it.home = f_ffn.at[i % 3]
        else:
            it.full = full[i]
            it.home = full[i]
        it.waits = []
        items.append(it)

    def spread(i, which, source, target):
        it = items[i]
        for k in range(1, 4):
            copy = push(
                source(pos(it.m, k)), target(k), xs_sem.at[i, which, k], xr_sem.at[i, which, k],
                along(it.axis, k, s),
            )
            copy.start()
            sends.append(copy)
            it.waits.append(copy)

    def spread_rows(i, whole, into):
        it = items[i]

        def part(f):
            return whole.at[pl.ds(mult(f, 2 * it.n8), 2 * it.n8), :]

        into[:, slot(it.m)] = part(it.m)[...]
        spread(i, 0, part, lambda k: into.at[:, slot(it.m)])

    def spread_left(i, whole, into):
        it = items[i]
        into[:, slot(it.m)] = whole[...]
        spread(i, 0, lambda f: whole, lambda k: into.at[:, slot(it.m)])

    def spread_cols(i, src, into):
        it = items[i]

        def cut(f):
            return pl.ds(mult(f, CC), CC)

        into[slot(it.m), :] = src[:, cut(it.m)]
        spread(i, 1, lambda f: src.at[:, cut(f)], lambda k: into.at[slot(it.m), :])

    def arrived(it):
        for copy in it.waits:
            copy.wait_recv()
        it.waits = []

    def settle(it):
        for copy in it.waits:
            copy.wait()
        it.waits = []

    def piece(it, q):
        return it.acc.at[:, pl.ds(mult(q, CC), CC)]

    cs_busy = [None, None]
    cs_count = [0]

    def halves(i, fill):
        it = items[i]
        at = cs_count[0] % 2
        cs_count[0] += 1
        if cs_busy[at] is not None:
            cs_busy[at].wait_send()
        out = cs.at[at, : it.n8]
        fill(1 - s, out)
        copy = push(out, it.cr, cs_sem.at[i], cr_sem.at[i], other)
        copy.start()
        cs_busy[at] = copy
        it.swap = copy
        fill(s, it.acc)

    def rows_product(i, ring, left):
        it = items[i]
        arrived(it)
        ring_use(ring)

        def fill(h, ref):
            rows = left[pl.ds(mult(h, it.n8), it.n8), :]
            for j in range(4):
                cols = slice(j * CC, j * CC + CC)
                ref[:, cols] = mm(rows, work[:, cols]).astype(BF)

        halves(i, fill)

    def cols_product(i, left, right):
        it = items[i]
        arrived(it)

        def fill(h, ref):
            for q in range(4):
                rows = left[pl.ds(mult(h * 4 + q, it.n8), it.n8), :]
                ref[:, q * CC : q * CC + CC] = mm(rows, right[...]).astype(BF)

        halves(i, fill)

    def misc_sum():
        it = items[MISC]
        arrived(it)

        def fill(h, ref):
            at = pl.ds(mult(h, it.n8), it.n8)
            total = l_misc[0, at, :].astype(F32)
            for k in range(1, 4):
                total = total + l_misc[k, at, :].astype(F32)
            ref[...] = total.astype(BF)

        halves(MISC, fill)

    row_items = {
        G1: (RN2, l_g1), U1: (RN2, l_u1), G2: (RN2B, l_g2), U2: (RN2B, l_u2),
        D2: (RCOT, l_d2), QKV: (RNA, l_qkv), IN: (RN1, l_in),
    }
    col_items = {D1: (la1, rc1), AO: (la_a, rc_a), RO: (la_o, rc_o)}

    def e1(i):
        if i in row_items:
            rows_product(i, *row_items[i])
        elif i in col_items:
            cols_product(i, *col_items[i])
        else:
            misc_sum()

    def cut_of(it):
        return {144: 80, 80: 48, 128: 64, 48: 32, 64: 32}[it.n8]

    def sides(it, at, axis, right, left):
        for j, (side, (src, dst)) in enumerate(((1, right), (3, left))):
            copy = push(src, dst, ys_sem.at[it.i, at + j], yr_sem.at[it.i, at + j], along(axis, side, s))
            copy.start()
            it.waits.append(copy)

    def e2(i):
        it = items[i]
        it.swap.wait_recv()
        it.acc[...] = (it.acc[...].astype(F32) + it.cr[...].astype(F32)).astype(BF)
        if i in DIRECT:
            for k in range(1, 4):
                copy = push(
                    piece(it, pos(it.n, k)), it.got.at[k - 1], ys_sem.at[i, k], yr_sem.at[i, k],
                    along(1 - it.axis, k, s),
                )
                copy.start()
                it.waits.append(copy)
            return
        cut = cut_of(it)
        far = piece(it, pos(it.n, 2))
        sides(
            it, 0, 1 - it.axis, (far.at[:cut], it.got.at[0, :cut]), (far.at[cut:], it.got.at[0, cut:])
        )

    def e2r(i):
        it = items[i]
        if i in DIRECT:
            return
        settle(it)
        cut = cut_of(it)
        right = piece(it, pos(it.n, 1))
        left = piece(it, pos(it.n, 3))
        right[:cut] = (right[:cut].astype(F32) + it.got[0, :cut].astype(F32)).astype(BF)
        left[cut:] = (left[cut:].astype(F32) + it.got[0, cut:].astype(F32)).astype(BF)
        sides(it, 2, 1 - it.axis, (right, it.got.at[1]), (left, it.got.at[2]))

    def rect(it, ref, f, q, lo=0, n=None):
        block, at = (f * 2 + s, q) if it.style == "r" else (s * 4 + q, f)
        rows = pl.ds(pl.multiple_of(block * it.n8 + lo, 16), n or it.n8)
        return ref.at[rows, pl.ds(mult(at, CC), CC)]

    def quarter(it, ref, f, part=None):
        if it.style == "r":
            rows = pl.ds(mult(f * 2 + s, it.n8), it.n8)
            if part is None:
                return ref.at[rows, :]
            return ref.at[rows, part * HW : part * HW + HW]
        cols = pl.ds(mult(f, CC), CC)
        if part is None:
            return ref.at[pl.ds(mult(s, 4 * it.n8), 4 * it.n8), cols]
        return ref.at[pl.ds(mult(s * 2 + part, 2 * it.n8), 2 * it.n8), cols]

    def e3(i):
        it = items[i]
        settle(it)
        total = piece(it, it.n)[...].astype(F32)
        for k in range(3) if i in DIRECT else (1, 2):
            total = total + it.got[k].astype(F32)
        it.fin[...] = total.astype(BF)
        spot = rect(it, it.full, it.m, it.n)
        own = pltpu.make_async_copy(it.fin, spot, loc_sem.at[i])
        own.start()
        it.waits.append(own)
        if i in DIRECT:
            for k in range(1, 4):
                copy = push(
                    it.fin, spot, gs_sem.at[i, k], gr_sem.at[i, k], along(1 - it.axis, k, s)
                )
                copy.start()
                it.waits.append(copy)
            return
        sides(it, 4, 1 - it.axis, (it.fin, spot), (it.fin, spot))

    def e3r(i):
        it = items[i]
        if i in DIRECT:
            return
        settle(it)
        cut = cut_of(it)
        left = rect(it, it.full, it.m, pos(it.n, 3), 0, cut)
        right = rect(it, it.full, it.m, pos(it.n, 1), cut, it.n8 - cut)
        sides(it, 6, 1 - it.axis, (left, left), (right, right))

    def both_ways(it, at, right, left):
        for side, part in ((1, right), (3, left)):
            copy = push(
                part, part, gs_sem.at[it.i, at + side // 2], gr_sem.at[it.i, at + side // 2],
                along(it.axis, side, s),
            )
            copy.start()
            it.waits.append(copy)

    def e4(i):
        it = items[i]
        settle(it)
        part = quarter(it, it.full, it.m)
        both_ways(it, 4, part, part)

    def e5(i):
        it = items[i]
        settle(it)
        both_ways(
            it, 6, quarter(it, it.full, pos(it.m, 3), 0), quarter(it, it.full, pos(it.m, 1), 1)
        )

    def to_other(it):
        if it.style == "c":
            rows = [pl.ds(mult(s, 4 * it.n8), 4 * it.n8)]
        else:
            rows = [pl.ds(mult(f * 2 + s, it.n8), it.n8) for f in range(4)]
        cols = pl.ds(0, D)
        if it.i in (QKV, AO, IN, RO):
            cols = pl.ds(mult(1 - s, HW), HW)
        return [
            push(
                it.full.at[r, cols], it.home.at[r, cols],
                gs_sem.at[it.i, 8 + j], gr_sem.at[it.i, 8 + j], other,
            )
            for j, r in enumerate(rows)
        ]

    def e6(i):
        it = items[i]
        settle(it)
        if i in owner:

            @pl.when(s != owner[i])
            def _():
                for copy in to_other(it):
                    copy.start()
        else:
            for copy in to_other(it):
                copy.start()

    def e7(i):
        it = items[i]
        if i in owner:

            @pl.when(s != owner[i])
            def _():
                for copy in to_other(it):
                    copy.wait_send()

            @pl.when(s == owner[i])
            def _():
                for copy in to_other(it):
                    copy.wait_recv()
        else:
            for copy in to_other(it):
                copy.wait()

    def gain(block, which):
        return s_sm[block, which : which + 1, :]

    rows = lax.broadcasted_iota(jnp.int32, (SEQ, RQ), 0)

    first = plan_ref[0, s] == 0
    x_s[...] = jnp.where(first, tok_ref[:SEQ, :], tok_ref[SEQ:, :])
    cot_at = pl.ds(mult(s, SEQ), SEQ)
    ring_start(RCOT, cot_ref.at[cot_at])
    weights(0, 1)
    n1 = rms(x_s[...].astype(F32), gain(0, 0)).astype(BF)
    n1_s[...] = n1
    ring_start(RN1, n1_s)
    uv_s[...] = mm(n1, s_in[...])
    taps = [s_sm[k // 2, 2 + k % 2 : 3 + k % 2, :RQ] for k in range(4)]
    vec = [s_sm[k // 2, 2 + k % 2 : 3 + k % 2, RQ : 2 * RQ] for k in range(4)]
    u = uv_s[:, :RQ]
    c = vec[0] + taps[0] * u
    for k in range(1, 4):
        c = c + taps[k] * rows_back(u, rows, k)
    c_s[...] = c
    weights(2, 3)
    for head in range(4):
        cols = slice(head * HD, head * HD + HD)
        cb = c_s[:, cols].astype(BF)
        ig_s[:, cols] = sigmoid(mm(cb, s_gt[:, cols]) + vec[1][:, cols])
        rg_s[:, cols] = sigmoid(
            mm(cb, s_gt[:, RQ + head * HD : RQ + head * HD + HD]) + vec[2][:, cols]
        )
    speed = softplus(vec[3])
    a = jnp.exp(-8.0 * rg_s[...] * speed)
    a_s[...] = a
    run = jnp.sqrt(jnp.maximum(1.0 - a * a, RATE_FLOOR)) * ig_s[...] * c_s[...]
    step = 1
    while step < SEQ:
        run = run + a * rows_back(run, rows, step)
        if 2 * step < SEQ:
            a = a * jnp.where(rows >= step, pltpu.roll(a, step, 0), 1.0)
        step *= 2
    h_s[...] = run
    o = (run * gelu(uv_s[:, RQ:])).astype(BF)
    for half in range(2):
        sb[0, :, half * HW : half * HW + HW] = mm(o, s_ro[half]).astype(BF)
    scatter_start(0, 0, 1)
    o_t[...] = o.T
    spread_left(RO, o_t, la_o)
    for h in range(2):
        x1 = x_s[mine[h], :].astype(F32) + scatter_wait(0, h)
        res[0, sub[h]] = x1
        gather_start(0, h, rms(x1, gain(0, 1)))

    def ffn_forward(block, p_in, p_out, ring):
        ring_make(ring, ag.at[p_in])

        def one(h, carry):
            gather_wait(p_in, h)
            half = half_of(h)
            n2 = ag[p_in, half, :]

            @pl.when(h == 1)
            def _():
                ring_go(ring)

            for j in range(3):
                cols = slice(j * CC, j * CC + CC)
                gate = mm(n2, s_g[block, :, cols])
                up = mm(n2, s_u[block, :, cols])
                gate_s[block, half, cols] = gate
                up_s[block, half, cols] = up
                hid_s[half, cols] = (gelu(gate) * up).astype(BF)
            if block == 0:

                @pl.when(h == 0)
                def _():
                    weights(6)

            hid = hid_s[half, :]
            for j in range(4):
                cols = slice(j * CC, j * CC + CC)
                sb[p_out % 2, half, cols] = mm(hid, s_d[block, :, cols]).astype(BF)
            scatter_start(p_out, h)
            return carry

        lax.fori_loop(0, 2, one, 0)
        hid_t[block] = hid_s[...].T

    weights(4, 5)
    ffn_forward(0, 0, 1, RN2)
    spread_left(D1, hid_t.at[0], la1)
    ring_pass(RCOT)
    ring_pass(RN1)
    for h in range(2):
        mid = (res[0, sub[h]] + scatter_wait(1, h)).astype(BF).astype(F32)
        res[1, sub[h]] = mid
        gather_start(1, h, rms(mid, gain(1, 0)))
    weights(7, 8, 9)

    p_s[:, :64, 64:] = jnp.zeros((3, 64, 64), F32)
    for h in range(2):
        gather_wait(1, h)
        if h == 1:
            ring_start(RNA, ag.at[1])
        half = slice(h * 64, h * 64 + 64)
        n = 64 * h + 64
        na = ag[1, half]
        q_s[half] = mm(na, s_q[...]).astype(BF)
        kv_s[half] = mm(na, s_kv[...]).astype(BF)
        keys = kv_s[:n, :HD]
        vals = kv_s[:n, HD:]
        col = lax.broadcasted_iota(jnp.int32, (64, n), 1)
        row = lax.broadcasted_iota(jnp.int32, (64, n), 0) + 64 * h
        for head in range(3):
            cols = slice(head * HD, head * HD + HD)
            score = jnp.where(col <= row, mm_nt(q_s[half, cols], keys) * HD ** (-0.5), -1e30)
            expo = jnp.exp(score - jnp.max(score, -1, keepdims=True))
            p = expo / jnp.sum(expo, -1, keepdims=True)
            p_s[head, half, :n] = p
            at_s[half, cols] = mm(p.astype(BF), vals).astype(BF)
        for c in range(2):
            sb[0, half, c * HW : c * HW + HW] = mm(at_s[half], s_ao[c]).astype(BF)
        scatter_start(2, h)
    att = at_s[...]
    att_t[...] = att.T
    spread_left(AO, att_t, la_a)
    ring_pass(RN2)
    for h in range(2):
        x1 = res[1, sub[h]] + scatter_wait(2, h)
        res[2, sub[h]] = x1
        gather_start(2, h, rms(x1, gain(1, 1)))
    ffn_forward(1, 2, 3, RN2B)
    spread_rows(D2, hid_t.at[1], l_d2)
    ring_load(RCOT)

    def ffn_back_rows(block, half, dF, p_out):
        for j in range(3):
            cols = slice(j * CC, j * CC + CC)
            dhid = mm_nt(dF, s_d[block, cols, :])
            value, slope = gelu_both(gate_s[block, half, cols])
            hid_s[half, cols] = (dhid * up_s[block, half, cols] * slope).astype(BF)
            du_s[half, cols] = (dhid * value).astype(BF)
        dg = hid_s[half, :]
        du = du_s[half, :]
        for j in range(4):
            cols = slice(j * CC, j * CC + CC)
            sb[p_out % 2, half, cols] = (
                mm_nt(dg, s_g[block, cols, :]) + mm_nt(du, s_u[block, cols, :])
            ).astype(BF)

    def ffn_back_send(block):
        g_t[block] = hid_s[...].T
        spread_rows(G2 if block else G1, g_t.at[block], l_g2 if block else l_g1)
        u_t[block] = du_s[...].T
        spread_rows(U2 if block else U1, u_t.at[block], l_u2 if block else l_u1)

    ffn_back_rows(1, pl.ds(0, SEQ), cot_ref[cot_at, :], 4)
    scatter_start(4, 0, 1)
    ffn_back_send(1)
    for h in range(2):
        yb[sub[h], :] = (res[2, sub[h]] + scatter_wait(3, h)).astype(BF)
    ring_pass(RNA)
    ring_pass(RN2B)
    e1(D2)
    gg11 = []
    for h in range(2):
        dv, gg = rms_back(res[2, sub[h]], gain(1, 1), scatter_wait(4, h))
        gg11.append(gg)
        own = pl.ds(pl.multiple_of(s * SEQ + h * 64 + t * 16, 16), 16)
        dx1 = cot_ref[own, :].astype(F32) + dv
        res[3, sub[h]] = dx1
        gather_start(3, h, dx1)
    e2(D2)

    gather_wait(3, 0)
    gather_wait(3, 1)
    spread_cols(AO, ag.at[3], rc_a)
    dA = ag[3]
    datt_s = both_s.at[:, :AQ]
    dq_s = both_s.at[:, AQ : 2 * AQ]
    datt_s[...] = (mm_nt(dA[:, :HW], s_ao[0]) + mm_nt(dA[:, HW:], s_ao[1])).astype(BF)
    dk = jnp.zeros((SEQ, HD), F32)
    dw = jnp.zeros((SEQ, HD), F32)
    for head in range(3):
        cols = slice(head * HD, head * HD + HD)
        p = p_s[head]
        datt = datt_s[:, cols]
        dpr = mm_nt(datt, kv_s[:, HD:])
        dw = dw + mm(p.astype(BF).T, datt)
        ds = (p * (dpr - jnp.sum(p * dpr, -1, keepdims=True)) * HD ** (-0.5)).astype(BF)
        dq_s[:, cols] = mm(ds, kv_s[:, :HD]).astype(BF)
        dk = dk + mm(ds.T, q_s[:, cols])
    dkvb[0, :, :HD] = dk.astype(BF)
    dkvb[0, :, HD:] = dw.astype(BF)
    kv_copies = [
        push(dkvb.at[0], dkvb.at[k], kvs_sem.at[k], kvr_sem.at[k], (s, peers[k], d))
        for k in range(1, 4)
    ]
    for copy in kv_copies:
        copy.start()
    dq = dq_s[...]
    for j in range(4):
        cols = slice(j * CC, j * CC + CC)
        sb[1, :, cols] = mm_nt(dq, s_q[cols, :]).astype(BF)
    scatter_start(5, 0, 1)
    e1(G2)
    e1(U2)
    ring_load(RNA)
    e3(D2)
    for copy in kv_copies:
        copy.wait()
    total = dkvb[0].astype(F32)
    for k in range(1, 4):
        total = total + dkvb[k].astype(F32)
    dkv_s = both_s.at[:, 2 * AQ : 2 * AQ + 256]
    dkv_s[...] = total.astype(BF)
    qkv_t[:AQ] = dq_s[...].T
    qkv_t[AQ:] = dkv_s[...].T
    spread_rows(QKV, qkv_t, l_qkv)
    e1(AO)
    e2(G2)
    e2(U2)
    gg10 = []
    for h in range(2):
        dn = scatter_wait(5, h) + mm_nt(dkv_s[mine[h], :], s_kv[...])
        dv, gg = rms_back(res[1, sub[h]], gain(1, 0), dn)
        gg10.append(gg)
        big_g = (res[3, sub[h]] + dv).astype(BF)
        gather_start(4, h, big_g)
        res[3, sub[h]] = big_g.astype(F32)
    e2(AO)
    e1(QKV)
    ring_load(RN2)
    e2r(G2)

    it = items[D1]
    cols_at = [pl.ds(mult(pos(it.m, k), CC), CC) for k in range(4)]
    d1_copies = [
        push(
            ag.at[4, :, cols_at[k]], rc1.at[slot(it.m), :], xs_sem.at[D1, 1, k], xr_sem.at[D1, 1, k],
            along(it.axis, k, s),
        )
        for k in range(1, 4)
    ]
    d1_rows = slot(it.m)

    def back_half(h, carry):
        gather_wait(4, h)

        @pl.when(h == 1)
        def _():
            rc1[d1_rows, :] = ag[4, :, cols_at[0]]
            for copy in d1_copies:
                copy.start()

        ffn_back_rows(0, half_of(h), ag[4, half_of(h), :], 6)
        scatter_start(6, h)
        return carry

    lax.fori_loop(0, 2, back_half, 0)
    it.waits += d1_copies
    sends.extend(d1_copies)
    ffn_back_send(0)
    e3(G2)
    e3(U2)
    e3(AO)
    e2(QKV)
    gg01 = []
    for h in range(2):
        dv, gg = rms_back(res[0, sub[h]], gain(0, 1), scatter_wait(6, h))
        gg01.append(gg)
        dx1 = res[3, sub[h]] + dv
        res[3, sub[h]] = dx1
        gather_start(5, h, dx1)
    e2r(QKV)
    e1(D1)
    e1(G1)
    e2(D1)
    e3(QKV)
    e1(U1)
    ring_load(RN1)

    gather_wait(5, 0)
    gather_wait(5, 1)
    spread_cols(RO, ag.at[5], rc_o)
    dA = ag[5]
    dO = mm_nt(dA[:, :HW], s_ro[0]) + mm_nt(dA[:, HW:], s_ro[1])
    value, slope = gelu_both(uv_s[:, RQ:])
    h = h_s[...]
    both_s[:, RQ:] = (dO * h * slope).astype(BF)
    e = dO * value
    a = a_s[...]
    coef = rows_ahead(a, rows, 1)
    step = 1
    while step < SEQ:
        e = e + coef * rows_ahead(e, rows, step)
        if 2 * step < SEQ:
            coef = coef * rows_ahead(coef, rows, step)
        step *= 2
    ig = ig_s[...]
    rg = rg_s[...]
    c = c_s[...]
    room = 1.0 - a * a
    m = jnp.sqrt(jnp.maximum(room, RATE_FLOOR))
    ga = e * rows_back(h, rows, 1) - jnp.where(room > RATE_FLOOR, e * ig * c * a / m, 0.0)
    dl = ga * a
    gv3 = jnp.sum(dl * rg, 0, keepdims=True) * (-8.0) * sigmoid(vec[3])
    er = -8.0 * dl * speed * rg * (1.0 - rg)
    ei = e * m * c * ig * (1.0 - ig)
    gv1 = jnp.sum(ei, 0, keepdims=True)
    gv2 = jnp.sum(er, 0, keepdims=True)
    c_s[...] = e * m * ig
    ig_s[...] = ei
    rg_s[...] = er
    for head in range(4):
        cols = slice(head * HD, head * HD + HD)
        late = slice(RQ + head * HD, RQ + head * HD + HD)
        dpin = ig_s[:, cols].astype(BF)
        dprec = rg_s[:, cols].astype(BF)
        cbt = c[:, cols].astype(BF).T
        misc_t[:, cols] = mm(cbt, dpin).astype(BF)
        misc_t[:, late] = mm(cbt, dprec).astype(BF)
        c_s[:, cols] += mm_nt(dpin, s_gt[:, cols]) + mm_nt(dprec, s_gt[:, late])
    dc = c_s[...]
    u = uv_s[:, :RQ]
    du = taps[0] * dc
    gtap = [jnp.sum(u * dc, 0, keepdims=True)]
    for k in range(1, 4):
        du = du + taps[k] * rows_ahead(dc, rows, k)
        gtap.append(jnp.sum(rows_back(u, rows, k) * dc, 0, keepdims=True))
    gv0 = jnp.sum(dc, 0, keepdims=True)
    both_s[:, :RQ] = du.astype(BF)
    both = both_s[...]
    for j in range(4):
        cols = slice(j * CC, j * CC + CC)
        sb[1, :, cols] = mm_nt(both, s_in[cols, :]).astype(BF)
    scatter_start(7, 0, 1)
    in_t[...] = both.T
    spread_rows(IN, in_t, l_in)
    e3r(QKV)
    e3r(G2)
    e2(G1)
    e2(U1)
    e4(AO)
    e1(RO)
    e2r(D1)
    e4(U2)
    gg00 = []
    for h in range(2):
        dv, gg = rms_back(x_s[mine[h], :].astype(F32), gain(0, 0), scatter_wait(7, h))
        gg00.append(gg)
        xb[sub[h], :] = (res[3, sub[h]] + dv).astype(BF)
    deliver(xb, dx_o, 0, 1)
    gnb[0, 0:1] = gg00[0] + gg00[1]
    gnb[0, 1:2] = gg01[0] + gg01[1]
    gnb[0, 2:3] = gg10[0] + gg10[1]
    gnb[0, 3:4] = gg11[0] + gg11[1]
    gnb[0, 4:8] = jnp.zeros((4, D), F32)
    gn_copies = [
        push(gnb.at[0], gnb.at[k], gns_sem.at[k], gnr_sem.at[k], (s, peers[k], d))
        for k in range(1, 4)
    ]
    for copy in gn_copies:
        copy.start()
    e2(RO)
    e1(IN)
    e2r(G1)
    e2r(U1)
    e4(QKV)
    e5(AO)
    e3(D1)
    e2(IN)
    e2r(RO)
    deliver(yb, y_o, 1, 0)
    for copy in gn_copies:
        copy.wait()
    gains = gnb[0] + gnb[1] + gnb[2] + gnb[3]
    small = gtap + [gv0, gv1, gv2, gv3]
    for g in range(4):
        for part in range(3):
            small.append(gains[g : g + 1, part * RQ : part * RQ + RQ])
    small.append(jnp.zeros((HD - len(small), RQ), F32))
    misc_t[:, 2 * RQ :] = jnp.concatenate(small, 0).astype(BF)
    it = items[MISC]

    def misc_rows(f):
        return misc_t.at[pl.ds(mult(f, 32), 32), :]

    l_misc[0] = misc_rows(it.m)[...]
    spread(MISC, 0, misc_rows, lambda k: l_misc.at[k])
    e4(G2)
    e4(D2)
    e5(QKV)
    e6(AO)
    e5(U2)
    e3r(D1)
    e3(G1)
    e2r(IN)
    e3(RO)
    e3(U1)
    e1(MISC)
    e2(MISC)
    e5(G2)
    e5(D2)
    e6(U2)
    e6(QKV)
    e3r(G1)
    e4(D1)
    e3r(U1)
    e3(IN)
    e3(MISC)
    e3r(RO)
    e6(G2)
    e6(D2)
    e4(G1)
    e3r(IN)
    e4(RO)
    e5(D1)
    e4(U1)
    e4(MISC)
    e5(G1)
    e4(IN)
    e5(RO)
    e6(D1)
    e5(U1)
    e5(MISC)
    e6(G1)
    e5(IN)
    e6(RO)
    e6(U1)
    e6(MISC)
    e6(IN)
    deliver_wait(yb, y_o, 1, 0)
    deliver_wait(xb, dx_o, 0, 1)
    for copy in swap:
        copy.wait_send()
    for copy in sends + cs_busy:
        copy.wait_send()
    for i in (D2, G2, AO, U2, QKV, G1, U1, D1, RO, IN, MISC):
        e7(i)


def whole_call(tokens, plan, cot, gains, conv, vec, weights):
    vm = pl.BlockSpec(memory_space=pltpu.VMEM)
    hbm = pl.BlockSpec(memory_space=pl.ANY)
    V = pltpu.VMEM
    dma = pltpu.SemaphoreType.DMA
    crs, gots, fins = [], [], []
    for i in range(11):
        n8 = PLAN[i][1] // 8
        crs.append(V((n8, D), BF))
        gots.append(V((3, n8, CC), BF))
        fins.append(V((n8, CC), BF))
    shapes = [
        (2, SEQ, D), (2, SEQ, D), (5, 4 * SEQ, D),
        (6, FQ, D), (640, D), (AQ, D), (1024, D), (RQ, D), (HD, D),
    ]
    return pl.pallas_call(
        whole_kernel,
        name="whole",
        out_shape=[jax.ShapeDtypeStruct(shape, BF) for shape in shapes],
        in_specs=[vm, pl.BlockSpec(memory_space=pltpu.SMEM), vm, vm, vm, vm] + [hbm] * 9,
        out_specs=[hbm] * 9,
        scratch_shapes=[
            V((D, 2 * RQ), BF), V((HD, 2 * RQ), BF), V((2, RQ, HW), BF), V((2, 8, D), F32),
            V((2, D, FQ), BF), V((2, D, FQ), BF), V((2, FQ, D), BF),
            V((D, AQ), BF), V((D, 256), BF), V((2, AQ, HW), BF),
            V((6, SEQ, D), BF), V((2, SEQ, D), BF), V((2, 3, SH, D), BF), V((4, SH, D), F32),
            V((SEQ, D), BF), V((SEQ, D), BF), V((SEQ, 2 * RQ), F32),
            V((SEQ, RQ), F32), V((SEQ, RQ), F32), V((SEQ, RQ), F32), V((SEQ, RQ), F32), V((SEQ, RQ), F32),
            V((SEQ, AQ), BF), V((SEQ, 256), BF), V((3, SEQ, SEQ), F32), V((SEQ, AQ), BF),
            V((2, SEQ, FQ), F32), V((2, SEQ, FQ), F32), V((SEQ, FQ), BF),
            V((SEQ, FQ), BF), V((SEQ, 2 * RQ), BF),
            V((4, SEQ, 256), BF), V((4, 8, D), F32), V((SH, D), BF), V((SH, D), BF), V((8, D), F32),
            V((4 * SEQ, D), BF), V((2, FQ, SEQ), BF), V((RQ, SEQ), BF), V((AQ, SEQ), BF),
            V((2, FQ, SEQ), BF), V((2, FQ, SEQ), BF), V((640, SEQ), BF), V((1024, SEQ), BF), V((HD, D), BF),
            V((FQ, 512), BF), V((RQ, 512), BF), V((AQ, 512), BF),
            V((512, CC), BF), V((512, CC), BF), V((512, CC), BF),
            V((288, 512), BF), V((288, 512), BF), V((288, 512), BF), V((288, 512), BF), V((288, 512), BF),
            V((160, 512), BF), V((256, 512), BF), V((4, 32, D), BF),
            V((144, D), BF), V((2, 144, D), BF),
            *crs, *gots, *fins,
            dma((10,)), dma((10,)), dma((10,)), dma((6, 2, 4)), dma((6, 2, 4)), dma((8, 2, 4)), dma((8, 2, 4)),
            dma((4,)), dma((4,)), dma((4,)), dma((4,)), dma((2, 2)), dma((2, 4, 2)), dma((2, 2, 4, 2)),
            dma((5, 4)), dma((5, 4)), dma((10,)), dma((11, 2, 4)), dma((11, 2, 4)),
            dma((11, 8)), dma((11, 8)), dma((11, 12)), dma((11, 12)), dma((11,)), dma((11,)), dma((11,)),
        ],
        compiler_params=pltpu.CompilerParams(
            collective_id=0, has_side_effects=True, vmem_limit_bytes=63 * 2**20
        ),
    )(tokens, plan, cot, gains, conv, vec, *weights)


def unpack_kernel(
    n_ref, dx, y, ffn, qkv, ao, rin, ro, misc,
    o_bound, o_gain, o_gate, o_up, o_dn, o_in, o_gt, o_conv, o_vec, o_ro, o_q, o_kv, o_ao,
):
    i = pl.program_id(0)
    s = n_ref[0]
    straight = n_ref[1] == 0
    for j in range(2):
        mine = jnp.where(straight, dx[j], dx[1 - j])
        o_bound[0, j * SEQ : j * SEQ + SEQ, :] = jnp.where(s == 0, mine, y[j]).astype(F32)
    o_gate[0] = ffn[0].T.astype(F32)
    o_up[0] = ffn[1].T.astype(F32)
    o_dn[0] = ffn[2].astype(F32)
    part = qkv[...].T.astype(F32)
    o_q[...] = part[:, :AQ]
    o_kv[...] = part[:, AQ:]
    part = rin[...].T.astype(F32)
    o_in[:, 0, :] = part[:, :RQ]
    o_in[:, 1, :] = part[:, RQ:]

    @pl.when(i == 0)
    def _():
        o_ao[...] = ao[...].astype(F32)
        o_ro[...] = ro[...].astype(F32)
        rows = pl.ds(pl.multiple_of(s * 64, 64), 64)
        o_gt[:, 0, :] = misc[rows, :RQ].astype(F32)
        o_gt[:, 1, :] = misc[rows, RQ : 2 * RQ].astype(F32)
        small = misc[:32, 2 * RQ :].astype(F32)

        def pick(at, step):
            return jnp.where(s == 0, small[at : at + step], small[at + step : at + 2 * step])

        o_conv[...] = pick(0, 2)
        o_vec[...] = pick(4, 2)
        gains = pick(8, 6)
        for j in range(2):
            for p in range(3):
                o_gain[0, j : j + 1, p * RQ : p * RQ + RQ] = gains[j * 3 + p : j * 3 + p + 1]


def unpack_call(scalars, dx, y, ffn, qkv, ao, rin, ro, misc):
    n = 3
    wide = D // n
    part = HW // n
    sds = jax.ShapeDtypeStruct
    fixed = lambda *zero: (lambda i, s: zero)
    return pl.pallas_call(
        unpack_kernel,
        name="unpack",
        out_shape=[
            sds((1, 2 * SEQ, D), F32), sds((1, 2, D), F32),
            sds((1, D, FQ), F32), sds((1, D, FQ), F32), sds((1, FQ, D), F32),
            sds((HW, 2, RQ), F32), sds((64, 2, RQ), F32), sds((2, RQ), F32), sds((2, RQ), F32),
            sds((RQ, HW), F32), sds((HW, AQ), F32), sds((HW, 256), F32), sds((AQ, HW), F32),
        ],
        grid_spec=pltpu.PrefetchScalarGridSpec(
            num_scalar_prefetch=1,
            grid=(n,),
            in_specs=[
                pl.BlockSpec((2, SEQ, wide), lambda i, s: (0, 0, i)),
                pl.BlockSpec((2, SEQ, wide), lambda i, s: (0, 0, i)),
                pl.BlockSpec((3, FQ, wide), lambda i, s: (0, 0, i)),
                pl.BlockSpec((640, part), lambda i, s: (0, s[0] * n + i)),
                pl.BlockSpec((AQ, HW), lambda i, s: (0, s[0])),
                pl.BlockSpec((1024, part), lambda i, s: (0, s[0] * n + i)),
                pl.BlockSpec((RQ, HW), lambda i, s: (0, s[0])),
                pl.BlockSpec((HD, D), fixed(0, 0)),
            ],
            out_specs=[
                pl.BlockSpec((1, 2 * SEQ, wide), lambda i, s: (0, 0, i)),
                pl.BlockSpec((1, 2, D), fixed(0, 0, 0)),
                pl.BlockSpec((1, wide, FQ), lambda i, s: (0, i, 0)),
                pl.BlockSpec((1, wide, FQ), lambda i, s: (0, i, 0)),
                pl.BlockSpec((1, FQ, wide), lambda i, s: (0, 0, i)),
                pl.BlockSpec((part, 2, RQ), lambda i, s: (i, 0, 0)),
                pl.BlockSpec((64, 2, RQ), fixed(0, 0, 0)),
                pl.BlockSpec((2, RQ), fixed(0, 0)),
                pl.BlockSpec((2, RQ), fixed(0, 0)),
                pl.BlockSpec((RQ, HW), fixed(0, 0)),
                pl.BlockSpec((part, AQ), lambda i, s: (i, 0)),
                pl.BlockSpec((part, 256), lambda i, s: (i, 0)),
                pl.BlockSpec((AQ, HW), fixed(0, 0)),
            ],
        ),
        compiler_params=pltpu.CompilerParams(vmem_limit_bytes=62 * 2**20),
    )(scalars, dx, y, ffn, qkv, ao, rin, ro, misc)


def per_device(
    tokens, plan_order, cotangent, norm_gains, ffn_gate, ffn_up, ffn_down,
    rec_in, rec_gates, rec_conv, rec_vec, rec_out, att_q, att_kv, att_out,
):
    y, dx, _, ffn, qkv, ao, rin, ro, misc = whole_call(
        tokens, plan_order, cotangent, norm_gains, rec_conv, rec_vec,
        (
            rec_in.reshape(HW, 2 * RQ), rec_gates.reshape(64, 2 * RQ), rec_out,
            ffn_gate, ffn_up, ffn_down, att_q, att_kv, att_out,
        ),
    )
    s = lax.axis_index("section").astype(jnp.int32)
    scalars = jnp.stack([s, plan_order[0, 0]])
    return unpack_call(scalars, dx, y, ffn, qkv, ao, rin, ro, misc)


def solution(mesh):
    placed = (
        P("dp", None),
        P("dp", None),
        P("dp", None),
        P("section", None, None),
        P("section", None, "tensor"),
        P("section", None, "tensor"),
        P("section", "tensor", None),
        P("section", None, "tensor"),
        P("section", None, "tensor"),
        P("section", "tensor"),
        P("section", "tensor"),
        P("tensor", "section"),
        P("section", "tensor"),
        P("section", None),
        P("tensor", "section"),
    )
    return jax.shard_map(
        per_device,
        mesh=mesh,
        in_specs=placed,
        out_specs=(
            P("section", "dp", None),
            P("section", None, None),
            P("section", None, "tensor"),
            P("section", None, "tensor"),
            P("section", "tensor", None),
            P("section", None, "tensor"),
            P("section", None, "tensor"),
            P("section", "tensor"),
            P("section", "tensor"),
            P("tensor", "section"),
            P("section", "tensor"),
            P("section", None),
            P("tensor", "section"),
        ),
        check_vma=False,
    )
```

```python
import jax
import jax.numpy as jnp
from jax import lax
from jax.experimental import pallas as pl
from jax.experimental.pallas import tpu as pltpu
from jax.sharding import PartitionSpec as P

HD = 128
SEQ = 128
NORM_EPS = 1e-06
RATE_FLOOR = 0.01
BF = jnp.bfloat16
F32 = jnp.float32
MESH = pl.DeviceIdType.MESH
NT = (((1,), (1,)), ((), ()))

D = 1536
FQ = 1152
RQ = 512
AQ = 384
SH = 32
CC = 384
HW = 768
X_AXIS = 0
Y_AXIS = 1
G1, U1, D1, G2, U2, D2, QKV, AO, IN, RO, MISC = range(11)
PLAN = {
    G1: ("r", FQ, Y_AXIS),
    U1: ("r", FQ, Y_AXIS),
    D1: ("c", FQ, X_AXIS),
    G2: ("r", FQ, X_AXIS),
    U2: ("r", FQ, X_AXIS),
    D2: ("r", FQ, Y_AXIS),
    QKV: ("r", 640, Y_AXIS),
    AO: ("c", AQ, Y_AXIS),
    IN: ("r", 1024, X_AXIS),
    RO: ("c", RQ, X_AXIS),
    MISC: ("r", HD, Y_AXIS),
}
RING_AXIS = (X_AXIS, Y_AXIS, Y_AXIS, X_AXIS, Y_AXIS)
RN1, RN2, RNA, RN2B, RCOT = range(5)
DIRECT = (U2, QKV, AO, RO, MISC,)
ROOM = {G2: 0, U2: 144, G1: 288, U1: 432, D1: 576, QKV: 720, IN: 800, AO: 928, RO: 976, MISC: 1040}


def mm(left, right):
    return jnp.dot(left, right, preferred_element_type=F32)


def mm_nt(left, right):
    return lax.dot_general(left, right, NT, preferred_element_type=F32)


def rms(values, gain):
    return values * lax.rsqrt(jnp.mean(values * values, -1, keepdims=True) + NORM_EPS) * gain


def rms_back(values, gain, dn):
    r = lax.rsqrt(jnp.mean(values * values, -1, keepdims=True) + NORM_EPS)
    dng = dn * gain
    dv = r * (dng - values * (r * r) * jnp.mean(dng * values, -1, keepdims=True))
    return dv, jnp.sum(dn * values * r, 0, keepdims=True)


GC = 0.7978845608028654
GA = 0.044715


def gelu(x):
    return 0.5 * x * (1.0 + jnp.tanh(GC * (x + GA * x * x * x)))


def gelu_both(x):
    th = jnp.tanh(GC * (x + GA * x * x * x))
    value = 0.5 * x * (1.0 + th)
    slope = 0.5 * (1.0 + th) + 0.5 * x * (1.0 - th * th) * GC * (1.0 + 3.0 * GA * x * x)
    return value, slope


def sigmoid(x):
    return 1.0 / (1.0 + jnp.exp(-x))


def softplus(x):
    return jnp.maximum(x, 0.0) + jnp.log(1.0 + jnp.exp(-jnp.abs(x)))


def rows_back(values, rows, k):
    return jnp.where(rows >= k, pltpu.roll(values, k, 0), 0.0)


def rows_ahead(values, rows, k):
    return jnp.where(rows < SEQ - k, pltpu.roll(values, SEQ - k, 0), 0.0)


class Item:
    pass


def whole_kernel(
    tok_ref, plan_ref, cot_ref, gain_ref, conv_ref, vec_ref,
    win, wgt, wro, wg, wu, wd, wq, wkv, wao,
    n_o, y_o, dx_o, ra, f_ffn, f_qkv, f_ao, f_in, f_ro, f_misc,
    s_in, s_gt, s_ro, s_sm, s_g, s_u, s_d, s_q, s_kv, s_ao,
    ag, sb, rb, res, x_s, n1_s, uv_s, c_s, ig_s, rg_s, a_s, h_s,
    q_s, kv_s, p_s, at_s, gate_s, up_s, hid_s, du_s, both_s,
    dkvb, gnb, yb, xb, smb,
    work, hid_t, o_t, att_t, g_t, u_t, qkv_t, in_t, misc_t,
    la1, la_o, la_a, rc1, rc_o, rc_a, l_g1, l_u1, l_g2, l_u2, l_d2, l_qkv, l_in, l_misc,
    a_d2, cs, raw_in, raw_gt, cot_s, raw_gain, raw_conv, raw_vec, in_sem, *rest,
):
    crs, gots, fins = rest[:11], rest[11:22], rest[22:33]
    (
        wl_sem, ws_sem, wr_sem, ags_sem, agr_sem, rss_sem, rsr_sem,
        kvs_sem, kvr_sem, gns_sem, gnr_sem, dl_sem, dls_sem, dlr_sem,
        rgs_sem, rgr_sem, wk_sem, xs_sem, xr_sem, ys_sem, yr_sem, gs_sem, gr_sem, loc_sem,
        cs_sem, cr_sem,
    ) = rest[33:]
    s = lax.axis_index("section")
    t = lax.axis_index("tensor")
    d = lax.axis_index("dp")
    place = (lax.rem(d, 4), d // 4)
    peers = [lax.rem(t + k, 4) for k in range(4)]
    def own_rows(h):
        return pl.ds(pl.multiple_of(h * 64 + t * 16, 16), 16)

    mine = [own_rows(h) for h in range(2)]

    def half_of(h):
        return pl.ds(pl.multiple_of(h * 64, 64), 64)


    def pos(base, k):
        return lax.rem(base + k, 4)

    def along(axis, k, core):
        if axis == X_AXIS:
            return (core, t, place[1] * 4 + pos(place[0], k))
        return (core, t, pos(place[1], k) * 4 + place[0])

    entry = [
        (win, raw_in), (wgt, raw_gt), (tok_ref, work.at[: 2 * SEQ]), (gain_ref, raw_gain),
        (conv_ref, raw_conv), (vec_ref, raw_vec),
        (cot_ref.at[pl.ds(pl.multiple_of(s * SEQ, SEQ), SEQ)], cot_s),
    ]
    entry = [pltpu.make_async_copy(a, b, in_sem.at[i]) for i, (a, b) in enumerate(entry)]
    for copy in entry:
        copy.start()
    barrier = pltpu.get_barrier_semaphore()
    other = (1 - s, t, d)
    for k in range(1, 4):
        for target in (
            (s, peers[k], d), (1 - s, peers[k], d), along(X_AXIS, k, s), along(Y_AXIS, k, s),
        ):
            pl.semaphore_signal(barrier, inc=1, device_id=target, device_id_type=MESH)
    pl.semaphore_signal(barrier, inc=1, device_id=other, device_id_type=MESH)

    def push(src, dst, send_sem, recv_sem, target):
        return pltpu.make_async_remote_copy(
            src_ref=src, dst_ref=dst, send_sem=send_sem, recv_sem=recv_sem,
            device_id=target, device_id_type=MESH,
        )

    half_in = pl.ds(pl.multiple_of(s * HW, HW), HW)
    half_gt = pl.ds(pl.multiple_of(s * 64, 64), 64)
    moves = [
        (s_in.at[half_in, :], s_in.at[half_in, :]),
        (smb, s_sm.at[s]),
        (s_gt.at[half_gt, :], s_gt.at[half_gt, :]),
        (wro, s_ro.at[s]),
        (wg.at[0], s_g.at[s]),
        (wu.at[0], s_u.at[s]),
        (wd.at[0], s_d.at[s]),
        (wq, s_q.at[half_in, :]),
        (wkv, s_kv.at[half_in, :]),
        (wao, s_ao.at[s]),
    ]
    local = [pltpu.make_async_copy(a, b, wl_sem.at[i]) for i, (a, b) in enumerate(moves)]
    swap = [push(a, b, ws_sem.at[i], wr_sem.at[i], other) for i, (a, b) in enumerate(moves)]
    for copy in local[3:]:
        copy.start()
    entry[0].wait()
    s_in[half_in, :] = raw_in[...].reshape(HW, 2 * RQ)
    entry[1].wait()
    s_gt[half_gt, :] = raw_gt[...].reshape(64, 2 * RQ)
    for copy in entry[3:6]:
        copy.wait()
    smb[...] = jnp.zeros((8, D), F32)
    smb[0:2, :] = raw_gain[0]
    smb[2:4, :RQ] = raw_conv[...].astype(F32)
    smb[2:4, RQ : 2 * RQ] = raw_vec[...].astype(F32)
    s_sm[s] = smb[...]
    entry[2].wait()
    x_s[...] = jnp.where(plan_ref[0, s] == 0, work[:SEQ, :], work[SEQ : 2 * SEQ, :])
    entry[6].wait()
    n_o[0] = s
    n_o[1] = plan_ref[0, 0]
    pl.semaphore_wait(barrier, 13)
    swap[1].start()
    swap[0].start()

    def weights(*which):
        for i in which:
            if i > 2:
                local[i].wait()
            swap[i].wait_recv()


    sub = [slice(0, 16), slice(16, 32)]

    def gather(p, h):
        return [
            push(
                ag.at[p, own_rows(h)], ag.at[p, own_rows(h)], ags_sem.at[p, h, k], agr_sem.at[p, h, k],
                (s, peers[k], d),
            )
            for k in (2, 1, 3)
        ]

    def gather_start(p, h, shard):
        ag[p, mine[h], :] = shard.astype(BF)
        for copy in gather(p, h):
            copy.start()

    def gather_wait(p, h):
        for copy in gather(p, h):
            copy.wait()

    def scatter(p, h):
        return [
            push(
                sb.at[p % 2, pl.ds(pl.multiple_of(h * 64 + peers[k] * 16, 16), 16)],
                rb.at[p % 2, k - 1, pl.ds(pl.multiple_of(h * 16, 16), 16)],
                rss_sem.at[p, h, k], rsr_sem.at[p, h, k], (s, peers[k], d),
            )
            for k in (2, 1, 3)
        ]

    def scatter_start(p, *halves):
        for h in halves:
            for copy in scatter(p, h):
                copy.start()

    def scatter_wait(p, h):
        for copy in scatter(p, h):
            copy.wait()
        total = sb[p % 2, mine[h], :].astype(F32)
        for k in range(3):
            total = total + rb[p % 2, k, h * 16 : h * 16 + 16].astype(F32)
        return total

    def deliver_copy(buf, out, core, which, k, h):
        return push(
            buf.at[sub[h]], out.at[s, mine[h]], dls_sem.at[which, k, h],
            dlr_sem.at[which, s, k, h], (core, peers[k], d),
        )

    def deliver(buf, out, core, which):
        @pl.when(s == core)
        def _():
            own = [
                pltpu.make_async_copy(buf.at[sub[h]], out.at[s, mine[h]], dl_sem.at[which, h])
                for h in range(2)
            ]
            for copy in own:
                copy.start()
            for k in range(1, 4):
                for h in range(2):
                    deliver_copy(buf, out, core, which, k, h).start()
            for copy in own:
                copy.wait()

        @pl.when(s != core)
        def _():
            for k in range(4):
                for h in range(2):
                    deliver_copy(buf, out, core, which, k, h).start()

    def deliver_wait(buf, out, core, which):
        def landed(sender, k, h):
            push(
                buf.at[sub[h]], out.at[sender, mine[h]], dls_sem.at[which, k, h],
                dlr_sem.at[which, sender, k, h], (core, peers[k], d),
            ).wait_recv()

        for h in range(2):

            @pl.when(s == core)
            def _(h=h):
                for k in range(1, 4):
                    deliver_copy(buf, out, core, which, k, h).wait_send()
                    landed(core, k, h)
                for k in range(4):
                    landed(1 - core, k, h)

            @pl.when(s != core)
            def _(h=h):
                for k in range(4):
                    deliver_copy(buf, out, core, which, k, h).wait_send()


    sends = []

    def mult(x, by):
        return pl.multiple_of(x * by, by)

    def slot(place_at):
        return pl.ds(mult(place_at, SEQ), SEQ)

    ring_got = [None] * 5

    def ring_make(g, src):
        axis = RING_AXIS[g]
        here = ra.at[g, slot(place[axis])]
        stay = pltpu.make_async_copy(src, here, wk_sem.at[g])
        copies = [
            push(src, here, rgs_sem.at[g, k], rgr_sem.at[g, k], along(axis, k, s)) for k in (1, 3)
        ]
        sends.extend(copies)
        ring_got[g] = [stay, copies]

    def ring_go(g):
        ring_got[g][0].start()
        for copy in ring_got[g][1]:
            copy.start()

    def ring_start(g, src):
        ring_make(g, src)
        ring_go(g)

    def ring_pass(g):
        axis = RING_AXIS[g]
        copies = []
        for j, (side, back) in enumerate(((1, 3), (3, 1))):
            ring_got[g][1][j].wait_recv()
            rows = ra.at[g, pl.ds(mult(pos(place[axis], back) * 2 + j, 64), 64)]
            copy = push(rows, rows, rgs_sem.at[g, 2 * j], rgr_sem.at[g, 2 * j], along(axis, side, s))
            copy.start()
            copies.append(copy)
        sends.extend(copies)
        ring_got[g][1] = copies

    in_work = [None, None]

    def ring_load(g):
        if in_work[0] == g:
            return
        ring_got[g][0].wait()
        for copy in ring_got[g][1]:
            copy.wait_recv()
        copy = pltpu.make_async_copy(ra.at[g], work, wk_sem.at[5 + g])
        copy.start()
        in_work[0] = g
        in_work[1] = copy

    def ring_use(g):
        ring_load(g)
        if in_work[1] is not None:
            in_work[1].wait()
            in_work[1] = None


    full = {QKV: f_qkv, AO: f_ao, IN: f_in, RO: f_ro, MISC: f_misc}
    owner = {G1: 0, U1: 0, D1: 0, G2: 1, U2: 1, D2: 1}
    items = []
    for i in range(11):
        it = Item()
        it.i = i
        it.style, it.total, it.axis = PLAN[i]
        it.n8 = it.total // 8
        it.m = place[it.axis]
        it.n = place[1 - it.axis]
        it.cr, it.got, it.fin = crs[i], gots[i], fins[i]
        it.acc = a_d2 if i == D2 else s_d.at[1, ROOM[i] : ROOM[i] + it.n8]
        if i in owner:
            it.full = f_ffn.at[(s if owner[i] == 0 else 1 - s) * 3 + i % 3]
            it.home = f_ffn.at[i % 3]
        else:
            it.full = full[i]
            it.home = full[i]
        it.waits = []
        items.append(it)

    def spread(i, which, source, target):
        it = items[i]
        for k in range(1, 4):
            copy = push(
                source(pos(it.m, k)), target(k), xs_sem.at[i, which, k], xr_sem.at[i, which, k],
                along(it.axis, k, s),
            )
            copy.start()
            sends.append(copy)
            it.waits.append(copy)

    def spread_rows(i, whole, into):
        it = items[i]

        def part(f):
            return whole.at[pl.ds(mult(f, 2 * it.n8), 2 * it.n8), :]

        into[:, slot(it.m)] = part(it.m)[...]
        spread(i, 0, part, lambda k: into.at[:, slot(it.m)])

    def spread_left(i, whole, into):
        it = items[i]
        into[:, slot(it.m)] = whole[...]
        spread(i, 0, lambda f: whole, lambda k: into.at[:, slot(it.m)])

    def spread_cols(i, src, into):
        it = items[i]

        def cut(f):
            return pl.ds(mult(f, CC), CC)

        into[slot(it.m), :] = src[:, cut(it.m)]
        spread(i, 1, lambda f: src.at[:, cut(f)], lambda k: into.at[slot(it.m), :])

    def arrived(it):
        for copy in it.waits:
            copy.wait_recv()
        it.waits = []

    def settle(it):
        for copy in it.waits:
            copy.wait()
        it.waits = []

    def piece(it, q):
        return it.acc.at[:, pl.ds(mult(q, CC), CC)]

    cs_busy = [None, None]
    cs_count = [0]

    def halves(i, fill):
        it = items[i]
        at = cs_count[0] % 2
        cs_count[0] += 1
        if cs_busy[at] is not None:
            cs_busy[at].wait_send()
        out = cs.at[at, : it.n8]
        fill(1 - s, out)
        copy = push(out, it.cr, cs_sem.at[i], cr_sem.at[i], other)
        copy.start()
        cs_busy[at] = copy
        it.swap = copy
        fill(s, it.acc)

    def rows_product(i, ring, left):
        it = items[i]
        arrived(it)
        ring_use(ring)

        def fill(h, ref):
            rows = left[pl.ds(mult(h, it.n8), it.n8), :]
            for j in range(4):
                cols = slice(j * CC, j * CC + CC)
                ref[:, cols] = mm(rows, work[:, cols]).astype(BF)

        halves(i, fill)

    def cols_product(i, left, right):
        it = items[i]
        arrived(it)

        def fill(h, ref):
            for q in range(4):
                rows = left[pl.ds(mult(h * 4 + q, it.n8), it.n8), :]
                ref[:, q * CC : q * CC + CC] = mm(rows, right[...]).astype(BF)

        halves(i, fill)

    def misc_sum():
        it = items[MISC]
        arrived(it)

        def fill(h, ref):
            at = pl.ds(mult(h, it.n8), it.n8)
            total = l_misc[0, at, :].astype(F32)
            for k in range(1, 4):
                total = total + l_misc[k, at, :].astype(F32)
            ref[...] = total.astype(BF)

        halves(MISC, fill)

    row_items = {
        G1: (RN2, l_g1), U1: (RN2, l_u1), G2: (RN2B, l_g2), U2: (RN2B, l_u2),
        D2: (RCOT, l_d2), QKV: (RNA, l_qkv), IN: (RN1, l_in),
    }
    col_items = {D1: (la1, rc1), AO: (la_a, rc_a), RO: (la_o, rc_o)}

    def e1(i):
        if i in row_items:
            rows_product(i, *row_items[i])
        elif i in col_items:
            cols_product(i, *col_items[i])
        else:
            misc_sum()

    def cut_of(it):
        return {144: 80, 80: 48, 128: 64, 48: 32, 64: 32}[it.n8]

    def sides(it, at, axis, right, left):
        for j, (side, (src, dst)) in enumerate(((1, right), (3, left))):
            copy = push(src, dst, ys_sem.at[it.i, at + j], yr_sem.at[it.i, at + j], along(axis, side, s))
            copy.start()
            it.waits.append(copy)

    def e2(i):
        it = items[i]
        it.swap.wait_recv()
        it.acc[...] = (it.acc[...].astype(F32) + it.cr[...].astype(F32)).astype(BF)
        if i in DIRECT:
            for k in range(1, 4):
                copy = push(
                    piece(it, pos(it.n, k)), it.got.at[k - 1], ys_sem.at[i, k], yr_sem.at[i, k],
                    along(1 - it.axis, k, s),
                )
                copy.start()
                it.waits.append(copy)
            return
        cut = cut_of(it)
        far = piece(it, pos(it.n, 2))
        sides(
            it, 0, 1 - it.axis, (far.at[:cut], it.got.at[0, :cut]), (far.at[cut:], it.got.at[0, cut:])
        )

    def e2r(i):
        it = items[i]
        if i in DIRECT:
            return
        settle(it)
        cut = cut_of(it)
        right = piece(it, pos(it.n, 1))
        left = piece(it, pos(it.n, 3))
        right[:cut] = (right[:cut].astype(F32) + it.got[0, :cut].astype(F32)).astype(BF)
        left[cut:] = (left[cut:].astype(F32) + it.got[0, cut:].astype(F32)).astype(BF)
        sides(it, 2, 1 - it.axis, (right, it.got.at[1]), (left, it.got.at[2]))

    def rect(it, ref, f, q, lo=0, n=None):
        block, at = (f * 2 + s, q) if it.style == "r" else (s * 4 + q, f)
        rows = pl.ds(pl.multiple_of(block * it.n8 + lo, 16), n or it.n8)
        return ref.at[rows, pl.ds(mult(at, CC), CC)]

    def quarter(it, ref, f, part=None):
        if it.style == "r":
            rows = pl.ds(mult(f * 2 + s, it.n8), it.n8)
            if part is None:
                return ref.at[rows, :]
            return ref.at[rows, part * HW : part * HW + HW]
        cols = pl.ds(mult(f, CC), CC)
        if part is None:
            return ref.at[pl.ds(mult(s, 4 * it.n8), 4 * it.n8), cols]
        return ref.at[pl.ds(mult(s * 2 + part, 2 * it.n8), 2 * it.n8), cols]

    def e3(i):
        it = items[i]
        settle(it)
        total = piece(it, it.n)[...].astype(F32)
        for k in range(3) if i in DIRECT else (1, 2):
            total = total + it.got[k].astype(F32)
        it.fin[...] = total.astype(BF)
        spot = rect(it, it.full, it.m, it.n)
        own = pltpu.make_async_copy(it.fin, spot, loc_sem.at[i])
        own.start()
        it.waits.append(own)
        if i in DIRECT:
            for k in range(1, 4):
                copy = push(
                    it.fin, spot, gs_sem.at[i, k], gr_sem.at[i, k], along(1 - it.axis, k, s)
                )
                copy.start()
                it.waits.append(copy)
            return
        sides(it, 4, 1 - it.axis, (it.fin, spot), (it.fin, spot))

    def e3r(i):
        it = items[i]
        if i in DIRECT:
            return
        settle(it)
        cut = cut_of(it)
        left = rect(it, it.full, it.m, pos(it.n, 3), 0, cut)
        right = rect(it, it.full, it.m, pos(it.n, 1), cut, it.n8 - cut)
        sides(it, 6, 1 - it.axis, (left, left), (right, right))

    def both_ways(it, at, right, left):
        for side, part in ((1, right), (3, left)):
            copy = push(
                part, part, gs_sem.at[it.i, at + side // 2], gr_sem.at[it.i, at + side // 2],
                along(it.axis, side, s),
            )
            copy.start()
            it.waits.append(copy)

    def to_other(it, ks):
        whole_c = it.style == "c" and it.i not in owner
        copies = []
        for k in ks:
            f = pos(it.m, k)
            if whole_c:
                if k != 2:
                    continue
                rows = pl.ds(mult(s, 4 * it.n8), 4 * it.n8)
            elif it.style == "c":
                rows = pl.ds(mult(s, 4 * it.n8), 4 * it.n8)
            else:
                rows = pl.ds(mult(f * 2 + s, it.n8), it.n8)
            cols = pl.ds(0, D)
            if it.i in (QKV, AO, IN, RO):
                cols = pl.ds(mult(1 - s, HW), HW)
            elif it.style == "c":
                cols = pl.ds(mult(f, CC), CC)
            copies.append(
                push(
                    it.full.at[rows, cols], it.home.at[rows, cols],
                    gs_sem.at[it.i, 8 + k], gr_sem.at[it.i, 8 + k], other,
                )
            )
        return copies

    def home(it, *ks):
        if it.i in owner:

            @pl.when(s != owner[it.i])
            def _():
                for copy in to_other(it, ks):
                    copy.start()
        else:
            for copy in to_other(it, ks):
                copy.start()

    def e4(i):
        it = items[i]
        settle(it)
        part = quarter(it, it.full, it.m)
        both_ways(it, 4, part, part)
        home(it, 0)

    def e5(i):
        it = items[i]
        settle(it)
        both_ways(
            it, 6, quarter(it, it.full, pos(it.m, 3), 0), quarter(it, it.full, pos(it.m, 1), 1)
        )
        home(it, 3, 1)

    def e6(i):
        it = items[i]
        settle(it)
        home(it, 2)

    def e7(i):
        it = items[i]
        if i in owner:

            @pl.when(s != owner[i])
            def _():
                for copy in to_other(it, range(4)):
                    copy.wait_send()

            @pl.when(s == owner[i])
            def _():
                for copy in to_other(it, range(4)):
                    copy.wait_recv()
        else:
            for copy in to_other(it, range(4)):
                copy.wait()

    def gain(block, which):
        return s_sm[block, which : which + 1, :]

    rows = lax.broadcasted_iota(jnp.int32, (SEQ, RQ), 0)

    ring_start(RCOT, cot_s)
    weights(1)
    n1_s[...] = rms(x_s[...].astype(F32), gain(0, 0)).astype(BF)
    for copy in swap[2:]:
        copy.start()
    ring_start(RN1, n1_s)
    uv_s[...] = mm(n1_s[:, half_in], s_in[half_in, :])
    weights(0)
    half_other = pl.ds(mult(1 - s, HW), HW)
    uv_s[...] += mm(n1_s[:, half_other], s_in[half_other, :])
    taps = [s_sm[k // 2, 2 + k % 2 : 3 + k % 2, :RQ] for k in range(4)]
    vec = [s_sm[k // 2, 2 + k % 2 : 3 + k % 2, RQ : 2 * RQ] for k in range(4)]
    u = uv_s[:, :RQ]
    c = vec[0] + taps[0] * u
    for k in range(1, 4):
        c = c + taps[k] * rows_back(u, rows, k)
    c_s[...] = c
    weights(2, 3)
    for head in range(4):
        cols = slice(head * HD, head * HD + HD)
        cb = c_s[:, cols].astype(BF)
        ig_s[:, cols] = sigmoid(mm(cb, s_gt[:, cols]) + vec[1][:, cols])
        rg_s[:, cols] = sigmoid(
            mm(cb, s_gt[:, RQ + head * HD : RQ + head * HD + HD]) + vec[2][:, cols]
        )
    speed = softplus(vec[3])
    a = jnp.exp(-8.0 * rg_s[...] * speed)
    a_s[...] = a
    run = jnp.sqrt(jnp.maximum(1.0 - a * a, RATE_FLOOR)) * ig_s[...] * c_s[...]
    step = 1
    while step < SEQ:
        run = run + a * rows_back(run, rows, step)
        if 2 * step < SEQ:
            a = a * jnp.where(rows >= step, pltpu.roll(a, step, 0), 1.0)
        step *= 2
    h_s[...] = run
    o = (run * gelu(uv_s[:, RQ:])).astype(BF)
    for half in range(2):
        sb[0, :, half * HW : half * HW + HW] = mm(o, s_ro[half]).astype(BF)
    scatter_start(0, 0, 1)
    o_t[...] = o.T
    spread_left(RO, o_t, la_o)
    for h in range(2):
        x1 = x_s[mine[h], :].astype(F32) + scatter_wait(0, h)
        res[0, sub[h]] = x1
        gather_start(0, h, rms(x1, gain(0, 1)))

    def ffn_forward(block, p_in, p_out, ring):
        ring_make(ring, ag.at[p_in])

        def one(h, carry):
            gather_wait(p_in, h)
            half = half_of(h)
            n2 = ag[p_in, half, :]

            @pl.when(h == 1)
            def _():
                ring_go(ring)

            for j in range(3):
                cols = slice(j * CC, j * CC + CC)
                gate = mm(n2, s_g[block, :, cols])
                up = mm(n2, s_u[block, :, cols])
                gate_s[block, half, cols] = gate
                up_s[block, half, cols] = up
                hid_s[half, cols] = (gelu(gate) * up).astype(BF)
            if block == 0:

                @pl.when(h == 0)
                def _():
                    weights(6)

            hid = hid_s[half, :]
            for j in range(4):
                cols = slice(j * CC, j * CC + CC)
                sb[p_out % 2, half, cols] = mm(hid, s_d[block, :, cols]).astype(BF)
            scatter_start(p_out, h)
            return carry

        lax.fori_loop(0, 2, one, 0)
        hid_t[block] = hid_s[...].T

    weights(4, 5)
    ffn_forward(0, 0, 1, RN2)
    spread_left(D1, hid_t.at[0], la1)
    ring_pass(RCOT)
    ring_pass(RN1)
    for h in range(2):
        mid = (res[0, sub[h]] + scatter_wait(1, h)).astype(BF).astype(F32)
        res[1, sub[h]] = mid
        gather_start(1, h, rms(mid, gain(1, 0)))
    weights(7, 8, 9)

    p_s[:, :64, 64:] = jnp.zeros((3, 64, 64), F32)
    for h in range(2):
        gather_wait(1, h)
        if h == 1:
            ring_start(RNA, ag.at[1])
        half = slice(h * 64, h * 64 + 64)
        n = 64 * h + 64
        na = ag[1, half]
        q_s[half] = mm(na, s_q[...]).astype(BF)
        kv_s[half] = mm(na, s_kv[...]).astype(BF)
        keys = kv_s[:n, :HD]
        vals = kv_s[:n, HD:]
        col = lax.broadcasted_iota(jnp.int32, (64, n), 1)
        row = lax.broadcasted_iota(jnp.int32, (64, n), 0) + 64 * h
        for head in range(3):
            cols = slice(head * HD, head * HD + HD)
            score = jnp.where(col <= row, mm_nt(q_s[half, cols], keys) * HD ** (-0.5), -1e30)
            expo = jnp.exp(score - jnp.max(score, -1, keepdims=True))
            p = expo / jnp.sum(expo, -1, keepdims=True)
            p_s[head, half, :n] = p
            at_s[half, cols] = mm(p.astype(BF), vals).astype(BF)
        for c in range(2):
            sb[0, half, c * HW : c * HW + HW] = mm(at_s[half], s_ao[c]).astype(BF)
        scatter_start(2, h)
    att = at_s[...]
    att_t[...] = att.T
    spread_left(AO, att_t, la_a)
    ring_pass(RN2)
    for h in range(2):
        x1 = res[1, sub[h]] + scatter_wait(2, h)
        res[2, sub[h]] = x1
        gather_start(2, h, rms(x1, gain(1, 1)))
    ffn_forward(1, 2, 3, RN2B)
    spread_rows(D2, hid_t.at[1], l_d2)
    ring_load(RCOT)

    def ffn_back_rows(block, half, dF, p_out):
        for j in range(3):
            cols = slice(j * CC, j * CC + CC)
            dhid = mm_nt(dF, s_d[block, cols, :])
            value, slope = gelu_both(gate_s[block, half, cols])
            hid_s[half, cols] = (dhid * up_s[block, half, cols] * slope).astype(BF)
            du_s[half, cols] = (dhid * value).astype(BF)
        dg = hid_s[half, :]
        du = du_s[half, :]
        for j in range(4):
            cols = slice(j * CC, j * CC + CC)
            sb[p_out % 2, half, cols] = (
                mm_nt(dg, s_g[block, cols, :]) + mm_nt(du, s_u[block, cols, :])
            ).astype(BF)

    def ffn_back_send(block):
        g_t[block] = hid_s[...].T
        spread_rows(G2 if block else G1, g_t.at[block], l_g2 if block else l_g1)
        u_t[block] = du_s[...].T
        spread_rows(U2 if block else U1, u_t.at[block], l_u2 if block else l_u1)

    ffn_back_rows(1, pl.ds(0, SEQ), cot_s[...], 4)
    scatter_start(4, 0, 1)
    ffn_back_send(1)
    for h in range(2):
        yb[sub[h], :] = (res[2, sub[h]] + scatter_wait(3, h)).astype(BF)
    ring_pass(RNA)
    ring_pass(RN2B)
    e1(D2)
    gg11 = []
    for h in range(2):
        dv, gg = rms_back(res[2, sub[h]], gain(1, 1), scatter_wait(4, h))
        gg11.append(gg)
        dx1 = cot_s[mine[h], :].astype(F32) + dv
        res[3, sub[h]] = dx1
        gather_start(3, h, dx1)
    e2(D2)

    gather_wait(3, 0)
    gather_wait(3, 1)
    spread_cols(AO, ag.at[3], rc_a)
    dA = ag[3]
    datt_s = both_s.at[:, :AQ]
    dq_s = both_s.at[:, AQ : 2 * AQ]
    datt_s[...] = (mm_nt(dA[:, :HW], s_ao[0]) + mm_nt(dA[:, HW:], s_ao[1])).astype(BF)
    dk = jnp.zeros((SEQ, HD), F32)
    dw = jnp.zeros((SEQ, HD), F32)
    for head in range(3):
        cols = slice(head * HD, head * HD + HD)
        p = p_s[head]
        datt = datt_s[:, cols]
        dpr = mm_nt(datt, kv_s[:, HD:])
        dw = dw + mm(p.astype(BF).T, datt)
        ds = (p * (dpr - jnp.sum(p * dpr, -1, keepdims=True)) * HD ** (-0.5)).astype(BF)
        dq_s[:, cols] = mm(ds, kv_s[:, :HD]).astype(BF)
        dk = dk + mm(ds.T, q_s[:, cols])
    dkvb[0, :, :HD] = dk.astype(BF)
    dkvb[0, :, HD:] = dw.astype(BF)
    kv_copies = [
        push(dkvb.at[0], dkvb.at[k], kvs_sem.at[k], kvr_sem.at[k], (s, peers[k], d))
        for k in range(1, 4)
    ]
    for copy in kv_copies:
        copy.start()
    dq = dq_s[...]
    for j in range(4):
        cols = slice(j * CC, j * CC + CC)
        sb[1, :, cols] = mm_nt(dq, s_q[cols, :]).astype(BF)
    scatter_start(5, 0, 1)
    e1(G2)
    e2r(D2)
    e1(U2)
    ring_load(RNA)
    for copy in kv_copies:
        copy.wait()
    total = dkvb[0].astype(F32)
    for k in range(1, 4):
        total = total + dkvb[k].astype(F32)
    dkv_s = both_s.at[:, 2 * AQ : 2 * AQ + 256]
    dkv_s[...] = total.astype(BF)
    qkv_t[:AQ] = dq_s[...].T
    qkv_t[AQ:] = dkv_s[...].T
    spread_rows(QKV, qkv_t, l_qkv)
    e1(AO)
    e2(G2)
    gg10 = []
    for h in range(2):
        dn = scatter_wait(5, h) + mm_nt(dkv_s[mine[h], :], s_kv[...])
        dv, gg = rms_back(res[1, sub[h]], gain(1, 0), dn)
        gg10.append(gg)
        big_g = (res[3, sub[h]] + dv).astype(BF)
        gather_start(4, h, big_g)
        res[3, sub[h]] = big_g.astype(F32)
    e2(U2)
    e2(AO)
    e3(D2)
    e1(QKV)
    ring_load(RN2)
    e2r(G2)

    it = items[D1]
    cols_at = [pl.ds(mult(pos(it.m, k), CC), CC) for k in range(4)]
    d1_copies = [
        push(
            ag.at[4, :, cols_at[k]], rc1.at[slot(it.m), :], xs_sem.at[D1, 1, k], xr_sem.at[D1, 1, k],
            along(it.axis, k, s),
        )
        for k in range(1, 4)
    ]
    d1_rows = slot(it.m)

    def back_half(h, carry):
        gather_wait(4, h)

        @pl.when(h == 1)
        def _():
            rc1[d1_rows, :] = ag[4, :, cols_at[0]]
            for copy in d1_copies:
                copy.start()

        ffn_back_rows(0, half_of(h), ag[4, half_of(h), :], 6)
        scatter_start(6, h)
        return carry

    lax.fori_loop(0, 2, back_half, 0)
    it.waits += d1_copies
    sends.extend(d1_copies)
    ffn_back_send(0)
    e3(U2)
    e3(G2)
    e3(AO)
    e2(QKV)
    e3r(D2)
    gg01 = []
    for h in range(2):
        dv, gg = rms_back(res[0, sub[h]], gain(0, 1), scatter_wait(6, h))
        gg01.append(gg)
        dx1 = res[3, sub[h]] + dv
        res[3, sub[h]] = dx1
        gather_start(5, h, dx1)
    e1(D1)
    e1(G1)
    e3(QKV)
    e4(AO)
    e2(D1)
    e4(D2)
    e1(U1)
    ring_load(RN1)

    gather_wait(5, 0)
    gather_wait(5, 1)
    spread_cols(RO, ag.at[5], rc_o)
    dA = ag[5]
    dO = mm_nt(dA[:, :HW], s_ro[0]) + mm_nt(dA[:, HW:], s_ro[1])
    value, slope = gelu_both(uv_s[:, RQ:])
    h = h_s[...]
    both_s[:, RQ:] = (dO * h * slope).astype(BF)
    e = dO * value
    a = a_s[...]
    coef = rows_ahead(a, rows, 1)
    step = 1
    while step < SEQ:
        e = e + coef * rows_ahead(e, rows, step)
        if 2 * step < SEQ:
            coef = coef * rows_ahead(coef, rows, step)
        step *= 2
    ig = ig_s[...]
    rg = rg_s[...]
    c = c_s[...]
    room = 1.0 - a * a
    m = jnp.sqrt(jnp.maximum(room, RATE_FLOOR))
    ga = e * rows_back(h, rows, 1) - jnp.where(room > RATE_FLOOR, e * ig * c * a / m, 0.0)
    dl = ga * a
    gv3 = jnp.sum(dl * rg, 0, keepdims=True) * (-8.0) * sigmoid(vec[3])
    er = -8.0 * dl * speed * rg * (1.0 - rg)
    ei = e * m * c * ig * (1.0 - ig)
    gv1 = jnp.sum(ei, 0, keepdims=True)
    gv2 = jnp.sum(er, 0, keepdims=True)
    c_s[...] = e * m * ig
    ig_s[...] = ei
    rg_s[...] = er
    for head in range(4):
        cols = slice(head * HD, head * HD + HD)
        late = slice(RQ + head * HD, RQ + head * HD + HD)
        dpin = ig_s[:, cols].astype(BF)
        dprec = rg_s[:, cols].astype(BF)
        cbt = c[:, cols].astype(BF).T
        misc_t[:, cols] = mm(cbt, dpin).astype(BF)
        misc_t[:, late] = mm(cbt, dprec).astype(BF)
        c_s[:, cols] += mm_nt(dpin, s_gt[:, cols]) + mm_nt(dprec, s_gt[:, late])
    dc = c_s[...]
    u = uv_s[:, :RQ]
    du = taps[0] * dc
    gtap = [jnp.sum(u * dc, 0, keepdims=True)]
    for k in range(1, 4):
        du = du + taps[k] * rows_ahead(dc, rows, k)
        gtap.append(jnp.sum(rows_back(u, rows, k) * dc, 0, keepdims=True))
    gv0 = jnp.sum(dc, 0, keepdims=True)
    both_s[:, :RQ] = du.astype(BF)
    both = both_s[...]
    for j in range(4):
        cols = slice(j * CC, j * CC + CC)
        sb[1, :, cols] = mm_nt(both, s_in[cols, :]).astype(BF)
    scatter_start(7, 0, 1)
    in_t[...] = both.T
    spread_rows(IN, in_t, l_in)
    e2(G1)
    e2(U1)
    e4(U2)
    e3r(G2)
    e1(RO)
    gg00 = []
    for h in range(2):
        dv, gg = rms_back(x_s[mine[h], :].astype(F32), gain(0, 0), scatter_wait(7, h))
        gg00.append(gg)
        xb[sub[h], :] = (res[3, sub[h]] + dv).astype(BF)
    deliver(xb, dx_o, 0, 1)
    gnb[0, 0:1] = gg00[0] + gg00[1]
    gnb[0, 1:2] = gg01[0] + gg01[1]
    gnb[0, 2:3] = gg10[0] + gg10[1]
    gnb[0, 3:4] = gg11[0] + gg11[1]
    gnb[0, 4:8] = jnp.zeros((4, D), F32)
    gn_copies = [
        push(gnb.at[0], gnb.at[k], gns_sem.at[k], gnr_sem.at[k], (s, peers[k], d))
        for k in range(1, 4)
    ]
    for copy in gn_copies:
        copy.start()
    e2(RO)
    e1(IN)
    e2r(U1)
    e2r(G1)
    e2r(D1)
    e5(AO)
    e2(IN)
    deliver(yb, y_o, 1, 0)
    for copy in gn_copies:
        copy.wait()
    gains = gnb[0] + gnb[1] + gnb[2] + gnb[3]
    small = gtap + [gv0, gv1, gv2, gv3]
    for g in range(4):
        for part in range(3):
            small.append(gains[g : g + 1, part * RQ : part * RQ + RQ])
    small.append(jnp.zeros((HD - len(small), RQ), F32))
    misc_t[:, 2 * RQ :] = jnp.concatenate(small, 0).astype(BF)
    it = items[MISC]

    def misc_rows(f):
        return misc_t.at[pl.ds(mult(f, 32), 32), :]

    l_misc[0] = misc_rows(it.m)[...]
    spread(MISC, 0, misc_rows, lambda k: l_misc.at[k])
    e4(QKV)
    e5(D2)
    e5(U2)
    e4(G2)
    e3(RO)
    e3(U1)
    e3(D1)
    e3(G1)
    e6(AO)
    e2r(IN)
    e6(U2)
    e1(MISC)
    e2(MISC)
    e5(QKV)
    e5(G2)
    e3r(U1)
    e6(D2)
    e4(RO)
    e3r(G1)
    e3(MISC)
    e3r(D1)
    e3(IN)
    e6(G2)
    e4(U1)
    e6(QKV)
    e4(D1)
    e3r(IN)
    e5(RO)
    e4(G1)
    e4(MISC)
    e5(U1)
    e4(IN)
    e5(D1)
    e6(RO)
    e5(G1)
    e5(MISC)
    e5(IN)
    e6(U1)
    e6(D1)
    e6(G1)
    e6(IN)
    e6(MISC)
    deliver_wait(yb, y_o, 1, 0)
    deliver_wait(xb, dx_o, 0, 1)
    for copy in swap:
        copy.wait_send()
    for copy in sends + cs_busy:
        copy.wait_send()
    for i in (D2, G2, AO, U2, QKV, G1, U1, D1, RO, IN, MISC):
        e7(i)


def whole_call(tokens, plan, cot, gains, conv, vec, weights):
    sm = pl.BlockSpec(memory_space=pltpu.SMEM)
    hbm = pl.BlockSpec(memory_space=pl.ANY)
    V = pltpu.VMEM
    dma = pltpu.SemaphoreType.DMA
    crs, gots, fins = [], [], []
    for i in range(11):
        n8 = PLAN[i][1] // 8
        crs.append(V((n8, D), BF))
        gots.append(V((3, n8, CC), BF))
        fins.append(V((n8, CC), BF))
    shapes = [
        (2, SEQ, D), (2, SEQ, D), (5, 4 * SEQ, D),
        (6, FQ, D), (640, D), (AQ, D), (1024, D), (RQ, D), (HD, D),
    ]
    return pl.pallas_call(
        whole_kernel,
        name="whole",
        out_shape=[jax.ShapeDtypeStruct((2,), jnp.int32)]
        + [jax.ShapeDtypeStruct(shape, BF) for shape in shapes],
        in_specs=[hbm, sm] + [hbm] * 13,
        out_specs=[sm] + [hbm] * 9,
        scratch_shapes=[
            V((D, 2 * RQ), BF), V((HD, 2 * RQ), BF), V((2, RQ, HW), BF), V((2, 8, D), F32),
            V((2, D, FQ), BF), V((2, D, FQ), BF), V((2, FQ, D), BF),
            V((D, AQ), BF), V((D, 256), BF), V((2, AQ, HW), BF),
            V((6, SEQ, D), BF), V((2, SEQ, D), BF), V((2, 3, SH, D), BF), V((4, SH, D), F32),
            V((SEQ, D), BF), V((SEQ, D), BF), V((SEQ, 2 * RQ), F32),
            V((SEQ, RQ), F32), V((SEQ, RQ), F32), V((SEQ, RQ), F32), V((SEQ, RQ), F32), V((SEQ, RQ), F32),
            V((SEQ, AQ), BF), V((SEQ, 256), BF), V((3, SEQ, SEQ), F32), V((SEQ, AQ), BF),
            V((2, SEQ, FQ), F32), V((2, SEQ, FQ), F32), V((SEQ, FQ), BF),
            V((SEQ, FQ), BF), V((SEQ, 2 * RQ), BF),
            V((4, SEQ, 256), BF), V((4, 8, D), F32), V((SH, D), BF), V((SH, D), BF), V((8, D), F32),
            V((4 * SEQ, D), BF), V((2, FQ, SEQ), BF), V((RQ, SEQ), BF), V((AQ, SEQ), BF),
            V((2, FQ, SEQ), BF), V((2, FQ, SEQ), BF), V((640, SEQ), BF), V((1024, SEQ), BF), V((HD, D), BF),
            V((FQ, 512), BF), V((RQ, 512), BF), V((AQ, 512), BF),
            V((512, CC), BF), V((512, CC), BF), V((512, CC), BF),
            V((288, 512), BF), V((288, 512), BF), V((288, 512), BF), V((288, 512), BF), V((288, 512), BF),
            V((160, 512), BF), V((256, 512), BF), V((4, 32, D), BF),
            V((144, D), BF), V((2, 144, D), BF),
            V((HW, 2, RQ), BF), V((64, 2, RQ), BF), V((SEQ, D), BF),
            V((1, 2, D), F32), V((2, RQ), BF), V((2, RQ), BF), dma((7,)),
            *crs, *gots, *fins,
            dma((10,)), dma((10,)), dma((10,)), dma((6, 2, 4)), dma((6, 2, 4)), dma((8, 2, 4)), dma((8, 2, 4)),
            dma((4,)), dma((4,)), dma((4,)), dma((4,)), dma((2, 2)), dma((2, 4, 2)), dma((2, 2, 4, 2)),
            dma((5, 4)), dma((5, 4)), dma((10,)), dma((11, 2, 4)), dma((11, 2, 4)),
            dma((11, 8)), dma((11, 8)), dma((11, 12)), dma((11, 12)), dma((11,)), dma((11,)), dma((11,)),
        ],
        compiler_params=pltpu.CompilerParams(
            collective_id=0, has_side_effects=True, vmem_limit_bytes=64 * 2**20 - 2**17
        ),
    )(tokens, plan, cot, gains, conv, vec, *weights)


def unpack_kernel(
    n_ref, dx, y, ffn, qkv, ao, rin, ro, misc,
    o_bound, o_gain, o_gate, o_up, o_dn, o_in, o_gt, o_conv, o_vec, o_ro, o_q, o_kv, o_ao,
):
    i = pl.program_id(0)
    s = n_ref[0]
    straight = n_ref[1] == 0
    for j in range(2):
        mine = jnp.where(straight, dx[j], dx[1 - j])
        o_bound[0, j * SEQ : j * SEQ + SEQ, :] = jnp.where(s == 0, mine, y[j]).astype(F32)
    o_gate[0] = ffn[0].T.astype(F32)
    o_up[0] = ffn[1].T.astype(F32)
    o_dn[0] = ffn[2].astype(F32)
    part = qkv[...].T.astype(F32)
    o_q[...] = part[:, :AQ]
    o_kv[...] = part[:, AQ:]
    part = rin[...].T.astype(F32)
    o_in[:, 0, :] = part[:, :RQ]
    o_in[:, 1, :] = part[:, RQ:]

    @pl.when(i == 0)
    def _():
        o_ao[...] = ao[...].astype(F32)
        o_ro[...] = ro[...].astype(F32)
        rows = pl.ds(pl.multiple_of(s * 64, 64), 64)
        o_gt[:, 0, :] = misc[rows, :RQ].astype(F32)
        o_gt[:, 1, :] = misc[rows, RQ : 2 * RQ].astype(F32)
        small = misc[:32, 2 * RQ :].astype(F32)

        def pick(at, step):
            return jnp.where(s == 0, small[at : at + step], small[at + step : at + 2 * step])

        o_conv[...] = pick(0, 2)
        o_vec[...] = pick(4, 2)
        gains = pick(8, 6)
        for j in range(2):
            for p in range(3):
                o_gain[0, j : j + 1, p * RQ : p * RQ + RQ] = gains[j * 3 + p : j * 3 + p + 1]


def unpack_call(scalars, dx, y, ffn, qkv, ao, rin, ro, misc):
    n = 3
    wide = D // n
    part = HW // n
    sds = jax.ShapeDtypeStruct
    fixed = lambda *zero: (lambda i, s: zero)
    return pl.pallas_call(
        unpack_kernel,
        name="unpack",
        out_shape=[
            sds((1, 2 * SEQ, D), F32), sds((1, 2, D), F32),
            sds((1, D, FQ), F32), sds((1, D, FQ), F32), sds((1, FQ, D), F32),
            sds((HW, 2, RQ), F32), sds((64, 2, RQ), F32), sds((2, RQ), F32), sds((2, RQ), F32),
            sds((RQ, HW), F32), sds((HW, AQ), F32), sds((HW, 256), F32), sds((AQ, HW), F32),
        ],
        grid_spec=pltpu.PrefetchScalarGridSpec(
            num_scalar_prefetch=1,
            grid=(n,),
            in_specs=[
                pl.BlockSpec((2, SEQ, wide), lambda i, s: (0, 0, i)),
                pl.BlockSpec((2, SEQ, wide), lambda i, s: (0, 0, i)),
                pl.BlockSpec((3, FQ, wide), lambda i, s: (0, 0, i)),
                pl.BlockSpec((640, part), lambda i, s: (0, s[0] * n + i)),
                pl.BlockSpec((AQ, HW), lambda i, s: (0, s[0])),
                pl.BlockSpec((1024, part), lambda i, s: (0, s[0] * n + i)),
                pl.BlockSpec((RQ, HW), lambda i, s: (0, s[0])),
                pl.BlockSpec((HD, D), fixed(0, 0)),
            ],
            out_specs=[
                pl.BlockSpec((1, 2 * SEQ, wide), lambda i, s: (0, 0, i)),
                pl.BlockSpec((1, 2, D), fixed(0, 0, 0)),
                pl.BlockSpec((1, wide, FQ), lambda i, s: (0, i, 0)),
                pl.BlockSpec((1, wide, FQ), lambda i, s: (0, i, 0)),
                pl.BlockSpec((1, FQ, wide), lambda i, s: (0, 0, i)),
                pl.BlockSpec((part, 2, RQ), lambda i, s: (i, 0, 0)),
                pl.BlockSpec((64, 2, RQ), fixed(0, 0, 0)),
                pl.BlockSpec((2, RQ), fixed(0, 0)),
                pl.BlockSpec((2, RQ), fixed(0, 0)),
                pl.BlockSpec((RQ, HW), fixed(0, 0)),
                pl.BlockSpec((part, AQ), lambda i, s: (i, 0)),
                pl.BlockSpec((part, 256), lambda i, s: (i, 0)),
                pl.BlockSpec((AQ, HW), fixed(0, 0)),
            ],
        ),
        compiler_params=pltpu.CompilerParams(vmem_limit_bytes=62 * 2**20),
    )(scalars, dx, y, ffn, qkv, ao, rin, ro, misc)


def per_device(
    tokens, plan_order, cotangent, norm_gains, ffn_gate, ffn_up, ffn_down,
    rec_in, rec_gates, rec_conv, rec_vec, rec_out, att_q, att_kv, att_out,
):
    scalars, y, dx, _, ffn, qkv, ao, rin, ro, misc = whole_call(
        tokens, plan_order, cotangent, norm_gains, rec_conv, rec_vec,
        (
            rec_in, rec_gates, rec_out,
            ffn_gate, ffn_up, ffn_down, att_q, att_kv, att_out,
        ),
    )
    return unpack_call(scalars, dx, y, ffn, qkv, ao, rin, ro, misc)


def solution(mesh):
    placed = (
        P("dp", None),
        P("dp", None),
        P("dp", None),
        P("section", None, None),
        P("section", None, "tensor"),
        P("section", None, "tensor"),
        P("section", "tensor", None),
        P("section", None, "tensor"),
        P("section", None, "tensor"),
        P("section", "tensor"),
        P("section", "tensor"),
        P("tensor", "section"),
        P("section", "tensor"),
        P("section", None),
        P("tensor", "section"),
    )
    return jax.shard_map(
        per_device,
        mesh=mesh,
        in_specs=placed,
        out_specs=(
            P("section", "dp", None),
            P("section", None, None),
            P("section", None, "tensor"),
            P("section", None, "tensor"),
            P("section", "tensor", None),
            P("section", None, "tensor"),
            P("section", None, "tensor"),
            P("section", "tensor"),
            P("section", "tensor"),
            P("tensor", "section"),
            P("section", "tensor"),
            P("section", None),
            P("tensor", "section"),
        ),
        check_vma=False,
    )
```

```python
import jax
import jax.numpy as jnp
from jax import lax
from jax.experimental import pallas as pl
from jax.experimental.pallas import tpu as pltpu
from jax.sharding import PartitionSpec as P

HD = 128
SEQ = 128
NORM_EPS = 1e-06
RATE_FLOOR = 0.01
BF = jnp.bfloat16
F32 = jnp.float32
MESH = pl.DeviceIdType.MESH
NT = (((1,), (1,)), ((), ()))

D = 1536
FQ = 1152
RQ = 512
AQ = 384
SH = 32
CC = 384
HW = 768
X_AXIS = 0
Y_AXIS = 1
G1, U1, D1, G2, U2, D2, QKV, AO, IN, RO, MISC = range(11)
PLAN = {
    G1: ("r", FQ, Y_AXIS),
    U1: ("r", FQ, Y_AXIS),
    D1: ("c", FQ, X_AXIS),
    G2: ("r", FQ, X_AXIS),
    U2: ("r", FQ, X_AXIS),
    D2: ("r", FQ, Y_AXIS),
    QKV: ("r", 640, Y_AXIS),
    AO: ("c", AQ, Y_AXIS),
    IN: ("r", 1024, X_AXIS),
    RO: ("c", RQ, X_AXIS),
    MISC: ("r", HD, Y_AXIS),
}
RING_AXIS = (X_AXIS, Y_AXIS, Y_AXIS, X_AXIS, Y_AXIS)
RN1, RN2, RNA, RN2B, RCOT = range(5)
DIRECT = (U2, QKV, AO, RO, MISC,)
ROOM = {G2: 0, U2: 144, G1: 288, U1: 432, D1: 576, QKV: 720, IN: 800, AO: 928, RO: 976, MISC: 1040}


def mm(left, right):
    return jnp.dot(left, right, preferred_element_type=F32)


def mm_nt(left, right):
    return lax.dot_general(left, right, NT, preferred_element_type=F32)


def rms(values, gain):
    return values * lax.rsqrt(jnp.mean(values * values, -1, keepdims=True) + NORM_EPS) * gain


def rms_back(values, gain, dn):
    r = lax.rsqrt(jnp.mean(values * values, -1, keepdims=True) + NORM_EPS)
    dng = dn * gain
    dv = r * (dng - values * (r * r) * jnp.mean(dng * values, -1, keepdims=True))
    return dv, jnp.sum(dn * values * r, 0, keepdims=True)


GC = 0.7978845608028654
GA = 0.044715


def gelu(x):
    return 0.5 * x * (1.0 + jnp.tanh(GC * (x + GA * x * x * x)))


def gelu_both(x):
    th = jnp.tanh(GC * (x + GA * x * x * x))
    value = 0.5 * x * (1.0 + th)
    slope = 0.5 * (1.0 + th) + 0.5 * x * (1.0 - th * th) * GC * (1.0 + 3.0 * GA * x * x)
    return value, slope


def sigmoid(x):
    return 1.0 / (1.0 + jnp.exp(-x))


def softplus(x):
    return jnp.maximum(x, 0.0) + jnp.log(1.0 + jnp.exp(-jnp.abs(x)))


def rows_back(values, rows, k):
    return jnp.where(rows >= k, pltpu.roll(values, k, 0), 0.0)


def rows_ahead(values, rows, k):
    return jnp.where(rows < SEQ - k, pltpu.roll(values, SEQ - k, 0), 0.0)


class Item:
    pass


def whole_kernel(
    tok_ref, plan_ref, cot_ref, gain_ref, conv_ref, vec_ref,
    win, wgt, wro, wg, wu, wd, wq, wkv, wao,
    n_o, y_o, dx_o, ra, f_ffn, f_qkv, f_ao, f_in, f_ro, f_misc,
    s_in, s_gt, s_ro, s_sm, s_g, s_u, s_d, s_q, s_kv, s_ao,
    ag, sb, rb, res, x_s, n1_s, uv_s, c_s, ig_s, rg_s, a_s, h_s,
    q_s, kv_s, p_s, at_s, gate_s, up_s, hid_s, du_s, both_s,
    dkvb, gnb, yb, xb, smb,
    work, hid_t, o_t, att_t, g_t, u_t, qkv_t, in_t, misc_t,
    la1, la_o, la_a, rc1, rc_o, rc_a, l_g1, l_u1, l_g2, l_u2, l_d2, l_qkv, l_in, l_misc,
    a_d2, cs, raw_in, raw_gt, cot_s, raw_gain, raw_conv, raw_vec, in_sem, *rest,
):
    crs, gots, fins = rest[:11], rest[11:22], rest[22:33]
    (
        wl_sem, ws_sem, wr_sem, ags_sem, agr_sem, rss_sem, rsr_sem,
        kvs_sem, kvr_sem, gns_sem, gnr_sem, dl_sem, dls_sem, dlr_sem,
        rgs_sem, rgr_sem, wk_sem, xs_sem, xr_sem, ys_sem, yr_sem, gs_sem, gr_sem, loc_sem,
        cs_sem, cr_sem,
    ) = rest[33:]
    s = lax.axis_index("section")
    t = lax.axis_index("tensor")
    d = lax.axis_index("dp")
    place = (lax.rem(d, 4), d // 4)
    peers = [lax.rem(t + k, 4) for k in range(4)]
    def own_rows(h):
        return pl.ds(pl.multiple_of(h * 64 + t * 16, 16), 16)

    mine = [own_rows(h) for h in range(2)]

    def half_of(h):
        return pl.ds(pl.multiple_of(h * 64, 64), 64)


    def pos(base, k):
        return lax.rem(base + k, 4)

    def along(axis, k, core):
        if axis == X_AXIS:
            return (core, t, place[1] * 4 + pos(place[0], k))
        return (core, t, pos(place[1], k) * 4 + place[0])

    entry = [
        (win, raw_in), (wgt, raw_gt), (tok_ref, work.at[: 2 * SEQ]), (gain_ref, raw_gain),
        (conv_ref, raw_conv), (vec_ref, raw_vec),
        (cot_ref.at[pl.ds(pl.multiple_of(s * SEQ, SEQ), SEQ)], cot_s),
    ]
    entry = [pltpu.make_async_copy(a, b, in_sem.at[i]) for i, (a, b) in enumerate(entry)]
    for copy in entry:
        copy.start()
    barrier = pltpu.get_barrier_semaphore()
    other = (1 - s, t, d)
    for k in range(1, 4):
        for target in (
            (s, peers[k], d), (1 - s, peers[k], d), along(X_AXIS, k, s), along(Y_AXIS, k, s),
        ):
            pl.semaphore_signal(barrier, inc=1, device_id=target, device_id_type=MESH)
    pl.semaphore_signal(barrier, inc=1, device_id=other, device_id_type=MESH)

    def push(src, dst, send_sem, recv_sem, target):
        return pltpu.make_async_remote_copy(
            src_ref=src, dst_ref=dst, send_sem=send_sem, recv_sem=recv_sem,
            device_id=target, device_id_type=MESH,
        )

    half_in = pl.ds(pl.multiple_of(s * HW, HW), HW)
    half_gt = pl.ds(pl.multiple_of(s * 64, 64), 64)
    moves = [
        (s_in.at[half_in, :], s_in.at[half_in, :]),
        (smb, s_sm.at[s]),
        (s_gt.at[half_gt, :], s_gt.at[half_gt, :]),
        (wro, s_ro.at[s]),
        (wg.at[0], s_g.at[s]),
        (wu.at[0], s_u.at[s]),
        (wd.at[0], s_d.at[s]),
        (wq, s_q.at[half_in, :]),
        (wkv, s_kv.at[half_in, :]),
        (wao, s_ao.at[s]),
    ]
    local = [pltpu.make_async_copy(a, b, wl_sem.at[i]) for i, (a, b) in enumerate(moves)]
    swap = [push(a, b, ws_sem.at[i], wr_sem.at[i], other) for i, (a, b) in enumerate(moves)]
    for copy in local[3:]:
        copy.start()
    entry[0].wait()
    s_in[half_in, :] = raw_in[...].reshape(HW, 2 * RQ)
    entry[1].wait()
    s_gt[half_gt, :] = raw_gt[...].reshape(64, 2 * RQ)
    for copy in entry[3:6]:
        copy.wait()
    smb[...] = jnp.zeros((8, D), F32)
    smb[0:2, :] = raw_gain[0]
    smb[2:4, :RQ] = raw_conv[...].astype(F32)
    smb[2:4, RQ : 2 * RQ] = raw_vec[...].astype(F32)
    s_sm[s] = smb[...]
    entry[2].wait()
    x_s[...] = jnp.where(plan_ref[0, s] == 0, work[:SEQ, :], work[SEQ : 2 * SEQ, :])
    entry[6].wait()
    n_o[0] = s
    n_o[1] = plan_ref[0, 0]
    pl.semaphore_wait(barrier, 13)
    swap[1].start()
    swap[0].start()

    def weights(*which):
        for i in which:
            if i > 2:
                local[i].wait()
            swap[i].wait_recv()


    sub = [slice(0, 16), slice(16, 32)]

    def gather(p, h):
        return [
            push(
                ag.at[p, own_rows(h)], ag.at[p, own_rows(h)], ags_sem.at[p, h, k], agr_sem.at[p, h, k],
                (s, peers[k], d),
            )
            for k in (2, 1, 3)
        ]

    def gather_start(p, h, shard):
        ag[p, mine[h], :] = shard.astype(BF)
        for copy in gather(p, h):
            copy.start()

    def gather_wait(p, h):
        for copy in gather(p, h):
            copy.wait()

    def scatter(p, h):
        return [
            push(
                sb.at[p % 2, pl.ds(pl.multiple_of(h * 64 + peers[k] * 16, 16), 16)],
                rb.at[p % 2, k - 1, pl.ds(pl.multiple_of(h * 16, 16), 16)],
                rss_sem.at[p, h, k], rsr_sem.at[p, h, k], (s, peers[k], d),
            )
            for k in (2, 1, 3)
        ]

    def scatter_start(p, *halves):
        for h in halves:
            for copy in scatter(p, h):
                copy.start()

    def scatter_wait(p, h):
        for copy in scatter(p, h):
            copy.wait()
        total = sb[p % 2, mine[h], :].astype(F32)
        for k in range(3):
            total = total + rb[p % 2, k, h * 16 : h * 16 + 16].astype(F32)
        return total

    def deliver_copy(buf, out, core, which, k, h):
        return push(
            buf.at[sub[h]], out.at[s, mine[h]], dls_sem.at[which, k, h],
            dlr_sem.at[which, s, k, h], (core, peers[k], d),
        )

    def deliver(buf, out, core, which):
        @pl.when(s == core)
        def _():
            own = [
                pltpu.make_async_copy(buf.at[sub[h]], out.at[s, mine[h]], dl_sem.at[which, h])
                for h in range(2)
            ]
            for copy in own:
                copy.start()
            for k in range(1, 4):
                for h in range(2):
                    deliver_copy(buf, out, core, which, k, h).start()
            for copy in own:
                copy.wait()

        @pl.when(s != core)
        def _():
            for k in range(4):
                for h in range(2):
                    deliver_copy(buf, out, core, which, k, h).start()

    def deliver_wait(buf, out, core, which):
        def landed(sender, k, h):
            push(
                buf.at[sub[h]], out.at[sender, mine[h]], dls_sem.at[which, k, h],
                dlr_sem.at[which, sender, k, h], (core, peers[k], d),
            ).wait_recv()

        for h in range(2):

            @pl.when(s == core)
            def _(h=h):
                for k in range(1, 4):
                    deliver_copy(buf, out, core, which, k, h).wait_send()
                    landed(core, k, h)
                for k in range(4):
                    landed(1 - core, k, h)

            @pl.when(s != core)
            def _(h=h):
                for k in range(4):
                    deliver_copy(buf, out, core, which, k, h).wait_send()


    sends = []

    def mult(x, by):
        return pl.multiple_of(x * by, by)

    def slot(place_at):
        return pl.ds(mult(place_at, SEQ), SEQ)

    ring_got = [None] * 5

    def ring_make(g, src):
        axis = RING_AXIS[g]
        here = ra.at[g, slot(place[axis])]
        stay = pltpu.make_async_copy(src, here, wk_sem.at[g])
        copies = [
            push(src, here, rgs_sem.at[g, k], rgr_sem.at[g, k], along(axis, k, s)) for k in (1, 3)
        ]
        sends.extend(copies)
        ring_got[g] = [stay, copies]

    def ring_go(g):
        ring_got[g][0].start()
        for copy in ring_got[g][1]:
            copy.start()

    def ring_start(g, src):
        ring_make(g, src)
        ring_go(g)

    def ring_pass(g):
        axis = RING_AXIS[g]
        copies = []
        for j, (side, back) in enumerate(((1, 3), (3, 1))):
            ring_got[g][1][j].wait_recv()
            rows = ra.at[g, pl.ds(mult(pos(place[axis], back) * 2 + j, 64), 64)]
            copy = push(rows, rows, rgs_sem.at[g, 2 * j], rgr_sem.at[g, 2 * j], along(axis, side, s))
            copy.start()
            copies.append(copy)
        sends.extend(copies)
        ring_got[g][1] = copies

    in_work = [None, None]

    def ring_load(g):
        if in_work[0] == g:
            return
        ring_got[g][0].wait()
        for copy in ring_got[g][1]:
            copy.wait_recv()
        copy = pltpu.make_async_copy(ra.at[g], work, wk_sem.at[5 + g])
        copy.start()
        in_work[0] = g
        in_work[1] = copy

    def ring_use(g):
        ring_load(g)
        if in_work[1] is not None:
            in_work[1].wait()
            in_work[1] = None


    full = {QKV: f_qkv, AO: f_ao, IN: f_in, RO: f_ro, MISC: f_misc}
    owner = {G1: 0, U1: 0, D1: 0, G2: 1, U2: 1, D2: 1}
    items = []
    for i in range(11):
        it = Item()
        it.i = i
        it.style, it.total, it.axis = PLAN[i]
        it.n8 = it.total // 8
        it.m = place[it.axis]
        it.n = place[1 - it.axis]
        it.cr, it.got, it.fin = crs[i], gots[i], fins[i]
        it.acc = a_d2 if i == D2 else s_d.at[1, ROOM[i] : ROOM[i] + it.n8]
        if i in owner:
            it.full = f_ffn.at[(s if owner[i] == 0 else 1 - s) * 3 + i % 3]
            it.home = f_ffn.at[i % 3]
        else:
            it.full = full[i]
            it.home = full[i]
        it.waits = []
        items.append(it)

    def spread(i, which, source, target):
        it = items[i]
        for k in range(1, 4):
            copy = push(
                source(pos(it.m, k)), target(k), xs_sem.at[i, which, k], xr_sem.at[i, which, k],
                along(it.axis, k, s),
            )
            copy.start()
            sends.append(copy)
            it.waits.append(copy)

    def spread_rows(i, whole, into):
        it = items[i]

        def part(f):
            return whole.at[pl.ds(mult(f, 2 * it.n8), 2 * it.n8), :]

        into[:, slot(it.m)] = part(it.m)[...]
        spread(i, 0, part, lambda k: into.at[:, slot(it.m)])

    def spread_left(i, whole, into):
        it = items[i]
        into[:, slot(it.m)] = whole[...]
        spread(i, 0, lambda f: whole, lambda k: into.at[:, slot(it.m)])

    def spread_cols(i, src, into):
        it = items[i]

        def cut(f):
            return pl.ds(mult(f, CC), CC)

        into[slot(it.m), :] = src[:, cut(it.m)]
        spread(i, 1, lambda f: src.at[:, cut(f)], lambda k: into.at[slot(it.m), :])

    def arrived(it):
        for copy in it.waits:
            copy.wait_recv()
        it.waits = []

    def settle(it):
        for copy in it.waits:
            copy.wait()
        it.waits = []

    def piece(it, q):
        return it.acc.at[:, pl.ds(mult(q, CC), CC)]

    cs_busy = [None, None]
    cs_count = [0]

    def halves(i, fill):
        it = items[i]
        at = cs_count[0] % 2
        cs_count[0] += 1
        if cs_busy[at] is not None:
            cs_busy[at].wait_send()
        out = cs.at[at, : it.n8]
        fill(1 - s, out)
        copy = push(out, it.cr, cs_sem.at[i], cr_sem.at[i], other)
        copy.start()
        cs_busy[at] = copy
        it.swap = copy
        fill(s, it.acc)

    def rows_product(i, ring, left):
        it = items[i]
        arrived(it)
        ring_use(ring)

        def fill(h, ref):
            rows = left[pl.ds(mult(h, it.n8), it.n8), :]
            for j in range(4):
                cols = slice(j * CC, j * CC + CC)
                ref[:, cols] = mm(rows, work[:, cols]).astype(BF)

        halves(i, fill)

    def cols_product(i, left, right):
        it = items[i]
        arrived(it)

        def fill(h, ref):
            for q in range(4):
                rows = left[pl.ds(mult(h * 4 + q, it.n8), it.n8), :]
                ref[:, q * CC : q * CC + CC] = mm(rows, right[...]).astype(BF)

        halves(i, fill)

    def misc_sum():
        it = items[MISC]
        arrived(it)

        def fill(h, ref):
            at = pl.ds(mult(h, it.n8), it.n8)
            total = l_misc[0, at, :].astype(F32)
            for k in range(1, 4):
                total = total + l_misc[k, at, :].astype(F32)
            ref[...] = total.astype(BF)

        halves(MISC, fill)

    row_items = {
        G1: (RN2, l_g1), U1: (RN2, l_u1), G2: (RN2B, l_g2), U2: (RN2B, l_u2),
        D2: (RCOT, l_d2), QKV: (RNA, l_qkv), IN: (RN1, l_in),
    }
    col_items = {D1: (la1, rc1), AO: (la_a, rc_a), RO: (la_o, rc_o)}

    def e1(i):
        if i in row_items:
            rows_product(i, *row_items[i])
        elif i in col_items:
            cols_product(i, *col_items[i])
        else:
            misc_sum()

    def cut_of(it):
        return {144: 80, 80: 48, 128: 64, 48: 32, 64: 32}[it.n8]

    def sides(it, at, axis, right, left):
        for j, (side, (src, dst)) in enumerate(((1, right), (3, left))):
            copy = push(src, dst, ys_sem.at[it.i, at + j], yr_sem.at[it.i, at + j], along(axis, side, s))
            copy.start()
            it.waits.append(copy)

    def e2(i):
        it = items[i]
        it.swap.wait_recv()
        it.acc[...] = (it.acc[...].astype(F32) + it.cr[...].astype(F32)).astype(BF)
        if i in DIRECT:
            for k in range(1, 4):
                copy = push(
                    piece(it, pos(it.n, k)), it.got.at[k - 1], ys_sem.at[i, k], yr_sem.at[i, k],
                    along(1 - it.axis, k, s),
                )
                copy.start()
                it.waits.append(copy)
            return
        cut = cut_of(it)
        far = piece(it, pos(it.n, 2))
        sides(
            it, 0, 1 - it.axis, (far.at[:cut], it.got.at[0, :cut]), (far.at[cut:], it.got.at[0, cut:])
        )

    def e2r(i):
        it = items[i]
        if i in DIRECT:
            return
        settle(it)
        cut = cut_of(it)
        right = piece(it, pos(it.n, 1))
        left = piece(it, pos(it.n, 3))
        right[:cut] = (right[:cut].astype(F32) + it.got[0, :cut].astype(F32)).astype(BF)
        left[cut:] = (left[cut:].astype(F32) + it.got[0, cut:].astype(F32)).astype(BF)
        sides(it, 2, 1 - it.axis, (right, it.got.at[1]), (left, it.got.at[2]))

    def rect(it, ref, f, q, lo=0, n=None):
        block, at = (f * 2 + s, q) if it.style == "r" else (s * 4 + q, f)
        rows = pl.ds(pl.multiple_of(block * it.n8 + lo, 16), n or it.n8)
        return ref.at[rows, pl.ds(mult(at, CC), CC)]

    def quarter(it, ref, f, part=None):
        if it.style == "r":
            rows = pl.ds(mult(f * 2 + s, it.n8), it.n8)
            if part is None:
                return ref.at[rows, :]
            return ref.at[rows, part * HW : part * HW + HW]
        cols = pl.ds(mult(f, CC), CC)
        if part is None:
            return ref.at[pl.ds(mult(s, 4 * it.n8), 4 * it.n8), cols]
        return ref.at[pl.ds(mult(s * 2 + part, 2 * it.n8), 2 * it.n8), cols]

    def e3(i):
        it = items[i]
        settle(it)
        total = piece(it, it.n)[...].astype(F32)
        for k in range(3) if i in DIRECT else (1, 2):
            total = total + it.got[k].astype(F32)
        it.fin[...] = total.astype(BF)
        spot = rect(it, it.full, it.m, it.n)
        own = pltpu.make_async_copy(it.fin, spot, loc_sem.at[i])
        own.start()
        it.waits.append(own)
        if i in DIRECT:
            for k in range(1, 4):
                copy = push(
                    it.fin, spot, gs_sem.at[i, k], gr_sem.at[i, k], along(1 - it.axis, k, s)
                )
                copy.start()
                it.waits.append(copy)
            return
        sides(it, 4, 1 - it.axis, (it.fin, spot), (it.fin, spot))

    def e3r(i):
        it = items[i]
        if i in DIRECT:
            return
        settle(it)
        cut = cut_of(it)
        left = rect(it, it.full, it.m, pos(it.n, 3), 0, cut)
        right = rect(it, it.full, it.m, pos(it.n, 1), cut, it.n8 - cut)
        sides(it, 6, 1 - it.axis, (left, left), (right, right))

    def both_ways(it, at, right, left):
        for side, part in ((1, right), (3, left)):
            copy = push(
                part, part, gs_sem.at[it.i, at + side // 2], gr_sem.at[it.i, at + side // 2],
                along(it.axis, side, s),
            )
            copy.start()
            it.waits.append(copy)

    def to_other(it, ks):
        whole_c = it.style == "c" and it.i not in owner
        copies = []
        for k in ks:
            f = pos(it.m, k)
            if whole_c:
                if k != 2:
                    continue
                rows = pl.ds(mult(s, 4 * it.n8), 4 * it.n8)
            elif it.style == "c":
                rows = pl.ds(mult(s, 4 * it.n8), 4 * it.n8)
            else:
                rows = pl.ds(mult(f * 2 + s, it.n8), it.n8)
            cols = pl.ds(0, D)
            if it.i in (QKV, AO, IN, RO):
                cols = pl.ds(mult(1 - s, HW), HW)
            elif it.style == "c":
                cols = pl.ds(mult(f, CC), CC)
            copies.append(
                push(
                    it.full.at[rows, cols], it.home.at[rows, cols],
                    gs_sem.at[it.i, 8 + k], gr_sem.at[it.i, 8 + k], other,
                )
            )
        return copies

    def home(it, *ks):
        if it.i in owner:

            @pl.when(s != owner[it.i])
            def _():
                for copy in to_other(it, ks):
                    copy.start()
        else:
            for copy in to_other(it, ks):
                copy.start()

    def e4(i):
        it = items[i]
        settle(it)
        part = quarter(it, it.full, it.m)
        both_ways(it, 4, part, part)
        home(it, 0)

    def e5(i):
        it = items[i]
        settle(it)
        both_ways(
            it, 6, quarter(it, it.full, pos(it.m, 3), 0), quarter(it, it.full, pos(it.m, 1), 1)
        )
        home(it, 3, 1)

    def e6(i):
        it = items[i]
        settle(it)
        home(it, 2)

    def e7(i):
        it = items[i]
        if i in owner:

            @pl.when(s != owner[i])
            def _():
                for copy in to_other(it, range(4)):
                    copy.wait_send()

            @pl.when(s == owner[i])
            def _():
                for copy in to_other(it, range(4)):
                    copy.wait_recv()
        else:
            for copy in to_other(it, range(4)):
                copy.wait()

    def gain(block, which):
        return s_sm[block, which : which + 1, :]

    rows = lax.broadcasted_iota(jnp.int32, (SEQ, RQ), 0)

    ring_start(RCOT, cot_s)
    weights(1)
    n1_s[...] = rms(x_s[...].astype(F32), gain(0, 0)).astype(BF)
    for copy in swap[2:]:
        copy.start()
    ring_start(RN1, n1_s)
    uv_s[...] = mm(n1_s[:, half_in], s_in[half_in, :])
    weights(0)
    half_other = pl.ds(mult(1 - s, HW), HW)
    uv_s[...] += mm(n1_s[:, half_other], s_in[half_other, :])
    taps = [s_sm[k // 2, 2 + k % 2 : 3 + k % 2, :RQ] for k in range(4)]
    vec = [s_sm[k // 2, 2 + k % 2 : 3 + k % 2, RQ : 2 * RQ] for k in range(4)]
    u = uv_s[:, :RQ]
    c = vec[0] + taps[0] * u
    for k in range(1, 4):
        c = c + taps[k] * rows_back(u, rows, k)
    c_s[...] = c
    weights(2, 3)
    for head in range(4):
        cols = slice(head * HD, head * HD + HD)
        cb = c_s[:, cols].astype(BF)
        ig_s[:, cols] = sigmoid(mm(cb, s_gt[:, cols]) + vec[1][:, cols])
        rg_s[:, cols] = sigmoid(
            mm(cb, s_gt[:, RQ + head * HD : RQ + head * HD + HD]) + vec[2][:, cols]
        )
    speed = softplus(vec[3])
    a = jnp.exp(-8.0 * rg_s[...] * speed)
    a_s[...] = a
    run = jnp.sqrt(jnp.maximum(1.0 - a * a, RATE_FLOOR)) * ig_s[...] * c_s[...]
    step = 1
    while step < SEQ:
        run = run + a * rows_back(run, rows, step)
        if 2 * step < SEQ:
            a = a * jnp.where(rows >= step, pltpu.roll(a, step, 0), 1.0)
        step *= 2
    h_s[...] = run
    o = (run * gelu(uv_s[:, RQ:])).astype(BF)
    for half in range(2):
        sb[0, :, half * HW : half * HW + HW] = mm(o, s_ro[half]).astype(BF)
    scatter_start(0, 0, 1)
    o_t[...] = o.T
    spread_left(RO, o_t, la_o)
    for h in range(2):
        x1 = x_s[mine[h], :].astype(F32) + scatter_wait(0, h)
        res[0, sub[h]] = x1
        gather_start(0, h, rms(x1, gain(0, 1)))

    def ffn_forward(block, p_in, p_out, ring):
        ring_make(ring, ag.at[p_in])

        def one(h, carry):
            gather_wait(p_in, h)
            half = half_of(h)
            n2 = ag[p_in, half, :]

            @pl.when(h == 1)
            def _():
                ring_go(ring)

            for j in range(3):
                cols = slice(j * CC, j * CC + CC)
                gate = mm(n2, s_g[block, :, cols])
                up = mm(n2, s_u[block, :, cols])
                gate_s[block, half, cols] = gate
                up_s[block, half, cols] = up
                hid_s[half, cols] = (gelu(gate) * up).astype(BF)
            if block == 0:

                @pl.when(h == 0)
                def _():
                    weights(6)

            hid = hid_s[half, :]
            for j in range(4):
                cols = slice(j * CC, j * CC + CC)
                sb[p_out % 2, half, cols] = mm(hid, s_d[block, :, cols]).astype(BF)
            scatter_start(p_out, h)
            return carry

        lax.fori_loop(0, 2, one, 0)
        hid_t[block] = hid_s[...].T

    weights(4, 5)
    ffn_forward(0, 0, 1, RN2)
    spread_left(D1, hid_t.at[0], la1)
    ring_pass(RCOT)
    ring_pass(RN1)
    for h in range(2):
        mid = (res[0, sub[h]] + scatter_wait(1, h)).astype(BF).astype(F32)
        res[1, sub[h]] = mid
        gather_start(1, h, rms(mid, gain(1, 0)))
    weights(7, 8, 9)

    p_s[:, :64, 64:] = jnp.zeros((3, 64, 64), F32)
    for h in range(2):
        gather_wait(1, h)
        if h == 1:
            ring_start(RNA, ag.at[1])
        half = slice(h * 64, h * 64 + 64)
        n = 64 * h + 64
        na = ag[1, half]
        q_s[half] = mm(na, s_q[...]).astype(BF)
        kv_s[half] = mm(na, s_kv[...]).astype(BF)
        keys = kv_s[:n, :HD]
        vals = kv_s[:n, HD:]
        col = lax.broadcasted_iota(jnp.int32, (64, n), 1)
        row = lax.broadcasted_iota(jnp.int32, (64, n), 0) + 64 * h
        for head in range(3):
            cols = slice(head * HD, head * HD + HD)
            score = jnp.where(col <= row, mm_nt(q_s[half, cols], keys) * HD ** (-0.5), -1e30)
            expo = jnp.exp(score - jnp.max(score, -1, keepdims=True))
            p = expo / jnp.sum(expo, -1, keepdims=True)
            p_s[head, half, :n] = p
            at_s[half, cols] = mm(p.astype(BF), vals).astype(BF)
        for c in range(2):
            sb[0, half, c * HW : c * HW + HW] = mm(at_s[half], s_ao[c]).astype(BF)
        scatter_start(2, h)
    att = at_s[...]
    att_t[...] = att.T
    spread_left(AO, att_t, la_a)
    ring_pass(RN2)
    for h in range(2):
        x1 = res[1, sub[h]] + scatter_wait(2, h)
        res[2, sub[h]] = x1
        gather_start(2, h, rms(x1, gain(1, 1)))
    ffn_forward(1, 2, 3, RN2B)
    spread_rows(D2, hid_t.at[1], l_d2)
    ring_load(RCOT)

    def ffn_back_rows(block, half, dF, p_out):
        for j in range(3):
            cols = slice(j * CC, j * CC + CC)
            dhid = mm_nt(dF, s_d[block, cols, :])
            value, slope = gelu_both(gate_s[block, half, cols])
            hid_s[half, cols] = (dhid * up_s[block, half, cols] * slope).astype(BF)
            du_s[half, cols] = (dhid * value).astype(BF)
        dg = hid_s[half, :]
        du = du_s[half, :]
        for j in range(4):
            cols = slice(j * CC, j * CC + CC)
            sb[p_out % 2, half, cols] = (
                mm_nt(dg, s_g[block, cols, :]) + mm_nt(du, s_u[block, cols, :])
            ).astype(BF)

    def ffn_back_send(block):
        g_t[block] = hid_s[...].T
        spread_rows(G2 if block else G1, g_t.at[block], l_g2 if block else l_g1)
        u_t[block] = du_s[...].T
        spread_rows(U2 if block else U1, u_t.at[block], l_u2 if block else l_u1)

    ffn_back_rows(1, pl.ds(0, SEQ), cot_s[...], 4)
    scatter_start(4, 0, 1)
    ffn_back_send(1)
    for h in range(2):
        yb[sub[h], :] = (res[2, sub[h]] + scatter_wait(3, h)).astype(BF)
    ring_pass(RNA)
    gg11 = []
    for h in range(2):
        dv, gg = rms_back(res[2, sub[h]], gain(1, 1), scatter_wait(4, h))
        gg11.append(gg)
        dx1 = cot_s[mine[h], :].astype(F32) + dv
        res[3, sub[h]] = dx1
        gather_start(3, h, dx1)
    ring_pass(RN2B)
    e1(D2)
    e2(D2)

    gather_wait(3, 0)
    gather_wait(3, 1)
    spread_cols(AO, ag.at[3], rc_a)
    dA = ag[3]
    datt_s = both_s.at[:, :AQ]
    dq_s = both_s.at[:, AQ : 2 * AQ]
    datt_s[...] = (mm_nt(dA[:, :HW], s_ao[0]) + mm_nt(dA[:, HW:], s_ao[1])).astype(BF)
    dk = jnp.zeros((SEQ, HD), F32)
    dw = jnp.zeros((SEQ, HD), F32)
    for head in range(3):
        cols = slice(head * HD, head * HD + HD)
        p = p_s[head]
        datt = datt_s[:, cols]
        dpr = mm_nt(datt, kv_s[:, HD:])
        dw = dw + mm(p.astype(BF).T, datt)
        ds = (p * (dpr - jnp.sum(p * dpr, -1, keepdims=True)) * HD ** (-0.5)).astype(BF)
        dq_s[:, cols] = mm(ds, kv_s[:, :HD]).astype(BF)
        dk = dk + mm(ds.T, q_s[:, cols])
    dkvb[0, :, :HD] = dk.astype(BF)
    dkvb[0, :, HD:] = dw.astype(BF)
    kv_copies = [
        push(dkvb.at[0], dkvb.at[k], kvs_sem.at[k], kvr_sem.at[k], (s, peers[k], d))
        for k in range(1, 4)
    ]
    for copy in kv_copies:
        copy.start()
    dq = dq_s[...]
    for j in range(4):
        cols = slice(j * CC, j * CC + CC)
        sb[1, :, cols] = mm_nt(dq, s_q[cols, :]).astype(BF)
    scatter_start(5, 0, 1)
    e1(G2)
    e2r(D2)
    e1(U2)
    ring_load(RNA)
    for copy in kv_copies:
        copy.wait()
    total = dkvb[0].astype(F32)
    for k in range(1, 4):
        total = total + dkvb[k].astype(F32)
    dkv_s = both_s.at[:, 2 * AQ : 2 * AQ + 256]
    dkv_s[...] = total.astype(BF)
    qkv_t[:AQ] = dq_s[...].T
    qkv_t[AQ:] = dkv_s[...].T
    spread_rows(QKV, qkv_t, l_qkv)
    e1(AO)
    e2(G2)
    gg10 = []
    for h in range(2):
        dn = scatter_wait(5, h) + mm_nt(dkv_s[mine[h], :], s_kv[...])
        dv, gg = rms_back(res[1, sub[h]], gain(1, 0), dn)
        gg10.append(gg)
        big_g = (res[3, sub[h]] + dv).astype(BF)
        gather_start(4, h, big_g)
        res[3, sub[h]] = big_g.astype(F32)
    e2(U2)
    e2(AO)
    e3(D2)
    e1(QKV)
    ring_load(RN2)
    e2r(G2)

    it = items[D1]
    cols_at = [pl.ds(mult(pos(it.m, k), CC), CC) for k in range(4)]
    d1_copies = [
        push(
            ag.at[4, :, cols_at[k]], rc1.at[slot(it.m), :], xs_sem.at[D1, 1, k], xr_sem.at[D1, 1, k],
            along(it.axis, k, s),
        )
        for k in range(1, 4)
    ]
    d1_rows = slot(it.m)

    def back_half(h, carry):
        gather_wait(4, h)

        @pl.when(h == 1)
        def _():
            rc1[d1_rows, :] = ag[4, :, cols_at[0]]
            for copy in d1_copies:
                copy.start()

        ffn_back_rows(0, half_of(h), ag[4, half_of(h), :], 6)
        scatter_start(6, h)
        return carry

    lax.fori_loop(0, 2, back_half, 0)
    it.waits += d1_copies
    sends.extend(d1_copies)
    ffn_back_send(0)
    e3(U2)
    e3(G2)
    e3(AO)
    e2(QKV)
    e3r(D2)
    gg01 = []
    for h in range(2):
        dv, gg = rms_back(res[0, sub[h]], gain(0, 1), scatter_wait(6, h))
        gg01.append(gg)
        dx1 = res[3, sub[h]] + dv
        res[3, sub[h]] = dx1
        gather_start(5, h, dx1)
    e1(D1)
    e1(G1)
    e3(QKV)
    e4(AO)
    e2(D1)
    e4(D2)
    e1(U1)
    ring_load(RN1)

    gather_wait(5, 0)
    gather_wait(5, 1)
    spread_cols(RO, ag.at[5], rc_o)
    dA = ag[5]
    dO = mm_nt(dA[:, :HW], s_ro[0]) + mm_nt(dA[:, HW:], s_ro[1])
    value, slope = gelu_both(uv_s[:, RQ:])
    h = h_s[...]
    both_s[:, RQ:] = (dO * h * slope).astype(BF)
    e = dO * value
    a = a_s[...]
    coef = rows_ahead(a, rows, 1)
    step = 1
    while step < SEQ:
        e = e + coef * rows_ahead(e, rows, step)
        if 2 * step < SEQ:
            coef = coef * rows_ahead(coef, rows, step)
        step *= 2
    ig = ig_s[...]
    rg = rg_s[...]
    c = c_s[...]
    room = 1.0 - a * a
    m = jnp.sqrt(jnp.maximum(room, RATE_FLOOR))
    ga = e * rows_back(h, rows, 1) - jnp.where(room > RATE_FLOOR, e * ig * c * a / m, 0.0)
    dl = ga * a
    gv3 = jnp.sum(dl * rg, 0, keepdims=True) * (-8.0) * sigmoid(vec[3])
    er = -8.0 * dl * speed * rg * (1.0 - rg)
    ei = e * m * c * ig * (1.0 - ig)
    gv1 = jnp.sum(ei, 0, keepdims=True)
    gv2 = jnp.sum(er, 0, keepdims=True)
    c_s[...] = e * m * ig
    ig_s[...] = ei
    rg_s[...] = er
    for head in range(4):
        cols = slice(head * HD, head * HD + HD)
        late = slice(RQ + head * HD, RQ + head * HD + HD)
        dpin = ig_s[:, cols].astype(BF)
        dprec = rg_s[:, cols].astype(BF)
        cbt = c[:, cols].astype(BF).T
        misc_t[:, cols] = mm(cbt, dpin).astype(BF)
        misc_t[:, late] = mm(cbt, dprec).astype(BF)
        c_s[:, cols] += mm_nt(dpin, s_gt[:, cols]) + mm_nt(dprec, s_gt[:, late])
    dc = c_s[...]
    u = uv_s[:, :RQ]
    du = taps[0] * dc
    gtap = [jnp.sum(u * dc, 0, keepdims=True)]
    for k in range(1, 4):
        du = du + taps[k] * rows_ahead(dc, rows, k)
        gtap.append(jnp.sum(rows_back(u, rows, k) * dc, 0, keepdims=True))
    gv0 = jnp.sum(dc, 0, keepdims=True)
    both_s[:, :RQ] = du.astype(BF)
    both = both_s[...]
    for j in range(4):
        cols = slice(j * CC, j * CC + CC)
        sb[1, :, cols] = mm_nt(both, s_in[cols, :]).astype(BF)
    scatter_start(7, 0, 1)
    in_t[...] = both.T
    spread_rows(IN, in_t, l_in)
    e2(G1)
    e2(U1)
    e4(U2)
    e3r(G2)
    e1(RO)
    gg00 = []
    for h in range(2):
        dv, gg = rms_back(x_s[mine[h], :].astype(F32), gain(0, 0), scatter_wait(7, h))
        gg00.append(gg)
        xb[sub[h], :] = (res[3, sub[h]] + dv).astype(BF)
    deliver(xb, dx_o, 0, 1)
    gnb[0, 0:1] = gg00[0] + gg00[1]
    gnb[0, 1:2] = gg01[0] + gg01[1]
    gnb[0, 2:3] = gg10[0] + gg10[1]
    gnb[0, 3:4] = gg11[0] + gg11[1]
    gnb[0, 4:8] = jnp.zeros((4, D), F32)
    gn_copies = [
        push(gnb.at[0], gnb.at[k], gns_sem.at[k], gnr_sem.at[k], (s, peers[k], d))
        for k in range(1, 4)
    ]
    for copy in gn_copies:
        copy.start()
    e2(RO)
    e1(IN)
    e2r(U1)
    e2r(G1)
    e2r(D1)
    e5(AO)
    e2(IN)
    deliver(yb, y_o, 1, 0)
    for copy in gn_copies:
        copy.wait()
    gains = gnb[0] + gnb[1] + gnb[2] + gnb[3]
    small = gtap + [gv0, gv1, gv2, gv3]
    for g in range(4):
        for part in range(3):
            small.append(gains[g : g + 1, part * RQ : part * RQ + RQ])
    small.append(jnp.zeros((HD - len(small), RQ), F32))
    misc_t[:, 2 * RQ :] = jnp.concatenate(small, 0).astype(BF)
    it = items[MISC]

    def misc_rows(f):
        return misc_t.at[pl.ds(mult(f, 32), 32), :]

    l_misc[0] = misc_rows(it.m)[...]
    spread(MISC, 0, misc_rows, lambda k: l_misc.at[k])
    e4(QKV)
    e5(D2)
    e5(U2)
    e4(G2)
    e3(RO)
    e3(U1)
    e3(D1)
    e3(G1)
    e6(AO)
    e2r(IN)
    e6(U2)
    e1(MISC)
    e2(MISC)
    e5(QKV)
    e5(G2)
    e3r(U1)
    e6(D2)
    e4(RO)
    e3r(G1)
    e3(MISC)
    e3r(D1)
    e3(IN)
    e6(G2)
    e4(U1)
    e6(QKV)
    e4(D1)
    e3r(IN)
    e5(RO)
    e4(G1)
    e4(MISC)
    e5(U1)
    e4(IN)
    e5(D1)
    e6(RO)
    e5(G1)
    e5(MISC)
    e5(IN)
    e6(U1)
    e6(D1)
    e6(G1)
    e6(IN)
    e6(MISC)
    deliver_wait(yb, y_o, 1, 0)
    deliver_wait(xb, dx_o, 0, 1)
    for copy in swap:
        copy.wait_send()
    for copy in sends + cs_busy:
        copy.wait_send()
    for i in (D2, G2, AO, U2, QKV, G1, U1, D1, RO, IN, MISC):
        e7(i)


def whole_call(tokens, plan, cot, gains, conv, vec, weights):
    sm = pl.BlockSpec(memory_space=pltpu.SMEM)
    hbm = pl.BlockSpec(memory_space=pl.ANY)
    V = pltpu.VMEM
    dma = pltpu.SemaphoreType.DMA
    crs, gots, fins = [], [], []
    for i in range(11):
        n8 = PLAN[i][1] // 8
        crs.append(V((n8, D), BF))
        gots.append(V((3, n8, CC), BF))
        fins.append(V((n8, CC), BF))
    shapes = [
        (2, SEQ, D), (2, SEQ, D), (5, 4 * SEQ, D),
        (6, FQ, D), (640, D), (AQ, D), (1024, D), (RQ, D), (HD, D),
    ]
    return pl.pallas_call(
        whole_kernel,
        name="whole",
        out_shape=[jax.ShapeDtypeStruct((2,), jnp.int32)]
        + [jax.ShapeDtypeStruct(shape, BF) for shape in shapes],
        in_specs=[hbm, sm] + [hbm] * 13,
        out_specs=[sm] + [hbm] * 9,
        scratch_shapes=[
            V((D, 2 * RQ), BF), V((HD, 2 * RQ), BF), V((2, RQ, HW), BF), V((2, 8, D), F32),
            V((2, D, FQ), BF), V((2, D, FQ), BF), V((2, FQ, D), BF),
            V((D, AQ), BF), V((D, 256), BF), V((2, AQ, HW), BF),
            V((6, SEQ, D), BF), V((2, SEQ, D), BF), V((2, 3, SH, D), BF), V((4, SH, D), F32),
            V((SEQ, D), BF), V((SEQ, D), BF), V((SEQ, 2 * RQ), F32),
            V((SEQ, RQ), F32), V((SEQ, RQ), F32), V((SEQ, RQ), F32), V((SEQ, RQ), F32), V((SEQ, RQ), F32),
            V((SEQ, AQ), BF), V((SEQ, 256), BF), V((3, SEQ, SEQ), F32), V((SEQ, AQ), BF),
            V((2, SEQ, FQ), F32), V((2, SEQ, FQ), F32), V((SEQ, FQ), BF),
            V((SEQ, FQ), BF), V((SEQ, 2 * RQ), BF),
            V((4, SEQ, 256), BF), V((4, 8, D), F32), V((SH, D), BF), V((SH, D), BF), V((8, D), F32),
            V((4 * SEQ, D), BF), V((2, FQ, SEQ), BF), V((RQ, SEQ), BF), V((AQ, SEQ), BF),
            V((2, FQ, SEQ), BF), V((2, FQ, SEQ), BF), V((640, SEQ), BF), V((1024, SEQ), BF), V((HD, D), BF),
            V((FQ, 512), BF), V((RQ, 512), BF), V((AQ, 512), BF),
            V((512, CC), BF), V((512, CC), BF), V((512, CC), BF),
            V((288, 512), BF), V((288, 512), BF), V((288, 512), BF), V((288, 512), BF), V((288, 512), BF),
            V((160, 512), BF), V((256, 512), BF), V((4, 32, D), BF),
            V((144, D), BF), V((2, 144, D), BF),
            V((HW, 2, RQ), BF), V((64, 2, RQ), BF), V((SEQ, D), BF),
            V((1, 2, D), F32), V((2, RQ), BF), V((2, RQ), BF), dma((7,)),
            *crs, *gots, *fins,
            dma((10,)), dma((10,)), dma((10,)), dma((6, 2, 4)), dma((6, 2, 4)), dma((8, 2, 4)), dma((8, 2, 4)),
            dma((4,)), dma((4,)), dma((4,)), dma((4,)), dma((2, 2)), dma((2, 4, 2)), dma((2, 2, 4, 2)),
            dma((5, 4)), dma((5, 4)), dma((10,)), dma((11, 2, 4)), dma((11, 2, 4)),
            dma((11, 8)), dma((11, 8)), dma((11, 12)), dma((11, 12)), dma((11,)), dma((11,)), dma((11,)),
        ],
        compiler_params=pltpu.CompilerParams(
            collective_id=0, has_side_effects=True, vmem_limit_bytes=64 * 2**20 - 2**17
        ),
    )(tokens, plan, cot, gains, conv, vec, *weights)


def unpack_kernel(
    n_ref, dx, y, ffn, qkv, ao, rin, ro, misc,
    o_bound, o_gain, o_gate, o_up, o_dn, o_in, o_gt, o_conv, o_vec, o_ro, o_q, o_kv, o_ao,
):
    i = pl.program_id(0)
    s = n_ref[0]
    straight = n_ref[1] == 0
    for j in range(2):
        mine = jnp.where(straight, dx[j], dx[1 - j])
        o_bound[0, j * SEQ : j * SEQ + SEQ, :] = jnp.where(s == 0, mine, y[j]).astype(F32)
    o_gate[0] = ffn[0].T.astype(F32)
    o_up[0] = ffn[1].T.astype(F32)
    o_dn[0] = ffn[2].astype(F32)
    part = qkv[...].T.astype(F32)
    o_q[...] = part[:, :AQ]
    o_kv[...] = part[:, AQ:]
    part = rin[...].T.astype(F32)
    o_in[:, 0, :] = part[:, :RQ]
    o_in[:, 1, :] = part[:, RQ:]

    @pl.when(i == 0)
    def _():
        o_ao[...] = ao[...].astype(F32)
        o_ro[...] = ro[...].astype(F32)
        rows = pl.ds(pl.multiple_of(s * 64, 64), 64)
        o_gt[:, 0, :] = misc[rows, :RQ].astype(F32)
        o_gt[:, 1, :] = misc[rows, RQ : 2 * RQ].astype(F32)
        small = misc[:32, 2 * RQ :].astype(F32)

        def pick(at, step):
            return jnp.where(s == 0, small[at : at + step], small[at + step : at + 2 * step])

        o_conv[...] = pick(0, 2)
        o_vec[...] = pick(4, 2)
        gains = pick(8, 6)
        for j in range(2):
            for p in range(3):
                o_gain[0, j : j + 1, p * RQ : p * RQ + RQ] = gains[j * 3 + p : j * 3 + p + 1]


def unpack_call(scalars, dx, y, ffn, qkv, ao, rin, ro, misc):
    n = 3
    wide = D // n
    part = HW // n
    sds = jax.ShapeDtypeStruct
    fixed = lambda *zero: (lambda i, s: zero)
    return pl.pallas_call(
        unpack_kernel,
        name="unpack",
        out_shape=[
            sds((1, 2 * SEQ, D), F32), sds((1, 2, D), F32),
            sds((1, D, FQ), F32), sds((1, D, FQ), F32), sds((1, FQ, D), F32),
            sds((HW, 2, RQ), F32), sds((64, 2, RQ), F32), sds((2, RQ), F32), sds((2, RQ), F32),
            sds((RQ, HW), F32), sds((HW, AQ), F32), sds((HW, 256), F32), sds((AQ, HW), F32),
        ],
        grid_spec=pltpu.PrefetchScalarGridSpec(
            num_scalar_prefetch=1,
            grid=(n,),
            in_specs=[
                pl.BlockSpec((2, SEQ, wide), lambda i, s: (0, 0, i)),
                pl.BlockSpec((2, SEQ, wide), lambda i, s: (0, 0, i)),
                pl.BlockSpec((3, FQ, wide), lambda i, s: (0, 0, i)),
                pl.BlockSpec((640, part), lambda i, s: (0, s[0] * n + i)),
                pl.BlockSpec((AQ, HW), lambda i, s: (0, s[0])),
                pl.BlockSpec((1024, part), lambda i, s: (0, s[0] * n + i)),
                pl.BlockSpec((RQ, HW), lambda i, s: (0, s[0])),
                pl.BlockSpec((HD, D), fixed(0, 0)),
            ],
            out_specs=[
                pl.BlockSpec((1, 2 * SEQ, wide), lambda i, s: (0, 0, i)),
                pl.BlockSpec((1, 2, D), fixed(0, 0, 0)),
                pl.BlockSpec((1, wide, FQ), lambda i, s: (0, i, 0)),
                pl.BlockSpec((1, wide, FQ), lambda i, s: (0, i, 0)),
                pl.BlockSpec((1, FQ, wide), lambda i, s: (0, 0, i)),
                pl.BlockSpec((part, 2, RQ), lambda i, s: (i, 0, 0)),
                pl.BlockSpec((64, 2, RQ), fixed(0, 0, 0)),
                pl.BlockSpec((2, RQ), fixed(0, 0)),
                pl.BlockSpec((2, RQ), fixed(0, 0)),
                pl.BlockSpec((RQ, HW), fixed(0, 0)),
                pl.BlockSpec((part, AQ), lambda i, s: (i, 0)),
                pl.BlockSpec((part, 256), lambda i, s: (i, 0)),
                pl.BlockSpec((AQ, HW), fixed(0, 0)),
            ],
        ),
        compiler_params=pltpu.CompilerParams(vmem_limit_bytes=62 * 2**20),
    )(scalars, dx, y, ffn, qkv, ao, rin, ro, misc)


def per_device(
    tokens, plan_order, cotangent, norm_gains, ffn_gate, ffn_up, ffn_down,
    rec_in, rec_gates, rec_conv, rec_vec, rec_out, att_q, att_kv, att_out,
):
    scalars, y, dx, _, ffn, qkv, ao, rin, ro, misc = whole_call(
        tokens, plan_order, cotangent, norm_gains, rec_conv, rec_vec,
        (
            rec_in, rec_gates, rec_out,
            ffn_gate, ffn_up, ffn_down, att_q, att_kv, att_out,
        ),
    )
    return unpack_call(scalars, dx, y, ffn, qkv, ao, rin, ro, misc)


def solution(mesh):
    placed = (
        P("dp", None),
        P("dp", None),
        P("dp", None),
        P("section", None, None),
        P("section", None, "tensor"),
        P("section", None, "tensor"),
        P("section", "tensor", None),
        P("section", None, "tensor"),
        P("section", None, "tensor"),
        P("section", "tensor"),
        P("section", "tensor"),
        P("tensor", "section"),
        P("section", "tensor"),
        P("section", None),
        P("tensor", "section"),
    )
    return jax.shard_map(
        per_device,
        mesh=mesh,
        in_specs=placed,
        out_specs=(
            P("section", "dp", None),
            P("section", None, None),
            P("section", None, "tensor"),
            P("section", None, "tensor"),
            P("section", "tensor", None),
            P("section", None, "tensor"),
            P("section", None, "tensor"),
            P("section", "tensor"),
            P("section", "tensor"),
            P("tensor", "section"),
            P("section", "tensor"),
            P("section", None),
            P("tensor", "section"),
        ),
        check_vma=False,
    )
```
